32 devices in a mesh: dp: 8 (over z, y), mp: 4 (over x, core).
Axes of the slice: x: 2, y: 2, z: 4, core: 2. Of those that a mesh axis runs over, the one named last changes fastest.
Arguments:
- inputs: bfloat16 [16384, 768], P(('dp', 'mp')), may hold values from -6 to 6
- cotangent: bfloat16 [16384, 768], P(('dp', 'mp')), may hold values from -12 to 12
- lengths: int32 [16], P('dp'), may hold values from 256 to 1024, as said below
- gains: float32 [2, 768], P(None, 'dp'), may hold values from 0.5 to 1.5
- w_qkv: float32 [3, 768, 768], P(None, 'dp', 'mp'), may hold values from -0.21875 to 0.21875
- m_qkv: float32 [3, 768, 768], P(None, 'dp', 'mp'), may hold values from -1536 to 1536
- v_qkv: float32 [3, 768, 768], P(None, 'dp', 'mp'), may hold values from 65536 to 262144
- w_out: float32 [768, 768], P('mp', 'dp'), may hold values from -4 to 4
- m_out: float32 [768, 768], P('mp', 'dp'), may hold values from -64 to 64
- v_out: float32 [768, 768], P('mp', 'dp'), may hold values from 128 to 512
- w_gu: float32 [2, 768, 2048], P(None, 'dp', 'mp'), may hold values from -0.21875 to 0.21875
- m_gu: float32 [2, 768, 2048], P(None, 'dp', 'mp'), may hold values from -320 to 320
- v_gu: float32 [2, 768, 2048], P(None, 'dp', 'mp'), may hold values from 2621.44 to 10485.76
- w_down: float32 [2048, 768], P('mp', 'dp'), may hold values from -0.125 to 0.125
- m_down: float32 [2048, 768], P('mp', 'dp'), may hold values from -512 to 512
- v_down: float32 [2048, 768], P('mp', 'dp'), may hold values from 6881.28 to 27852.8
- m_gain: float32 [2, 768], P(None, 'dp'), may hold values from -768 to 768
- v_gain: float32 [2, 768], P(None, 'dp'), may hold values from 16384 to 65536
Outputs:
- output: bfloat16 [16384, 768], P(('dp', 'mp'))
- input_grad: float32 [16384, 768], P(('dp', 'mp'))
- new_gains: float32 [2, 768], P(None, 'dp')
- gain_moment: float32 [2, 768], P(None, 'dp')
- gain_second: float32 [2, 768], P(None, 'dp')
- new_qkv: float32 [3, 768, 768], P(None, 'dp', 'mp')
- qkv_moment: float32 [3, 768, 768], P(None, 'dp', 'mp')
- qkv_second: float32 [3, 768, 768], P(None, 'dp', 'mp')
- new_out: float32 [768, 768], P('mp', 'dp')
- out_moment: float32 [768, 768], P('mp', 'dp')
- out_second: float32 [768, 768], P('mp', 'dp')
- new_gu: float32 [2, 768, 2048], P(None, 'dp', 'mp')
- gu_moment: float32 [2, 768, 2048], P(None, 'dp', 'mp')
- gu_second: float32 [2, 768, 2048], P(None, 'dp', 'mp')
- new_down: float32 [2048, 768], P('mp', 'dp')
- down_moment: float32 [2048, 768], P('mp', 'dp')
- down_second: float32 [2048, 768], P('mp', 'dp')
The draws below stay inside these ranges and needn't reach their ends.
Inputs may be any that keep to these rules, and one draw needn't show every extreme that they name: `lengths`: blocks at positions at or beyond a sequence's length are padding and are never attended to; some sequence is unpadded and some has the least length.
All inputs are finite; a program needn't handle non-finite values.
Results may differ from the reference program's by a relative error of at most 0.025.
Values may be sent and summed in bfloat16 or wider, within the bound.
No kernel may reach another device: no remote copies, remote signals or barrier semaphores. Data moves between devices by JAX's collectives and lax.ppermute only.
A program may use at most 128 MiB of HBM per device.

```python
import math
import jax
import jax.numpy as jnp
from jax import lax

D = 768
H = 12
DH = 64
FF = 2048
L = 1024
STEP = 10
HD = 768
SEQS = 16
TOKENS = 16384
N_MP = 4


def draw_lengths(key, part):
    key = jax.random.fold_in(key, 11)
    key_one, key_two, key_three = jax.random.split(key, 3)
    drawn_lengths = jax.random.randint(key_one, (SEQS,), L // 4, L + 1)
    longest = jax.random.randint(key_two, (), 0, SEQS)
    shortest = (longest + jax.random.randint(key_three, (), 1, SEQS)) % SEQS
    slot_index = jnp.arange(SEQS)
    drawn_lengths = jnp.where(slot_index == longest, L, drawn_lengths)
    drawn_lengths = jnp.where(slot_index == shortest, L // 4, drawn_lengths)
    return drawn_lengths.astype(jnp.int32)


def raised(result, key, source, target, shards_of, factor):
    owner, partner = [(jnp.arange(result.shape[axis_at]) // (result.shape[axis_at] // shards_of)).reshape([-1 if axis == axis_at else 1 for axis in range(result.ndim)]) for axis_at in (source, target)]
    chosen = jax.random.permutation(key, shards_of)[partner]
    strong = (owner == chosen) | (owner == (partner + shards_of // 2) % shards_of)
    return jnp.where(strong, factor * result, result)


def block_levels(own_key, dims, pieces, smallest, high):
    def one(axis_at, blocks):
        heights = jax.random.uniform(jax.random.fold_in(jax.random.fold_in(own_key, 6), axis_at), (blocks,), jnp.float32, smallest / len(pieces), high / len(pieces))
        return jnp.repeat(jnp.exp(heights), dims[axis_at] // blocks).reshape((-1,) + (1,) * (len(dims) - axis_at - 1))

    factor_of = one(*pieces[0])
    for cut in pieces[1:]:
        factor_of = factor_of * one(*cut)
    return factor_of


def normal_values(own_key, shape, deviation, reach, cuts=(), dtype=jnp.bfloat16):
    factor_of = block_levels(own_key, shape, cuts, -0.22, 0.18) if cuts else 1.0
    entries = jax.random.normal(own_key, shape, jnp.float32) * deviation * factor_of
    return jnp.minimum(jnp.maximum(entries, -reach), reach).astype(dtype)


def bell_draw_with(rng, dims, deviation, bound, shards, heavy, kind=jnp.bfloat16):
    entries = deviation * jax.random.normal(rng, dims, jnp.float32)
    if shards:
        entries = entries * block_levels(rng, dims, shards, -0.22, 0.18)
    return jnp.clip(raised(entries, jax.random.fold_in(rng, 3), *heavy), -bound, bound).astype(kind)


def setup_inputs(seed: int = 0) -> dict:
    key_list = jax.random.split(jax.random.key(seed), 19)
    return {
        "inputs": normal_values(key_list[0], (TOKENS, D), 1.0, 6.0, ((0, 32),)),
        "cotangent": bell_draw_with(key_list[1], (TOKENS, D), 1.0, 12.0, ((0, 32),), (0, 1, 32, 2.75)),
        "lengths": draw_lengths(jax.random.fold_in(key_list[18], 71), 0),
        "gains": jnp.clip(1.0 + 0.1 * jax.random.normal(key_list[3], (2, D), jnp.float32), 0.5, 1.5),
        "w_qkv": normal_values(key_list[4], (3, D, HD), D ** -0.5, 0.21875, ((1, 8), (2, 4)), jnp.float32),
        "m_qkv": normal_values(key_list[5], (3, D, HD), (2 * TOKENS ** 0.5), 1536.0, ((1, 8), (2, 4)), jnp.float32),
        "v_qkv": jnp.clip(jnp.exp(math.log(262144.0) - 1.3862944 * jax.random.uniform(key_list[6], (3, D, HD), jnp.float32) ** block_levels(key_list[6], (3, D, HD), ((1, 8), (2, 4)), -0.2, 0.2)), 65536.0, 262144.0),
        "w_out": normal_values(key_list[7], (HD, D), (max(1, 3 * HD // L)) ** -0.5, 4.0, ((0, 4), (1, 8)), jnp.float32),
        "m_out": normal_values(key_list[8], (HD, D), ((8 * TOKENS // L) ** 0.5), 64.0, ((0, 4), (1, 8)), jnp.float32),
        "v_out": jnp.clip(jnp.exp(math.log(512.0) - 1.3862944 * jax.random.uniform(key_list[9], (HD, D), jnp.float32) ** block_levels(key_list[9], (HD, D), ((0, 4), (1, 8)), -0.2, 0.2)), 128.0, 512.0),
        "w_gu": normal_values(key_list[10], (2, D, FF), D ** -0.5, 0.21875, ((1, 8), (2, 4)), jnp.float32),
        "m_gu": normal_values(key_list[11], (2, D, FF), (0.4 * TOKENS ** 0.5), 320.0, ((1, 8), (2, 4)), jnp.float32),
        "v_gu": jnp.clip(jnp.exp(math.log(10485.76) - 1.3862944 * jax.random.uniform(key_list[12], (2, D, FF), jnp.float32) ** block_levels(key_list[12], (2, D, FF), ((1, 8), (2, 4)), -0.2, 0.2)), 2621.44, 10485.76),
        "w_down": normal_values(key_list[13], (FF, D), FF ** -0.5, 0.125, ((0, 4), (1, 8)), jnp.float32),
        "m_down": normal_values(key_list[14], (FF, D), (0.65 * TOKENS ** 0.5), 512.0, ((0, 4), (1, 8)), jnp.float32),
        "v_down": jnp.clip(jnp.exp(math.log(27852.8) - 1.3981289 * jax.random.uniform(key_list[15], (FF, D), jnp.float32) ** block_levels(key_list[15], (FF, D), ((0, 4), (1, 8)), -0.2, 0.2)), 6881.28, 27852.8),
        "m_gain": normal_values(key_list[16], (2, D), (TOKENS ** 0.5), 768.0, ((1, 8),), jnp.float32),
        "v_gain": jnp.clip(jnp.exp(math.log(65536.0) - 1.3862944 * jax.random.uniform(key_list[17], (2, D), jnp.float32) ** block_levels(key_list[17], (2, D), ((1, 8),), -0.2, 0.2)), 16384.0, 65536.0),
    }


NORM_EPS = 1e-06
MASK_FILL = -1e+30
BETA_ONE = 0.5
BETA_TWO = 0.5
ADAM_EPS = 1e-08
DECAY_RATE = 0.01
GAIN_RATE = 0.5
PRECISE = lax.Precision.HIGHEST

@jax.custom_vjp
def low(v):
    return lax.optimization_barrier(v.astype(jnp.bfloat16)).astype(jnp.float32)

@jax.custom_vjp
def low_back(v):
    return v

def low_keep(v):
    return (low(v), None)

def low_pass(kept, grad):
    return (grad,)

def back_keep(v):
    return (v, None)

def back_low(kept, grad):
    return (low(grad),)
low.defvjp(low_keep, low_pass)
low_back.defvjp(back_keep, back_low)

def rms_normed(value, gain):
    inverse = lax.rsqrt(lax.optimization_barrier(jnp.mean(value * value, axis=-1, keepdims=True)) + NORM_EPS)
    return value * inverse * gain

def matmul(left, right):
    return jnp.dot(left, right, precision=PRECISE, preferred_element_type=jnp.float32)

def attend_one(query_rows, key_rows, value_rows, length):
    scores = jnp.einsum('qhd,khd->hqk', query_rows, key_rows, precision=PRECISE) * DH ** (-0.5)
    scores = low_back(scores)
    valid_keys = jnp.arange(L) < length
    scores = jnp.where(valid_keys[None, None, :], scores, MASK_FILL)
    shifted = scores - lax.optimization_barrier(jnp.max(scores, axis=-1, keepdims=True))
    expo = jnp.exp(shifted)
    probs = expo / lax.optimization_barrier(jnp.sum(expo, axis=-1, keepdims=True))
    return jnp.einsum('hqk,khd->qhd', low(probs), value_rows, precision=PRECISE)

def block_forward(inputs_wide, gains, w_qkv, w_out, w_gu, w_down, lengths):
    gain_low = low(gains)
    qkv_low = low(w_qkv)
    out_low = low(w_out)
    gu_low = low(w_gu)
    down_low = low(w_down)
    attend_saved = jax.checkpoint(attend_one)

    def sequence_attend(entry):
        return attend_saved(entry[0], entry[1], entry[2], entry[3])
    first_normed = low(rms_normed(inputs_wide, gain_low[0]))
    group_heads = H // N_MP
    head_width = group_heads * DH
    branch = jnp.zeros_like(inputs_wide)
    for group_index in range(N_MP):
        group_copy = low_back(first_normed)
        columns = slice(group_index * head_width, (group_index + 1) * head_width)
        projected = [low(low_back(matmul(group_copy, qkv_low[member][:, columns]))) for member in range(3)]
        shaped = [item_proj.reshape(SEQS, L, group_heads, DH) for item_proj in projected]
        mixed_heads = lax.map(sequence_attend, (shaped[0], shaped[1], shaped[2], lengths))
        heads_out = low(low_back(mixed_heads.reshape(TOKENS, head_width)))
        branch = branch + low(matmul(heads_out, out_low[columns, :]))
    branch = low_back(branch)
    second_in = inputs_wide + branch
    second_normed = low(rms_normed(second_in, gain_low[1]))
    group_units = FF // N_MP
    ffn_branch = jnp.zeros_like(inputs_wide)
    for group_index in range(N_MP):
        group_copy = low_back(second_normed)
        units = slice(group_index * group_units, (group_index + 1) * group_units)
        gate_value = low_back(matmul(group_copy, gu_low[0][:, units]))
        up_value = low_back(matmul(group_copy, gu_low[1][:, units]))
        hidden = low(jax.nn.gelu(gate_value) * up_value)
        ffn_branch = ffn_branch + low(matmul(hidden, down_low[units, :]))
    ffn_branch = low_back(ffn_branch)
    return second_in + ffn_branch

def adamw_step(weight, moment, second, gradient, step_rate, decay_rate):
    moment_new = BETA_ONE * moment + (1.0 - BETA_ONE) * gradient
    second_new = BETA_TWO * second + (1.0 - BETA_TWO) * gradient * gradient
    fix_one = 1.0 - BETA_ONE ** STEP
    fix_two = 1.0 - BETA_TWO ** STEP
    update = moment_new / fix_one / (jnp.sqrt(second_new / fix_two) + ADAM_EPS)
    return (weight - step_rate * (update + decay_rate * weight), moment_new, second_new)

def reference(inputs, cotangent, lengths, gains, w_qkv, m_qkv, v_qkv, w_out, m_out, v_out, w_gu, m_gu, v_gu, w_down, m_down, v_down, m_gain, v_gain):
    inputs_wide = inputs.astype(jnp.float32)

    def forward(input_value, gain_value, qkv_value, out_value, gu_value, down_value):
        return block_forward(input_value, gain_value, qkv_value, out_value, gu_value, down_value, lengths)
    output, pull_back = jax.vjp(forward, inputs_wide, gains, w_qkv, w_out, w_gu, w_down)
    gradients = pull_back(cotangent.astype(jnp.float32))
    new_gains, gain_moment, gain_second = adamw_step(gains, m_gain, v_gain, gradients[1], GAIN_RATE, 0.0)
    new_qkv, qkv_moment, qkv_second = adamw_step(w_qkv, m_qkv, v_qkv, gradients[2], D ** (-0.5), DECAY_RATE)
    new_out, out_moment, out_second = adamw_step(w_out, m_out, v_out, gradients[3], max(1, 3 * HD // L) ** (-0.5), DECAY_RATE)
    new_gu, gu_moment, gu_second = adamw_step(w_gu, m_gu, v_gu, gradients[4], D ** (-0.5), DECAY_RATE)
    new_down, down_moment, down_second = adamw_step(w_down, m_down, v_down, gradients[5], FF ** (-0.5), DECAY_RATE)
    return (output.astype(jnp.bfloat16), gradients[0], new_gains, gain_moment, gain_second, new_qkv, qkv_moment, qkv_second, new_out, out_moment, out_second, new_gu, gu_moment, gu_second, new_down, down_moment, down_second)
```

```python
import functools
import math

import jax
import jax.numpy as jnp
from jax import lax
from jax.experimental import pallas as pl
from jax.experimental.pallas import tpu as pltpu
from jax.sharding import PartitionSpec as P

D = 768
DH = 64
FF = 2048
L = 1024
STEP = 10
HD = 768

NORM_EPS = 1e-06
MASK_FILL = -1e30
BETA_ONE = 0.5
BETA_TWO = 0.5
ADAM_EPS = 1e-08
DECAY_RATE = 0.01
GAIN_RATE = 0.5

AXES = ("dp", "mp")
BF = jnp.bfloat16
F32 = jnp.float32
SCALE = DH ** (-0.5)
SCALE2 = SCALE * math.log2(math.e)
VMEM_LIMIT = 48 * 1024 * 1024
TILE = 256
COST_CUT = 1


def params(**kw):
    return pltpu.CompilerParams(vmem_limit_bytes=VMEM_LIMIT, **kw)


def cost(flops, nbytes, trans=0):
    return pl.CostEstimate(flops=int(flops) // COST_CUT, bytes_accessed=int(nbytes) // COST_CUT, transcendentals=0)


def round_low(value):
    return lax.reduce_precision(value, 8, 7)


def after(values, anchor):
    return lax.optimization_barrier((values, anchor))[0]


def dot_nn(a, b):
    return lax.dot_general(a, b, (((1,), (0,)), ((), ())), preferred_element_type=F32)


def dot_nt(a, b):
    return lax.dot_general(a, b, (((1,), (1,)), ((), ())), preferred_element_type=F32)


def dot_tn(a, b):
    return lax.dot_general(a, b, (((0,), (0,)), ((), ())), preferred_element_type=F32)


class Net:
    def __init__(self, n_dp, n_mp):
        self.n_dp, self.n_mp = n_dp, n_mp
        self.n_y = 2
        self.n_z = n_dp // 2
        self.fast = n_dp == 8 and n_mp == 4 and (D // n_dp) % 16 == 0

    def perm(self, move):
        pairs = []
        for dp in range(self.n_dp):
            for mp in range(self.n_mp):
                z, y, x, c = dp // 2, dp % 2, mp // 2, mp % 2
                z2, y2, x2, c2 = move(z, y, x, c)
                pairs.append((dp * self.n_mp + mp, (z2 * 2 + y2) * self.n_mp + x2 * 2 + c2))
        return pairs

    def core(self, v):
        return lax.ppermute(v, AXES, self.perm(lambda z, y, x, c: (z, y, x, 1 - c)))

    def x(self, v):
        return lax.ppermute(v, AXES, self.perm(lambda z, y, x, c: (z, y, 1 - x, c)))

    def y(self, v):
        return lax.ppermute(v, AXES, self.perm(lambda z, y, x, c: (z, 1 - y, x, c)))

    def z(self, v, r):
        return lax.ppermute(v, AXES, self.perm(lambda z, y, x, c: ((z + r) % self.n_z, y, x, c)))


def gather_line(net, shard):
    if not net.fast:
        return [shard]
    return [shard] + [net.z(shard, r) for r in (1, 2, 3)]


def gather_plane(net, line, span):
    line = [piece[:, span] for piece in line]
    if not net.fast:
        own = lax.all_gather(line[0], "dp", axis=0, tiled=True)[None]
        return [(own, None, 0)], [(net.x(own), None, 0)]
    lo, hi = jnp.stack(line[:2]), jnp.stack(line[2:])
    y_lo = net.y(lo)
    x_hi = net.x(hi)
    y_hi = net.y(hi)
    x_lo = net.x(lo)
    d_lo = net.x(y_lo)
    d_hi = net.y(x_hi)
    own = [(lo, 0, 0), (hi, 2, 0), (y_lo, 0, 1), (y_hi, 2, 1)]
    other = [(x_lo, 0, 0), (x_hi, 2, 0), (d_lo, 0, 1), (d_hi, 2, 1)]
    return own, other


def block_row(net, pos, offset, flip):
    z = lax.rem(pos[0] + net.n_z + offset, net.n_z)
    y = pos[1] if not flip else 1 - pos[1]
    return z * 2 + y


def assemble(net, target, pieces, metas, pos):
    for ref, (first, flip) in zip(pieces, metas):
        count, rows, _ = ref.shape
        for index in range(count):
            if first is None:
                target[...] = ref[0]
            else:
                block = block_row(net, pos, -(first + index), flip)
                start = pl.multiple_of(block * rows, 16)
                target[pl.ds(start, rows), :] = ref[index]


SMEM_SPEC = pl.BlockSpec(memory_space=pltpu.SMEM)


def whole(shape):
    return pl.BlockSpec(shape, lambda *_: (0,) * len(shape))


def ceil_to(n, m):
    return -(-n // m) * m


def turned(value):
    rows, cols = value.shape
    padded = jnp.pad(value, ((0, ceil_to(rows, 128) - rows), (0, ceil_to(cols, 128) - cols)))
    return padded.T[:cols, :rows]


VMEM_SPEC = pl.BlockSpec(memory_space=pltpu.VMEM)


def pack_attend_kernel(qkv_ref, out_ref, pack_ref):
    width = qkv_ref.shape[2]
    for member in range(3):
        pack_ref[:, member * width : (member + 1) * width] = qkv_ref[member].astype(BF)
    pack_ref[:, 3 * width :] = turned(out_ref[...]).astype(BF)


def pack_attend(w_qkv, w_out):
    _, rows, width = w_qkv.shape
    return pl.pallas_call(
        pack_attend_kernel,
        in_specs=[VMEM_SPEC] * 2,
        out_specs=VMEM_SPEC,
        out_shape=jax.ShapeDtypeStruct((rows, 4 * width), BF),
        compiler_params=params(),
        name="pack_attend",
    )(w_qkv, w_out)


def pack_feed_kernel(gu_ref, down_ref, pack_ref):
    units = gu_ref.shape[2] // 2
    turned_down = turned(down_ref[...]).astype(BF)
    for part in range(2):
        span = slice(part * units, (part + 1) * units)
        base = 3 * part * units
        pack_ref[:, base : base + units] = gu_ref[0, :, span].astype(BF)
        pack_ref[:, base + units : base + 2 * units] = gu_ref[1, :, span].astype(BF)
        pack_ref[:, base + 2 * units : base + 3 * units] = turned_down[:, span]


def pack_feed(w_gu, w_down):
    _, rows, units = w_gu.shape
    return pl.pallas_call(
        pack_feed_kernel,
        in_specs=[VMEM_SPEC] * 2,
        out_specs=VMEM_SPEC,
        out_shape=jax.ShapeDtypeStruct((rows, 3 * units), BF),
        compiler_params=params(),
        name="pack_feed",
    )(w_gu, w_down)


def norm_kernel(net, pos, x_ref, g_ref, h_ref, gain_ref):
    @pl.when(pl.program_id(0) == 0)
    def _():
        if not net.fast:
            gain_ref[...] = g_ref[...]
        else:
            for block in range(net.n_dp):
                rank = lax.rem(pos[0] + net.n_z - block // 2, net.n_z)
                flip = lax.rem(pos[1] + block, 2)
                size = D // net.n_dp
                gain_ref[:, block * size : (block + 1) * size] = g_ref[flip, rank][:, :size]

    value = x_ref[...].astype(F32)
    inverse = lax.rsqrt(jnp.mean(value * value, axis=1, keepdims=True) + NORM_EPS)
    h_ref[...] = (value * inverse * gain_ref[0:1, :]).astype(BF)


def first_norm(net, pos, x, gains):
    rows = x.shape[0]
    return pl.pallas_call(
        functools.partial(norm_kernel, net),
        grid=(rows // TILE,),
        in_specs=[SMEM_SPEC, pl.BlockSpec((TILE, D), lambda i: (i, 0)), whole(gains.shape)],
        out_specs=[pl.BlockSpec((TILE, D), lambda i: (i, 0)), whole((8, D))],
        out_shape=[jax.ShapeDtypeStruct((rows, D), BF), jax.ShapeDtypeStruct((8, D), F32)],
        compiler_params=params(),
        name="first_norm",
    )(pos, x, gains)


def gather_gains(net, gains):
    low = round_low(gains)
    if not net.fast:
        return jnp.pad(lax.all_gather(low, "dp", axis=1, tiled=True), ((0, 6), (0, 0)))
    low = jnp.pad(low, ((0, 6), (0, 128 - low.shape[1])))
    here = jnp.stack([low] + [net.z(low, r) for r in (1, 2, 3)])
    return jnp.stack([here, net.y(here)])


def project_kernel(net, metas, pos, h_ref, *refs):
    count = len(metas)
    pieces, (qkv_ref, wqkv_ref, wout_ref, full) = refs[:count], refs[count:]

    @pl.when(pl.program_id(0) == 0)
    def _():
        assemble(net, full, pieces, metas, pos)
        wqkv_ref[...] = full[:, : wqkv_ref.shape[1]]
        wout_ref[...] = full[:, wqkv_ref.shape[1] :]

    qkv_ref[...] = dot_nn(h_ref[...], wqkv_ref[...]).astype(BF)


def project(net, pos, h1, pieces, head_width):
    rows = h1.shape[0]
    arrays = [p[0] for p in pieces]
    metas = [(p[1], p[2]) for p in pieces]
    return pl.pallas_call(
        functools.partial(project_kernel, net, metas),
        grid=(rows // TILE,),
        in_specs=[SMEM_SPEC, pl.BlockSpec((TILE, D), lambda i: (i, 0))] + [whole(a.shape) for a in arrays],
        out_specs=[
            pl.BlockSpec((TILE, 3 * head_width), lambda i: (i, 0)),
            whole((D, 3 * head_width)),
            whole((D, head_width)),
        ],
        out_shape=[
            jax.ShapeDtypeStruct((rows, 3 * head_width), BF),
            jax.ShapeDtypeStruct((D, 3 * head_width), BF),
            jax.ShapeDtypeStruct((D, head_width), BF),
        ],
        scratch_shapes=[pltpu.VMEM((D, 4 * head_width), BF)],
        compiler_params=params(),
        cost_estimate=cost(2 * rows * D * 3 * head_width, 2 * (rows * (D + 3 * head_width) + 2 * D * D)),
        name="project",
    )(pos, h1, *arrays)


def key_valid(meta, seq, count, axis, shape, start):
    place = lax.broadcasted_iota(jnp.int32, shape, axis) + start + meta[count + seq]
    place = jnp.where(place >= L, place - L, place)
    return place < meta[seq]


def attend_kernel(heads, seqs, meta, qkv_ref, o_ref, lse_ref):
    seq, step = pl.program_id(0), pl.program_id(1)
    width = heads * DH
    valid = key_valid(meta, seq, seqs, 1, (1, L), 0)
    start = pl.multiple_of(step * TILE, TILE)
    queries = qkv_ref[pl.ds(start, TILE), 0:width]
    lane = lax.broadcasted_iota(jnp.int32, (TILE, 128), 1)
    logs = jnp.zeros((TILE, 128), F32)
    outs = []
    for head in range(heads):
        cols = slice(head * DH, (head + 1) * DH)
        keys = qkv_ref[:, width + head * DH : width + (head + 1) * DH]
        values = qkv_ref[:, 2 * width + head * DH : 2 * width + (head + 1) * DH]
        scores = dot_nt(queries[:, cols], keys) * SCALE2
        scores = jnp.where(valid, scores, MASK_FILL)
        top = jnp.max(scores, axis=1, keepdims=True)
        expo = jnp.exp2(scores - top)
        total = jnp.sum(expo, axis=1, keepdims=True)
        mixed = dot_nn(expo.astype(BF), values)
        outs.append(mixed / total)
        logs = jnp.where(lane == head, top + jnp.log2(total), logs)
    o_ref[...] = jnp.concatenate(outs, axis=1).astype(BF)
    lse_ref[...] = logs.T[0:8]


def attend(meta, qkv, head_width, seqs):
    rows = qkv.shape[0]
    heads = head_width // DH
    steps = L // TILE
    return pl.pallas_call(
        functools.partial(attend_kernel, heads, seqs),
        grid=(seqs, steps),
        in_specs=[SMEM_SPEC, pl.BlockSpec((L, 3 * head_width), lambda s, i: (s, 0))],
        out_specs=[
            pl.BlockSpec((TILE, head_width), lambda s, i: (s * steps + i, 0)),
            pl.BlockSpec((8, TILE), lambda s, i: (0, s * steps + i)),
        ],
        out_shape=[
            jax.ShapeDtypeStruct((rows, head_width), BF),
            jax.ShapeDtypeStruct((8, rows), F32),
        ],
        compiler_params=params(),
        cost_estimate=cost(4 * 4 * rows * L * head_width, 8 * rows * head_width),
        name="attend",
    )(meta, qkv)


def attend_back_kernel(heads, seqs, block, meta, qkv_ref, do_ref, o_ref, lse_ref, out_ref, inner, dq_acc):
    seq, step = pl.program_id(0), pl.program_id(1)
    width = heads * DH
    start = pl.multiple_of(step * block, block)

    @pl.when(step == 0)
    def _():
        dq_acc[...] = jnp.zeros_like(dq_acc)
        lane = lax.broadcasted_iota(jnp.int32, (TILE, 128), 1)
        for part in range(L // TILE):
            rows = slice(part * TILE, (part + 1) * TILE)
            product = do_ref[rows, :].astype(F32) * o_ref[rows, :].astype(F32)
            sums = jnp.zeros((TILE, 128), F32)
            for head in range(heads):
                one = jnp.sum(product[:, head * DH : (head + 1) * DH], axis=1, keepdims=True)
                sums = jnp.where(lane == head, one, sums)
            inner[:, rows] = sums.T[0:8]

    valid = key_valid(meta, seq, seqs, 0, (block, 1), start)
    for head in range(heads):
        cols = slice(head * DH, (head + 1) * DH)
        queries = qkv_ref[:, cols]
        grads = do_ref[:, cols]
        keys = qkv_ref[pl.ds(start, block), width + head * DH : width + (head + 1) * DH]
        values = qkv_ref[pl.ds(start, block), 2 * width + head * DH : 2 * width + (head + 1) * DH]
        scores = dot_nt(keys, queries) * SCALE2 - lse_ref[head : head + 1, :]
        probs = jnp.where(valid, jnp.exp2(scores), 0.0)
        grad_probs = dot_nt(values, grads)
        grad_scores = (probs * (grad_probs - inner[head : head + 1, :])).astype(BF)
        grad_values = dot_nn(probs.astype(BF), grads)
        grad_keys = dot_nn(grad_scores, queries) * SCALE
        out_ref[pl.ds(start, block), width + head * DH : width + (head + 1) * DH] = grad_keys.astype(BF)
        out_ref[pl.ds(start, block), 2 * width + head * DH : 2 * width + (head + 1) * DH] = (
            grad_values.astype(BF)
        )
        dq_acc[cols, :] += dot_tn(keys, grad_scores)

    @pl.when(step == pl.num_programs(1) - 1)
    def _():
        out_ref[:, 0:width] = (dq_acc[...] * SCALE).T.astype(BF)


def attend_back(meta, qkv, grad, mixed, lse, head_width, seqs):
    rows = qkv.shape[0]
    heads = head_width // DH
    block = TILE
    return pl.pallas_call(
        functools.partial(attend_back_kernel, heads, seqs, block),
        grid=(seqs, L // block),
        in_specs=[
            SMEM_SPEC,
            pl.BlockSpec((L, 3 * head_width), lambda s, i: (s, 0)),
            pl.BlockSpec((L, head_width), lambda s, i: (s, 0)),
            pl.BlockSpec((L, head_width), lambda s, i: (s, 0)),
            pl.BlockSpec((8, L), lambda s, i: (0, s)),
        ],
        out_specs=pl.BlockSpec((L, 3 * head_width), lambda s, i: (s, 0)),
        out_shape=jax.ShapeDtypeStruct((rows, 3 * head_width), BF),
        scratch_shapes=[pltpu.VMEM((8, L), F32), pltpu.VMEM((head_width, L), F32)],
        compiler_params=params(),
        cost_estimate=cost(4 * 10 * rows * L * head_width, 16 * rows * head_width),
        name="attend_back",
    )(meta, qkv, grad, mixed, lse)


def feed_kernel(net, metas, units, first, pos, h_ref, dy_ref, *refs):
    groups = []
    for group in metas:
        groups.append(refs[: len(group)])
        refs = refs[len(group) :]
    if not first:
        f_prev, d_prev, refs = refs[0], refs[1], refs[2:]
    mid_refs, (f_ref, d_ref, full) = refs[:2], refs[2:]

    @pl.when(pl.program_id(0) == 0)
    def _():
        for index, group in enumerate(metas):
            assemble(net, full.at[index], groups[index], group, pos)

    hidden_in, back_in = h_ref[...], dy_ref[...]
    root = math.sqrt(2.0 / math.pi)
    f_part = d_part = 0.0
    for index in range(2):
        w_gate, w_up, w_down = (full[index, :, j * units : (j + 1) * units] for j in range(3))
        gate = dot_nn(hidden_in, w_gate)
        up = dot_nn(hidden_in, w_up)
        grad_hidden = dot_nn(back_in, w_down)
        square = gate * gate
        tanh = jnp.tanh(gate * (root + (root * 0.044715) * square))
        half = 0.5 * (1.0 + tanh)
        gelu = gate * half
        slope = half + (0.5 * gate) * (1.0 - tanh * tanh) * (root + (3.0 * root * 0.044715) * square)
        hidden = (gelu * up).astype(BF)
        grad_gate = (grad_hidden * up * slope).astype(BF)
        grad_up = (grad_hidden * gelu).astype(BF)
        mid_ref = mid_refs[index]
        mid_ref[:, 0:units] = grad_gate
        mid_ref[:, units : 2 * units] = grad_up
        mid_ref[:, 2 * units : 3 * units] = hidden
        f_part += dot_nt(hidden, w_down)
        d_part += dot_nt(grad_gate, w_gate) + dot_nt(grad_up, w_up)
    if not first:
        f_part += f_prev[...].astype(F32)
        d_part += d_prev[...].astype(F32)
    f_ref[...] = f_part.astype(BF)
    d_ref[...] = d_part.astype(BF)


def feed(net, pos, h2, back, groups, units, previous):
    rows = h2.shape[0]
    arrays = [p[0] for group in groups for p in group]
    metas = [[(p[1], p[2]) for p in group] for group in groups]
    row_spec = pl.BlockSpec((TILE, D), lambda i: (i, 0))
    mid_spec = pl.BlockSpec((TILE, 3 * units), lambda i: (i, 0))
    return pl.pallas_call(
        functools.partial(feed_kernel, net, metas, units, not previous),
        grid=(rows // TILE,),
        in_specs=[SMEM_SPEC, row_spec, row_spec] + [whole(a.shape) for a in arrays] + [row_spec] * len(previous),
        out_specs=[mid_spec, mid_spec, row_spec, row_spec],
        out_shape=[jax.ShapeDtypeStruct((rows, 3 * units), BF)] * 2 + [jax.ShapeDtypeStruct((rows, D), BF)] * 2,
        scratch_shapes=[pltpu.VMEM((2, D, 3 * units), BF)],
        compiler_params=params(),
        cost_estimate=cost(2 * rows * D * 12 * units, 2 * (rows * 8 * D + 6 * D * units), 2 * rows * units),
        name="feed",
    )(pos, h2, back, *arrays, *previous)


def second_kernel(x_ref, a_ref, b_ref, gain_ref, h_ref):
    value = x_ref[...].astype(F32) + (a_ref[...].astype(F32) + b_ref[...].astype(F32))
    inverse = lax.rsqrt(jnp.mean(value * value, axis=1, keepdims=True) + NORM_EPS)
    h_ref[...] = (value * inverse * gain_ref[1:2, :]).astype(BF)


def second_norm(x, a_own, a_other, gain):
    rows = x.shape[0]
    steps = rows // TILE
    row_spec = pl.BlockSpec((TILE, D), lambda i: (i, 0))
    swapped = pl.BlockSpec((TILE, D), lambda i: (lax.rem(i + steps // 2, steps), 0))
    return pl.pallas_call(
        second_kernel,
        grid=(steps,),
        in_specs=[row_spec, row_spec, swapped, whole((8, D))],
        out_specs=row_spec,
        out_shape=jax.ShapeDtypeStruct((rows, D), BF),
        compiler_params=params(),
        cost_estimate=cost(10 * rows * D, 8 * rows * D),
        name="second_norm",
    )(x, a_own, a_other, gain)


def middle_kernel(own_steps, x_ref, a_ref, b_ref, dy_ref, d_ref, e_ref, gain_ref, wo_ref, wx_ref,
                  da_ref, do_ref, dx_ref, dx2_ref):
    step = pl.program_id(0)
    gain = gain_ref[1:2, :]
    second_in = x_ref[...].astype(F32) + (a_ref[...].astype(F32) + b_ref[...].astype(F32))
    inverse = lax.rsqrt(jnp.mean(second_in * second_in, axis=1, keepdims=True) + NORM_EPS)
    normed = second_in * inverse
    grad = d_ref[...].astype(F32) + e_ref[...].astype(F32)
    scaled = grad * gain
    center = jnp.mean(scaled * normed, axis=1, keepdims=True)
    total = dy_ref[...].astype(F32) + inverse * (scaled - normed * center)
    low = total.astype(BF)
    da_ref[...] = low
    do_ref[...] = dot_nn(low, wo_ref[...]).astype(BF)
    dx_ref[...] = dot_nn(low, wx_ref[...]).astype(BF)

    @pl.when(step < own_steps)
    def _():
        dx2_ref[...] = total


def middle(x, a_own, a_other, back, d_own, d_other, gain, w_own, w_other):
    rows = x.shape[0]
    steps = rows // TILE
    half = steps // 2
    width = w_own.shape[1]
    row_spec = pl.BlockSpec((TILE, D), lambda i: (i, 0))
    swapped = pl.BlockSpec((TILE, D), lambda i: (lax.rem(i + half, steps), 0))
    head_spec = pl.BlockSpec((TILE, width), lambda i: (i, 0))
    return pl.pallas_call(
        functools.partial(middle_kernel, half),
        grid=(steps,),
        in_specs=[row_spec, row_spec, swapped, row_spec, row_spec, swapped, whole((8, D)),
                  whole((D, width)), whole((D, width))],
        out_specs=[row_spec, head_spec, head_spec,
                   pl.BlockSpec((TILE, D), lambda i: (jnp.minimum(i, half - 1), 0))],
        out_shape=[
            jax.ShapeDtypeStruct((rows, D), BF),
            jax.ShapeDtypeStruct((rows, width), BF),
            jax.ShapeDtypeStruct((rows, width), BF),
            jax.ShapeDtypeStruct((rows // 2, D), F32),
        ],
        compiler_params=params(),
        cost_estimate=cost(4 * rows * D * width, 20 * rows * D),
        name="middle",
    )(x, a_own, a_other, back, d_own, d_other, gain, w_own, w_other)


def grad_kernel(net, spans, pos, left_ref, right_ref, mid_ref, tail_ref, *refs):
    outs, full = refs[:-1], refs[-1]
    for source, other, target, size in spans:
        left = (left_ref, right_ref)[source]
        values = (mid_ref, tail_ref)[other[0]][:, other[1] : other[1] + size]
        full[:, target : target + size] = dot_tn(left[...], values).astype(BF)
    if len(outs) == 1:
        outs[0][...] = full[...]
        return
    rows = outs[0].shape[1]
    for flip in range(2):
        for offset in range(net.n_z):
            block = block_row(net, pos, offset, flip)
            start = pl.multiple_of(block * rows, 16)
            outs[flip * 2 + offset // 2][offset % 2] = full[pl.ds(start, rows), :]


def grad_pack(net, pos, left, right, mid, tail, spans, width):
    rows = left.shape[0]
    if net.fast:
        shapes = [jax.ShapeDtypeStruct((2, D // net.n_dp, width), BF)] * 4
    else:
        shapes = [jax.ShapeDtypeStruct((D, width), BF)]
    return pl.pallas_call(
        functools.partial(grad_kernel, net, spans),
        in_specs=[SMEM_SPEC] + [pl.BlockSpec(memory_space=pltpu.VMEM)] * 4,
        out_specs=[pl.BlockSpec(memory_space=pltpu.VMEM)] * len(shapes),
        out_shape=shapes,
        scratch_shapes=[pltpu.VMEM((D, width), BF)],
        compiler_params=params(),
        cost_estimate=cost(2 * rows * D * width, 2 * (rows * (2 * D + width) + D * width)),
        name="weight_grad",
    )(pos, left, right, mid, tail)


def add_low(a, b):
    return (a.astype(F32) + b.astype(F32)).astype(BF)


def sum_kernel(count, *refs):
    ins, outs = refs[: 6 * count], refs[6 * count :]
    for pack in range(count):
        for part in range(2):
            own, across, along = (ins[6 * pack + 2 * j + part] for j in range(3))
            width = own.shape[2]
            for index in range(2):
                total = own[index].astype(F32) + (across[index].astype(F32) + along[index].astype(F32))
                out = outs[2 * part + index]
                out[:, pack * width : (pack + 1) * width] = total.astype(out.dtype)


def sum_plane(parts):
    _, rows, width = parts[0].shape
    count = len(parts) // 6
    width *= count
    return pl.pallas_call(
        functools.partial(sum_kernel, count),
        grid=(1,),
        in_specs=[whole(p.shape) for p in parts],
        out_specs=[whole((rows, width))] * 4,
        out_shape=[jax.ShapeDtypeStruct((rows, width), F32)] + [jax.ShapeDtypeStruct((rows, width), BF)] * 3,
        compiler_params=params(),
        cost_estimate=cost(8 * rows * width, 24 * rows * width),
        name="sum_plane",
    )(*parts)


class Scatter:
    def __init__(self, net, own, other):
        self.net = net
        if not net.fast:
            total = own[0].astype(F32) + net.x(other[0]).astype(F32)
            self.pieces = [lax.psum_scatter(total, "dp", scatter_dimension=0, tiled=True)]
            return
        self.own = own
        x_lo, x_hi, d_lo, d_hi = other
        self.x_hi = x_hi
        self.in_d_lo = net.x(d_lo)
        self.in_d_hi = net.y(d_hi)
        self.in_x_lo = net.x(x_lo)
        self.in_y_hi = net.y(own[3])

    def turn(self, anchor):
        if not self.net.fast:
            return
        y_lo, d_lo, x_hi, d_hi = after((self.own[2], self.in_d_lo, self.x_hi, self.in_d_hi), anchor)
        self.y_sum, self.x_sum = add_low(y_lo, d_lo), add_low(x_hi, d_hi)
        self.in_y_lo = self.net.y(self.y_sum)
        self.in_x_hi = self.net.x(self.x_sum)

    def marks(self):
        return (self.y_sum, self.x_sum) if self.net.fast else ()


def finish_line(net, scatters, anchor):
    if not net.fast:
        return [jnp.concatenate([s.pieces[0] for s in scatters], axis=1)]
    parts = []
    for s in scatters:
        parts += [s.own[0], s.own[1], s.in_x_lo, s.in_x_hi, s.in_y_lo, s.in_y_hi]
    s0, s1, s2, s3 = sum_plane(after(parts, anchor))
    return [s0, net.z(s1, 1), net.z(s2, 2), net.z(s3, 3)]


def adamw(outs, ins, place, gradient, rate, decay):
    weight, moment, second = (ref[place] for ref in ins)
    moment = BETA_ONE * moment + (1.0 - BETA_ONE) * gradient
    second = BETA_TWO * second + (1.0 - BETA_TWO) * gradient * gradient
    fix_one = 1.0 - BETA_ONE**STEP
    fix_two = 1.0 - BETA_TWO**STEP
    update = moment / fix_one / (jnp.sqrt(second / fix_two) + ADAM_EPS)
    outs[0][place] = weight - rate * (update + decay * weight)
    outs[1][place] = moment
    outs[2][place] = second


def total_of(refs, span):
    total = refs[0][:, span].astype(F32)
    for ref in refs[1:]:
        total += ref[:, span].astype(F32)
    return total


def put_row(out_ref, column):
    row = turned(column)
    out_ref[...] = jnp.zeros_like(out_ref)
    out_ref[0:1, 0 : row.shape[1]] = row


def adam_attend_kernel(count, *refs):
    pieces, refs = refs[:count], refs[count:]
    qkv, out, qkv_new, out_new, gain_ref = refs[0:3], refs[3:6], refs[6:9], refs[9:12], refs[12]
    width = qkv[0].shape[2]
    column = 0.0
    for member in range(3):
        gradient = total_of(pieces, slice(member * width, (member + 1) * width))
        low = qkv[0][member].astype(BF).astype(F32)
        column += jnp.sum(low * gradient, axis=1, keepdims=True)
        adamw(qkv_new, qkv, member, gradient, D ** (-0.5), DECAY_RATE)
    gradient = turned(total_of(pieces, slice(3 * width, 4 * width)))
    adamw(out_new, out, ..., gradient, max(1, 3 * HD // L) ** (-0.5), DECAY_RATE)
    put_row(gain_ref, column)


def adam_feed_kernel(count, *refs):
    pieces, refs = refs[:count], refs[count:]
    gu, down, gu_new, down_new, gain_ref = refs[0:3], refs[3:6], refs[6:9], refs[9:12], refs[12]
    units = gu[0].shape[2] // 2
    column = 0.0
    for part in range(2):
        span = slice(part * units, (part + 1) * units)
        base = 3 * part * units
        for member in range(2):
            gradient = total_of(pieces, slice(base + member * units, base + (member + 1) * units))
            low = gu[0][member, :, span].astype(BF).astype(F32)
            column += jnp.sum(low * gradient, axis=1, keepdims=True)
            adamw(gu_new, gu, (member, slice(None), span), gradient, D ** (-0.5), DECAY_RATE)
        gradient = turned(total_of(pieces, slice(base + 2 * units, base + 3 * units)))
        adamw(down_new, down, (span, slice(None)), gradient, FF ** (-0.5), DECAY_RATE)
    put_row(gain_ref, column)


def adam_call(kernel, pieces, states, name):
    shapes = [jax.ShapeDtypeStruct(s.shape, F32) for s in states] + [jax.ShapeDtypeStruct((8, 128), F32)]
    return pl.pallas_call(
        functools.partial(kernel, len(pieces)),
        grid=(1,),
        in_specs=[whole(a.shape) for a in list(pieces) + list(states)],
        out_specs=[whole(s.shape) for s in shapes],
        out_shape=shapes,
        compiler_params=params(),
        cost_estimate=cost(20 * sum(s.size for s in states), 10 * sum(s.size for s in states)),
        name=name,
    )(*pieces, *states)


def gain_step(weight, moment, second, gradient):
    moment_new = BETA_ONE * moment + (1.0 - BETA_ONE) * gradient
    second_new = BETA_TWO * second + (1.0 - BETA_TWO) * gradient * gradient
    fix_one = 1.0 - BETA_ONE**STEP
    fix_two = 1.0 - BETA_TWO**STEP
    update = moment_new / fix_one / (jnp.sqrt(second_new / fix_two) + ADAM_EPS)
    return (weight - GAIN_RATE * update, moment_new, second_new)


def body(
    net,
    inputs,
    cotangent,
    lengths,
    gains,
    w_qkv,
    m_qkv,
    v_qkv,
    w_out,
    m_out,
    v_out,
    w_gu,
    m_gu,
    v_gu,
    w_down,
    m_down,
    v_down,
    m_gain,
    v_gain,
):
    own_rows = inputs.shape[0]
    rows = 2 * own_rows
    shard = w_qkv.shape[1]
    width = w_qkv.shape[2]
    half_units = w_gu.shape[2] // 2
    dp, mp = lax.axis_index("dp"), lax.axis_index("mp")
    core = lax.rem(mp, 2)
    pos = jnp.stack([dp // 2, lax.rem(dp, 2)]).astype(jnp.int32)

    if own_rows % L == 0:
        each = own_rows // L
        seqs = 2 * each
        pair = mp + 1 - 2 * core
        own_len = lax.dynamic_slice(lengths, (mp * each,), (each,))
        other_len = lax.dynamic_slice(lengths, (pair * each,), (each,))
        meta = jnp.concatenate([own_len, other_len, jnp.zeros((seqs,), jnp.int32)])
    else:
        seqs = rows // L
        len_here = lax.dynamic_slice(lengths, ((mp // 2) * seqs,), (seqs,))
        meta = jnp.concatenate([len_here, jnp.full((seqs,), core * own_rows, jnp.int32)])

    gain_pieces = gather_gains(net, gains)
    line_a = gather_line(net, pack_attend(w_qkv, w_out))
    a_own, a_other = gather_plane(net, line_a, slice(0, 4 * width))
    line_f = gather_line(net, pack_feed(w_gu, w_down))
    pack_width = 3 * half_units
    f_pieces = [gather_plane(net, line_f, slice(p * pack_width, (p + 1) * pack_width)) for p in range(2)]

    x_pair = jnp.concatenate([inputs, net.core(inputs)], axis=0)
    back = jnp.concatenate([cotangent, net.core(cotangent)], axis=0)
    h1, gain_wide = first_norm(net, pos, x_pair, gain_pieces)

    qkv_own, wqkv_own, wout_own = project(net, pos, h1, a_own, width)
    o_own, lse_own = attend(meta, qkv_own, width, seqs)
    h1_late = after(h1, line_f[1:])
    qkv_other, wqkv_other, wout_other = project(net, pos, h1_late, a_other, width)
    o_other, lse_other = attend(meta, qkv_other, width, seqs)

    branch = (dot_nt(o_own, wout_own) + dot_nt(o_other, wout_other)).astype(BF)
    branch_in = net.core(branch)
    h2 = second_norm(x_pair, branch, branch_in, gain_wide)

    f_spans = [(0, (0, 0), 0, 2 * half_units), (1, (0, 2 * half_units), 2 * half_units, half_units)]
    sums = []
    mids = []
    previous = []
    for groups in f_pieces:
        mid_own, mid_other, f_part, d_part = feed(net, pos, h2, back, groups, half_units, previous)
        previous = [f_part, d_part]
        mids.append((mid_own, mid_other))
    d_in = net.core(d_part)
    for mid_own, mid_other in mids:
        g_other = grad_pack(net, pos, h2, back, mid_other, mid_other, f_spans, pack_width)
        g_own = grad_pack(net, pos, h2, back, mid_own, mid_own, f_spans, pack_width)
        sums.append(Scatter(net, g_own, g_other))

    da, do_own, do_other, dx2 = middle(
        x_pair, branch, branch_in, back, d_part, d_in, gain_wide, wout_own, wout_other
    )
    sums[0].turn(da)
    do_other = after(do_other, sums[0].marks())
    dqkv_other = attend_back(meta, qkv_other, do_other, o_other, lse_other, width, seqs)
    sums[1].turn(dqkv_other)
    a_spans = [(0, (0, 0), 0, 3 * width), (1, (1, 0), 3 * width, width)]
    g_other = grad_pack(net, pos, h1, da, dqkv_other, o_other, a_spans, 4 * width)
    do_own = after(do_own, (g_other, sums[1].marks()))
    dqkv_own = attend_back(meta, qkv_own, do_own, o_own, lse_own, width, seqs)
    g_own = grad_pack(net, pos, h1, da, dqkv_own, o_own, a_spans, 4 * width)
    sum_a = Scatter(net, g_own, g_other)
    pieces_f = finish_line(net, sums, g_own)
    sum_a.turn(pieces_f[0])
    marks = (sum_a.marks(), pieces_f[0])

    dqkv_own, dqkv_last = after((dqkv_own, dqkv_other), marks)
    dh1 = (dot_nt(dqkv_own, wqkv_own) + dot_nt(dqkv_last, wqkv_other)).astype(BF)
    dh1_in = net.core(dh1[own_rows:])
    f_in = net.core(after(f_part[own_rows:], marks))
    x_own = inputs.astype(F32)
    second_in = x_own + (branch[:own_rows].astype(F32) + branch_in[own_rows:].astype(F32))
    output = (second_in + (f_part[:own_rows].astype(F32) + f_in.astype(F32))).astype(BF)
    grad_first = dh1[:own_rows].astype(F32) + dh1_in.astype(F32)
    r_own = lax.rsqrt(jnp.mean(x_own * x_own, axis=1, keepdims=True) + NORM_EPS)
    n_own = x_own * r_own
    scaled = grad_first * gain_wide[0]
    center = jnp.mean(scaled * n_own, axis=1, keepdims=True)
    input_grad = dx2 + r_own * (scaled - n_own * center)
    pieces_a = finish_line(net, [sum_a], dh1)

    states_f = [w_gu, m_gu, v_gu, w_down, m_down, v_down]
    feed_new = adam_call(adam_feed_kernel, pieces_f, states_f, "adam_feed")
    states_a = [w_qkv, m_qkv, v_qkv, w_out, m_out, v_out]
    pieces_a = after(pieces_a, (output, input_grad, feed_new))
    attend_new = adam_call(adam_attend_kernel, pieces_a, states_a, "adam_attend")
    terms = jnp.concatenate([attend_new[-1][0:1], feed_new[-1][0:1]], axis=0)
    pair_sum = terms + net.core(terms)
    gain_grad = (pair_sum + net.x(pair_sum))[:, :shard] / round_low(gains)
    new_gains, gain_moment, gain_second = gain_step(gains, m_gain, v_gain, gain_grad)
    return (output, input_grad, new_gains, gain_moment, gain_second) + tuple(attend_new[:6]) + tuple(feed_new[:6])


def solution(mesh):
    net = Net(mesh.shape["dp"], mesh.shape["mp"])
    rows = P(("dp", "mp"), None)
    gain = P(None, "dp")
    wide = P(None, "dp", "mp")
    tall = P("mp", "dp")
    return jax.shard_map(
        functools.partial(body, net),
        mesh=mesh,
        in_specs=(rows, rows, P("dp"), gain) + (wide,) * 3 + (tall,) * 3 + (wide,) * 3 + (tall,) * 3 + (gain,) * 2,
        out_specs=(rows, rows) + (gain,) * 3 + (wide,) * 3 + (tall,) * 3 + (wide,) * 3 + (tall,) * 3,
        check_vma=False,
    )
```

```python
import functools
import math

import jax
import jax.numpy as jnp
from jax import lax
from jax.experimental import pallas as pl
from jax.experimental.pallas import tpu as pltpu
from jax.sharding import PartitionSpec as P

D = 768
DH = 64
FF = 2048
L = 1024
STEP = 10
HD = 768

NORM_EPS = 1e-06
MASK_FILL = -1e30
BETA_ONE = 0.5
BETA_TWO = 0.5
ADAM_EPS = 1e-08
DECAY_RATE = 0.01
GAIN_RATE = 0.5

AXES = ("dp", "mp")
BF = jnp.bfloat16
F32 = jnp.float32
SCALE = DH ** (-0.5)
SCALE2 = SCALE * math.log2(math.e)
VMEM_LIMIT = 24 * 1024 * 1024
TILE = 256
FEED_TILE = 512
COST_CUT = 1


def params(**kw):
    return pltpu.CompilerParams(vmem_limit_bytes=VMEM_LIMIT, **kw)


def cost(flops, nbytes, trans=0):
    return pl.CostEstimate(flops=int(flops) // COST_CUT, bytes_accessed=int(nbytes) // COST_CUT, transcendentals=0)


def round_low(value):
    return lax.reduce_precision(value, 8, 7)


def after(values, anchor):
    return lax.optimization_barrier((values, anchor))[0]


def dot_nn(a, b):
    return lax.dot_general(a, b, (((1,), (0,)), ((), ())), preferred_element_type=F32)


def dot_nt(a, b):
    return lax.dot_general(a, b, (((1,), (1,)), ((), ())), preferred_element_type=F32)


def dot_tn(a, b):
    return lax.dot_general(a, b, (((0,), (0,)), ((), ())), preferred_element_type=F32)


def together(*values):
    return lax.optimization_barrier(values)


def hbm(array):
    return pltpu.with_memory_space_constraint(array, pltpu.HBM)


SMEM_SPEC = pl.BlockSpec(memory_space=pltpu.SMEM)
VMEM_SPEC = pl.BlockSpec(memory_space=pltpu.VMEM)


def whole(shape):
    return pl.BlockSpec(shape, lambda *_: (0,) * len(shape))


def in_vmem(kernel, name, scalars, arrays, outs, scratch=(), flops=0):
    nbytes = sum(a.size * a.dtype.itemsize for a in arrays)
    return pl.pallas_call(
        kernel,
        in_specs=[SMEM_SPEC] * len(scalars) + [VMEM_SPEC] * len(arrays),
        out_specs=[VMEM_SPEC] * len(outs),
        out_shape=[pltpu.VMEM(shape, dtype) for shape, dtype in outs],
        scratch_shapes=[pltpu.VMEM(shape, dtype) for shape, dtype in scratch],
        compiler_params=params(),
        cost_estimate=cost(flops, nbytes),
        name=name,
    )(*scalars, *arrays)


class Net:
    def __init__(self, n_dp, n_mp):
        self.n_dp, self.n_mp = n_dp, n_mp
        self.n_y = 2
        self.n_z = n_dp // 2
        self.fast = n_dp == 8 and n_mp == 4 and (D // n_dp) % 16 == 0

    def perm(self, move):
        pairs = []
        for dp in range(self.n_dp):
            for mp in range(self.n_mp):
                z, y, x, c = dp // 2, dp % 2, mp // 2, mp % 2
                z2, y2, x2, c2 = move(z, y, x, c)
                pairs.append((dp * self.n_mp + mp, (z2 * 2 + y2) * self.n_mp + x2 * 2 + c2))
        return pairs

    def core(self, v):
        return lax.ppermute(v, AXES, self.perm(lambda z, y, x, c: (z, y, x, 1 - c)))

    def x(self, v):
        return lax.ppermute(v, AXES, self.perm(lambda z, y, x, c: (z, y, 1 - x, c)))

    def cross(self, v):
        return lax.ppermute(v, AXES, self.perm(lambda z, y, x, c: (z, y, 1 - x, 1 - c)))

    def y(self, v):
        return lax.ppermute(v, AXES, self.perm(lambda z, y, x, c: (z, 1 - y, x, c)))

    def z(self, v, r):
        return lax.ppermute(v, AXES, self.perm(lambda z, y, x, c: ((z + r) % self.n_z, y, x, c)))


def gather_line(net, shard):
    if not net.fast:
        return [shard]
    return [shard] + [net.z(shard, r) for r in range(1, net.n_z)]


def stacked(net, line, span):
    if not net.fast:
        return line[0][:, span]
    return jnp.stack([piece[:, span] for piece in line])


class Plane:
    def __init__(self, net, line, near):
        self.net, self.line, self.near = net, line, near
        if net.fast:
            self.near_in = [net.y(line), net.x(line)]
        else:
            own = lax.all_gather(line, "dp", axis=0, tiled=True)[None]
            self.near_in = [own, net.x(own)]
        self.far_in = []

    def turn(self):
        if self.net.fast:
            y_all, x_all = self.near_in
            self.far_in = [self.net.x(y_all[:2]), self.net.y(x_all[2:])]

    def own(self):
        if not self.net.fast:
            return [(self.near_in[0], None, 0, 0)]
        return [(self.line, self.near, 0, 0), (self.near_in[0], self.near, 0, 1)]

    def other(self):
        if not self.net.fast:
            return [(self.near_in[1], None, 0, 0)]
        return [
            (self.near_in[1], self.near, 0, 0),
            (self.far_in[0], self.near, 0, 1),
            (self.far_in[1], self.near, 2, 1),
        ]


def block_row(net, pos, near, rank, flip):
    z = lax.rem(pos[0] + net.n_z + rank, net.n_z) if near else rank
    y = pos[1] if not flip else 1 - pos[1]
    return z * 2 + y


def assemble(net, target, pieces, metas, pos):
    for ref, (near, first, flip) in zip(pieces, metas):
        if near is None:
            target[...] = ref[0]
            continue
        rows = D // net.n_dp
        for index in range(ref.shape[0]):
            rank = first + index
            block = block_row(net, pos, near, -rank if near else rank, flip)
            start = pl.multiple_of(block * rows, 16)
            target[pl.ds(start, rows), :] = ref[index, 0:rows, :]


def ceil_to(n, m):
    return -(-n // m) * m


def turned(value):
    rows, cols = value.shape
    padded = jnp.pad(value, ((0, ceil_to(rows, 128) - rows), (0, ceil_to(cols, 128) - cols)))
    return padded.T[:cols, :rows]


def pack_attend_kernel(qkv_ref, out_ref, gain_ref, pack_ref):
    rows, width = qkv_ref.shape[1:]
    parts = [qkv_ref[member].astype(BF) for member in range(3)] + [turned(out_ref[...]).astype(BF)]
    for member, part in enumerate(parts):
        pack_ref[0:rows, member * width : (member + 1) * width] = part
    if pack_ref.shape[0] > rows:
        gains = jnp.pad(gain_ref[...], ((0, 6), (0, 4 * width - rows)))
        pack_ref[rows:, :] = gains.astype(BF)


def pack_attend(net, w_qkv, w_out, gains):
    _, rows, width = w_qkv.shape
    total = rows + 8 if net.fast else rows
    return pl.pallas_call(
        pack_attend_kernel,
        grid=(1,),
        in_specs=[whole(w_qkv.shape), whole(w_out.shape), whole(gains.shape)],
        out_specs=whole((total, 4 * width)),
        out_shape=jax.ShapeDtypeStruct((total, 4 * width), BF),
        compiler_params=params(),
        name="pack_attend",
    )(hbm(w_qkv), hbm(w_out), hbm(gains))


def pack_feed_kernel(gu_ref, down_ref, pack_ref):
    units = gu_ref.shape[2] // 2
    for part in range(2):
        span = slice(part * units, (part + 1) * units)
        base = 3 * part * units
        pack_ref[:, base : base + units] = gu_ref[0, :, span].astype(BF)
        pack_ref[:, base + units : base + 2 * units] = gu_ref[1, :, span].astype(BF)
        pack_ref[:, base + 2 * units : base + 3 * units] = down_ref[:, span].astype(BF)


def pack_feed(w_gu, w_down):
    _, rows, units = w_gu.shape
    return pl.pallas_call(
        pack_feed_kernel,
        grid=(1,),
        in_specs=[whole(w_gu.shape), whole(w_down.shape)],
        out_specs=whole((rows, 3 * units)),
        out_shape=jax.ShapeDtypeStruct((rows, 3 * units), BF),
        compiler_params=params(),
        name="pack_feed",
    )(hbm(w_gu), hbm(w_down))


def spread_gains(net, gain_ref, pieces, pos):
    rows = D // net.n_dp
    for block in range(net.n_dp):
        rank = lax.rem(pos[0] + net.n_z - block // 2, net.n_z)
        here = pieces[0][rank].astype(F32)[rows : rows + 8, :rows]
        there = pieces[1][rank].astype(F32)[rows : rows + 8, :rows]
        gain_ref[:, block * rows : (block + 1) * rows] = jnp.where(pos[1] == block % 2, here, there)


def row_tiles(rows, size):
    return [slice(start, start + size) for start in range(0, rows, size)]


def project_kernel(net, metas, first, pos, x_ref, *refs):
    if not net.fast and first:
        given, refs = refs[0], refs[1:]
    count = len(metas)
    pieces, refs = refs[:count], refs[count:]
    if first:
        h_ref, gain_ref, refs = refs[0], refs[1], refs[2:]
    qkv_ref, wqkv_ref, wout_ref, full = refs
    assemble(net, full, pieces, metas, pos)
    wqkv_ref[...] = full[:, : wqkv_ref.shape[1]]
    wout_ref[...] = full[:, wqkv_ref.shape[1] :]
    if first and net.fast:
        spread_gains(net, gain_ref, pieces, pos)
    elif first:
        gain_ref[...] = given[...]
    for tile in row_tiles(x_ref.shape[0], TILE):
        if first:
            value = x_ref[tile, :].astype(F32)
            inverse = lax.rsqrt(jnp.mean(value * value, axis=1, keepdims=True) + NORM_EPS)
            rows = (value * inverse * gain_ref[0:1, :]).astype(BF)
            h_ref[tile, :] = rows
        else:
            rows = x_ref[tile, :]
        qkv_ref[tile, :] = dot_nn(rows, wqkv_ref[...]).astype(BF)


def project(net, pos, x, pieces, head_width, gains=None, first=False):
    rows = x.shape[0]
    arrays = [x] + ([gains] if first and not net.fast else []) + [p[0] for p in pieces]
    metas = [p[1:] for p in pieces]
    outs = [((rows, 3 * head_width), BF), ((D, 3 * head_width), BF), ((D, head_width), BF)]
    if first:
        outs = [((rows, D), BF), ((8, D), F32)] + outs
    return in_vmem(
        functools.partial(project_kernel, net, metas, first),
        "project",
        [pos],
        arrays,
        outs,
        [((D, 4 * head_width), BF)],
        2 * rows * D * 3 * head_width,
    )


def key_valid(meta, seq, count, axis, shape, start):
    place = lax.broadcasted_iota(jnp.int32, shape, axis) + start + meta[count + seq]
    place = jnp.where(place >= L, place - L, place)
    return place < meta[seq]


def attend_kernel(heads, seqs, meta, qkv_ref, o_ref, lse_ref):
    width = heads * DH
    lane = lax.broadcasted_iota(jnp.int32, (TILE, 128), 1)

    def rows(seq, valid, step, carry):
        start = pl.multiple_of(seq * L + step * TILE, TILE)
        queries = qkv_ref[pl.ds(start, TILE), 0:width]
        logs = jnp.zeros((TILE, 128), F32)
        outs = []
        for head in range(heads):
            keys = qkv_ref[seq * L : (seq + 1) * L, width + head * DH : width + (head + 1) * DH]
            values = qkv_ref[seq * L : (seq + 1) * L, 2 * width + head * DH : 2 * width + (head + 1) * DH]
            scores = dot_nt(queries[:, head * DH : (head + 1) * DH], keys) * SCALE2
            scores = jnp.where(valid, scores, MASK_FILL)
            top = jnp.max(scores, axis=1, keepdims=True)
            expo = jnp.exp2(scores - top)
            total = jnp.sum(expo, axis=1, keepdims=True)
            mixed = dot_nn(expo.astype(BF), values)
            outs.append(mixed / total)
            logs = jnp.where(lane == head, top + jnp.log2(total), logs)
        o_ref[pl.ds(start, TILE), :] = jnp.concatenate(outs, axis=1).astype(BF)
        lse_ref[:, pl.ds(start, TILE)] = logs.T[0:8]
        return carry

    for seq in range(seqs):
        valid = key_valid(meta, seq, seqs, 1, (1, L), 0)
        lax.fori_loop(0, L // TILE, functools.partial(rows, seq, valid), 0)


def attend(meta, qkv, head_width, seqs):
    rows = qkv.shape[0]
    return in_vmem(
        functools.partial(attend_kernel, head_width // DH, seqs),
        "attend",
        [meta],
        [qkv],
        [((rows, head_width), BF), ((8, rows), F32)],
        flops=16 * rows * L * head_width,
    )


def attend_back_kernel(heads, seqs, block, meta, qkv_ref, do_ref, o_ref, lse_ref, out_ref, inner, dq_acc):
    width = heads * DH
    lane = lax.broadcasted_iota(jnp.int32, (TILE, 128), 1)

    def keys_of(seq, step, carry):
        span = slice(seq * L, (seq + 1) * L)
        offset = pl.multiple_of(step * block, block)
        start = pl.multiple_of(seq * L + step * block, block)
        valid = key_valid(meta, seq, seqs, 0, (block, 1), offset)
        for head in range(heads):
            cols = slice(head * DH, (head + 1) * DH)
            queries = qkv_ref[span, cols]
            grads = do_ref[span, cols]
            keys = qkv_ref[pl.ds(start, block), width + head * DH : width + (head + 1) * DH]
            values = qkv_ref[pl.ds(start, block), 2 * width + head * DH : 2 * width + (head + 1) * DH]
            scores = dot_nt(keys, queries) * SCALE2 - lse_ref[head : head + 1, span]
            probs = jnp.where(valid, jnp.exp2(scores), 0.0)
            grad_probs = dot_nt(values, grads)
            grad_scores = (probs * (grad_probs - inner[head : head + 1, :])).astype(BF)
            grad_values = dot_nn(probs.astype(BF), grads)
            grad_keys = dot_nn(grad_scores, queries) * SCALE
            out_ref[pl.ds(start, block), width + head * DH : width + (head + 1) * DH] = grad_keys.astype(BF)
            out_ref[pl.ds(start, block), 2 * width + head * DH : 2 * width + (head + 1) * DH] = (
                grad_values.astype(BF)
            )
            dq_acc[cols, :] += dot_tn(keys, grad_scores)
        return carry

    for seq in range(seqs):
        dq_acc[...] = jnp.zeros_like(dq_acc)
        for part in range(L // TILE):
            rows = slice(seq * L + part * TILE, seq * L + (part + 1) * TILE)
            product = do_ref[rows, :].astype(F32) * o_ref[rows, :].astype(F32)
            sums = jnp.zeros((TILE, 128), F32)
            for head in range(heads):
                one = jnp.sum(product[:, head * DH : (head + 1) * DH], axis=1, keepdims=True)
                sums = jnp.where(lane == head, one, sums)
            inner[:, part * TILE : (part + 1) * TILE] = sums.T[0:8]
        lax.fori_loop(0, L // block, functools.partial(keys_of, seq), 0)
        out_ref[seq * L : (seq + 1) * L, 0:width] = (dq_acc[...] * SCALE).T.astype(BF)


def attend_back(meta, qkv, grad, mixed, lse, head_width, seqs):
    rows = qkv.shape[0]
    return in_vmem(
        functools.partial(attend_back_kernel, head_width // DH, seqs, TILE),
        "attend_back",
        [meta],
        [qkv, grad, mixed, lse],
        [((rows, 3 * head_width), BF)],
        [((8, L), F32), ((head_width, L), F32)],
        40 * rows * L * head_width,
    )[0]


def feed_kernel(net, metas, units, first, pos, h_ref, dy_ref, *refs):
    groups = []
    for group in metas:
        groups.append(refs[: len(group)])
        refs = refs[len(group) :]
    if not first:
        f_prev, d_prev, refs = refs[0], refs[1], refs[2:]
    mid_refs, (f_ref, d_ref, full) = refs[:2], refs[2:]
    for index, group in enumerate(metas):
        assemble(net, full.at[index], groups[index], group, pos)
    root = math.sqrt(2.0 / math.pi)
    for tile in row_tiles(h_ref.shape[0], FEED_TILE):
        hidden_in, back_in = h_ref[tile, :], dy_ref[tile, :]
        f_part = d_part = 0.0
        for index in range(2):
            w_gate, w_up, w_down = (full[index, :, j * units : (j + 1) * units] for j in range(3))
            gate = dot_nn(hidden_in, w_gate)
            up = dot_nn(hidden_in, w_up)
            grad_hidden = dot_nn(back_in, w_down)
            square = gate * gate
            tanh = jnp.tanh(gate * (root + (root * 0.044715) * square))
            half = 0.5 * (1.0 + tanh)
            gelu = gate * half
            slope = half + (0.5 * gate) * (1.0 - tanh * tanh) * (root + (3.0 * root * 0.044715) * square)
            hidden = (gelu * up).astype(BF)
            grad_gate = (grad_hidden * up * slope).astype(BF)
            grad_up = (grad_hidden * gelu).astype(BF)
            mid_ref = mid_refs[index]
            mid_ref[tile, 0:units] = grad_gate
            mid_ref[tile, units : 2 * units] = grad_up
            mid_ref[tile, 2 * units : 3 * units] = hidden
            f_part += dot_nt(hidden, w_down)
            d_part += dot_nt(grad_gate, w_gate) + dot_nt(grad_up, w_up)
        if not first:
            f_part += f_prev[tile, :].astype(F32)
            d_part += d_prev[tile, :].astype(F32)
        f_ref[tile, :] = f_part.astype(BF)
        d_ref[tile, :] = d_part.astype(BF)


def feed(net, pos, h2, back, groups, units, previous):
    rows = h2.shape[0]
    arrays = [h2, back] + [p[0] for group in groups for p in group] + list(previous)
    metas = [[p[1:] for p in group] for group in groups]
    return in_vmem(
        functools.partial(feed_kernel, net, metas, units, not previous),
        "feed",
        [pos],
        arrays,
        [((rows, 3 * units), BF)] * 2 + [((rows, D), BF)] * 2,
        [((2, D, 3 * units), BF)],
        2 * rows * D * 12 * units,
    )


def second_kernel(x_ref, a_ref, b_ref, gain_ref, h_ref):
    tiles = row_tiles(x_ref.shape[0], TILE)
    for index, tile in enumerate(tiles):
        other = tiles[(index + len(tiles) // 2) % len(tiles)]
        value = x_ref[tile, :].astype(F32) + (a_ref[tile, :].astype(F32) + b_ref[other, :].astype(F32))
        inverse = lax.rsqrt(jnp.mean(value * value, axis=1, keepdims=True) + NORM_EPS)
        h_ref[tile, :] = (value * inverse * gain_ref[1:2, :]).astype(BF)


def second_norm(x, a_own, a_other, gain):
    return in_vmem(second_kernel, "second_norm", [], [x, a_own, a_other, gain], [(x.shape, BF)], (), 10 * x.size)[0]


def middle_kernel(x_ref, a_ref, b_ref, dy_ref, d_ref, e_ref, gain_ref, wo_ref, wx_ref,
                  da_ref, do_ref, dx_ref, dx2_ref):
    gain = gain_ref[1:2, :]
    tiles = row_tiles(x_ref.shape[0], TILE)
    for index, tile in enumerate(tiles):
        other = tiles[(index + len(tiles) // 2) % len(tiles)]
        second_in = x_ref[tile, :].astype(F32) + (a_ref[tile, :].astype(F32) + b_ref[other, :].astype(F32))
        inverse = lax.rsqrt(jnp.mean(second_in * second_in, axis=1, keepdims=True) + NORM_EPS)
        normed = second_in * inverse
        grad = d_ref[tile, :].astype(F32) + e_ref[other, :].astype(F32)
        scaled = grad * gain
        center = jnp.mean(scaled * normed, axis=1, keepdims=True)
        total = dy_ref[tile, :].astype(F32) + inverse * (scaled - normed * center)
        low = total.astype(BF)
        da_ref[tile, :] = low
        do_ref[tile, :] = dot_nn(low, wo_ref[...]).astype(BF)
        dx_ref[tile, :] = dot_nn(low, wx_ref[...]).astype(BF)
        if index < len(tiles) // 2:
            dx2_ref[tile, :] = total


def middle(x, a_own, a_other, back, d_own, d_other, gain, w_own, w_other):
    rows = x.shape[0]
    width = w_own.shape[1]
    return in_vmem(
        middle_kernel,
        "middle",
        [],
        [x, a_own, a_other, back, d_own, d_other, gain, w_own, w_other],
        [((rows, D), BF), ((rows, width), BF), ((rows, width), BF), ((rows // 2, D), F32)],
        (),
        4 * rows * D * width,
    )


def grad_kernel(net, near, spans, pos, left_ref, right_ref, mid_ref, tail_ref, *refs):
    outs, full = refs[:-1], refs[-1]
    for source, other, target, size in spans:
        left = (left_ref, right_ref)[source]
        values = (mid_ref, tail_ref)[other[0]][:, other[1] : other[1] + size]
        full[:, target : target + size] = dot_tn(left[...], values).astype(BF)
    if len(outs) == 1:
        outs[0][...] = full[...]
        return
    rows = D // net.n_dp
    slots = []
    for flip in range(2):
        for rank in range(net.n_z):
            slots.append((flip, rank))
    for out in outs:
        for index in range(out.shape[0]):
            flip, rank = slots.pop(0)
            block = block_row(net, pos, near, rank, flip)
            start = pl.multiple_of(block * rows, 16)
            out[index] = full[pl.ds(start, rows), :]


def grad_pack(net, pos, left, right, mid, tail, spans, width, near, split):
    rows = left.shape[0]
    outs = [((n, D // net.n_dp, width), BF) for n in split] if net.fast else [((D, width), BF)]
    return in_vmem(
        functools.partial(grad_kernel, net, near, spans),
        "weight_grad",
        [pos],
        [left, right, mid, tail],
        outs,
        [((D, width), BF)],
        2 * rows * D * width,
    )


def add_low(a, b):
    return (a.astype(F32) + b.astype(F32)).astype(BF)


def sum_kernel(*refs):
    ins, outs = refs[:-4], refs[-4:]
    for pack in range(len(ins) // 3):
        own, across, along = ins[3 * pack : 3 * pack + 3]
        width = own.shape[2]
        span = slice(pack * width, (pack + 1) * width)
        for rank, out in enumerate(outs):
            total = own[rank].astype(F32) + (across[rank].astype(F32) + along[rank].astype(F32))
            out[:, span] = total.astype(out.dtype)


def sum_plane(parts):
    _, rows, width = parts[0].shape
    shape = (rows, width * (len(parts) // 3))
    return in_vmem(sum_kernel, "sum_plane", [], parts, [(shape, F32)] + [(shape, BF)] * 3, (), 100 * rows * width)


def turn_kernel(x_ref, y_ref, lo_ref, hi_ref, x_out, y_out):
    x_out[0:2] = x_ref[0:2]
    x_out[2:4] = (x_ref[2:4].astype(F32) + hi_ref[...].astype(F32)).astype(BF)
    y_out[0:2] = (y_ref[0:2].astype(F32) + lo_ref[...].astype(F32)).astype(BF)
    y_out[2:4] = y_ref[2:4]


class Scatter:
    def __init__(self, net, other):
        self.net = net
        self.other = other
        self.far_in = [net.x(other[1]), net.y(other[2])] if net.fast else []

    def own(self, own):
        if self.net.fast:
            self.o_all, self.y_all = own
        else:
            total = own[0].astype(F32) + self.net.x(self.other[0]).astype(F32)
            self.pieces = lax.psum_scatter(total, "dp", scatter_dimension=0, tiled=True)

    def turn(self):
        self.sums, self.near_in = [], []
        if self.net.fast:
            x_all = self.other[0]
            parts = [x_all, self.y_all] + list(self.far_in)
            self.sums = in_vmem(turn_kernel, "turn", [], parts, [(x_all.shape, BF)] * 2, (), 2 * x_all.size)
            self.near_in = [self.net.x(self.sums[0]), self.net.y(self.sums[1])]


def finish(net, scatters):
    if not net.fast:
        total = jnp.concatenate([s.pieces for s in scatters], axis=1)
        return [total], ()
    sums = sum_plane(sum(([s.o_all] + s.near_in for s in scatters), []))
    return [sums[0]] + [net.z(sums[r], r) for r in range(1, net.n_z)], sums[0]


def adamw(outs, ins, place, gradient, rate, decay):
    weight, moment, second = (ref[place] for ref in ins)
    moment = BETA_ONE * moment + (1.0 - BETA_ONE) * gradient
    second = BETA_TWO * second + (1.0 - BETA_TWO) * gradient * gradient
    fix_one = 1.0 - BETA_ONE**STEP
    fix_two = 1.0 - BETA_TWO**STEP
    update = moment / fix_one / (jnp.sqrt(second / fix_two) + ADAM_EPS)
    outs[0][place] = weight - rate * (update + decay * weight)
    outs[1][place] = moment
    outs[2][place] = second


def total_of(refs, span):
    total = refs[0][:, span].astype(F32)
    for ref in refs[1:]:
        total += ref[:, span].astype(F32)
    return total


def put_row(out_ref, column):
    row = turned(column)
    out_ref[...] = jnp.zeros_like(out_ref)
    out_ref[0:1, 0 : row.shape[1]] = row


def adam_attend_kernel(count, *refs):
    pieces, refs = refs[:count], refs[count:]
    qkv, out, qkv_new, out_new, gain_ref = refs[0:3], refs[3:6], refs[6:9], refs[9:12], refs[12]
    width = qkv[0].shape[2]
    column = 0.0
    for member in range(3):
        gradient = total_of(pieces, slice(member * width, (member + 1) * width))
        low = qkv[0][member].astype(BF).astype(F32)
        column += jnp.sum(low * gradient, axis=1, keepdims=True)
        adamw(qkv_new, qkv, member, gradient, D ** (-0.5), DECAY_RATE)
    gradient = turned(total_of(pieces, slice(3 * width, 4 * width)))
    adamw(out_new, out, ..., gradient, max(1, 3 * HD // L) ** (-0.5), DECAY_RATE)
    put_row(gain_ref, column)


def adam_feed_kernel(count, *refs):
    pieces, refs = refs[:count], refs[count:]
    gu, down, gu_new, down_new, gain_ref = refs[0:3], refs[3:6], refs[6:9], refs[9:12], refs[12]
    units = gu[0].shape[2] // 2
    column = 0.0
    for part in range(2):
        span = slice(part * units, (part + 1) * units)
        base = 3 * part * units
        for member in range(2):
            gradient = total_of(pieces, slice(base + member * units, base + (member + 1) * units))
            low = gu[0][member, :, span].astype(BF).astype(F32)
            column += jnp.sum(low * gradient, axis=1, keepdims=True)
            adamw(gu_new, gu, (member, slice(None), span), gradient, D ** (-0.5), DECAY_RATE)
        gradient = total_of(pieces, slice(base + 2 * units, base + 3 * units))
        adamw(down_new, down, (slice(None), span), gradient, FF ** (-0.5), DECAY_RATE)
    put_row(gain_ref, column)


def adam_call(kernel, pieces, states, name):
    shapes = [jax.ShapeDtypeStruct(s.shape, F32) for s in states] + [jax.ShapeDtypeStruct((8, 128), F32)]
    return pl.pallas_call(
        functools.partial(kernel, len(pieces)),
        grid=(1,),
        in_specs=[whole(a.shape) for a in list(pieces) + list(states)],
        out_specs=[whole(s.shape) for s in shapes],
        out_shape=shapes,
        compiler_params=params(),
        cost_estimate=cost(20 * sum(s.size for s in states), 10 * sum(s.size for s in states)),
        name=name,
    )(*pieces, *[hbm(a) for a in states])


def gain_step(weight, moment, second, gradient):
    moment_new = BETA_ONE * moment + (1.0 - BETA_ONE) * gradient
    second_new = BETA_TWO * second + (1.0 - BETA_TWO) * gradient * gradient
    fix_one = 1.0 - BETA_ONE**STEP
    fix_two = 1.0 - BETA_TWO**STEP
    update = moment_new / fix_one / (jnp.sqrt(second_new / fix_two) + ADAM_EPS)
    return (weight - GAIN_RATE * update, moment_new, second_new)


def body(
    net,
    inputs,
    cotangent,
    lengths,
    gains,
    w_qkv,
    m_qkv,
    v_qkv,
    w_out,
    m_out,
    v_out,
    w_gu,
    m_gu,
    v_gu,
    w_down,
    m_down,
    v_down,
    m_gain,
    v_gain,
):
    own_rows = inputs.shape[0]
    rows = 2 * own_rows
    shard = w_qkv.shape[1]
    width = w_qkv.shape[2]
    half_units = w_gu.shape[2] // 2
    dp, mp = lax.axis_index("dp"), lax.axis_index("mp")
    core = lax.rem(mp, 2)
    pos = jnp.stack([dp // 2, lax.rem(dp, 2)]).astype(jnp.int32)

    if own_rows % L == 0:
        each = own_rows // L
        seqs = 2 * each
        pair = mp + 1 - 2 * core
        own_len = lax.dynamic_slice(lengths, (mp * each,), (each,))
        other_len = lax.dynamic_slice(lengths, (pair * each,), (each,))
        meta = jnp.concatenate([own_len, other_len, jnp.zeros((seqs,), jnp.int32)])
    else:
        seqs = rows // L
        len_here = lax.dynamic_slice(lengths, ((mp // 2) * seqs,), (seqs,))
        meta = jnp.concatenate([len_here, jnp.full((seqs,), core * own_rows, jnp.int32)])

    x_in = net.core(inputs)
    back_in = net.core(cotangent)
    pack_a = pack_attend(net, w_qkv, w_out, gains)
    line_a = gather_line(net, pack_a)
    stack_a = stacked(net, line_a, slice(0, 4 * width))
    line_f = gather_line(net, pack_feed(after(w_gu, stack_a), w_down.T))
    plane_a = Plane(net, stack_a, True)
    gain_given = None
    if not net.fast:
        gain_all = lax.all_gather(gains.astype(BF), "dp", axis=1, tiled=True).astype(F32)
        gain_given = jnp.pad(gain_all, ((0, 6), (0, 0)))

    x_pair = jnp.concatenate([inputs, x_in], axis=0)
    back = jnp.concatenate([cotangent, back_in], axis=0)
    x_pair, back = together(x_pair, back)
    plane_a.turn()
    h1, gain_wide, qkv_own, wqkv_own, wout_own = project(net, pos, x_pair, plane_a.own(), width, gain_given, True)
    o_own, lse_own = attend(meta, qkv_own, width, seqs)
    o_own, plane_a.far_in, line_f = together(o_own, plane_a.far_in, line_f)

    pack_width = 3 * half_units
    feed_one = Plane(net, stacked(net, line_f, slice(0, pack_width)), True)
    h1_late = after(h1, o_own)
    qkv_other, wqkv_other, wout_other = project(net, pos, h1_late, plane_a.other(), width)
    o_other, lse_other = attend(meta, qkv_other, width, seqs)
    o_other, feed_one.near_in = together(o_other, feed_one.near_in)
    feed_one.turn()

    branch = (dot_nt(o_own, wout_own) + dot_nt(o_other, wout_other)).astype(BF)
    branch_in = net.core(branch)
    line_f = after(line_f, feed_one.near_in)
    feed_two = Plane(net, stacked(net, line_f, slice(pack_width, 2 * pack_width)), True)
    h2 = second_norm(x_pair, branch, branch_in, gain_wide)

    f_spans = [(0, (0, 0), 0, 2 * half_units), (1, (0, 2 * half_units), 2 * half_units, half_units)]

    def feed_grads(mid_own, mid_other):
        g_other = grad_pack(net, pos, h2, back, mid_other, mid_other, f_spans, pack_width, True, (4, 2, 2))
        total = Scatter(net, g_other)
        g_own = grad_pack(net, pos, h2, back, mid_own, mid_own, f_spans, pack_width, True, (4, 4))
        total.own(g_own)
        return total, (g_own[0], g_other[0])

    groups = [feed_one.own(), feed_one.other()]
    mid_own, mid_other, f_part, d_part = feed(net, pos, h2, back, groups, half_units, [])
    mid_own, mid_other, f_part, d_part, feed_two.near_in = together(
        mid_own, mid_other, f_part, d_part, feed_two.near_in
    )
    feed_two.turn()
    sum_one, done_one = feed_grads(mid_own, mid_other)
    previous = after([f_part, d_part], done_one)
    groups = [feed_two.own(), feed_two.other()]
    mid_own, mid_other, f_part, d_part = feed(net, pos, h2, back, groups, half_units, previous)
    mid_own, mid_other, f_part, d_part, sum_one.far_in = together(
        mid_own, mid_other, f_part, d_part, sum_one.far_in
    )
    d_in = net.core(d_part)
    sum_one.turn()
    mid_own, mid_other = after((mid_own, mid_other), sum_one.sums)
    sum_two, done_two = feed_grads(mid_own, mid_other)
    d_in = after(d_in, done_two)

    da, do_own, do_other, dx2 = middle(
        x_pair, branch, branch_in, back, d_part, d_in, gain_wide, wout_own, wout_other
    )
    da, do_own, do_other, dx2, sum_one.near_in, sum_two.far_in = together(
        da, do_own, do_other, dx2, sum_one.near_in, sum_two.far_in
    )
    sum_two.turn()
    do_other = after(do_other, sum_two.sums)
    dqkv_other = attend_back(meta, qkv_other, do_other, o_other, lse_other, width, seqs)
    dqkv_other, sum_two.near_in = together(dqkv_other, sum_two.near_in)
    a_spans = [(0, (0, 0), 0, 3 * width), (1, (1, 0), 3 * width, width)]
    g_other = grad_pack(net, pos, h1, da, dqkv_other, o_other, a_spans, 4 * width, True, (4, 2, 2))
    sum_a = Scatter(net, g_other)
    pieces_f, mark_f = finish(net, [sum_one, sum_two])
    do_own = after(do_own, (g_other, mark_f))
    dqkv_own = attend_back(meta, qkv_own, do_own, o_own, lse_own, width, seqs)
    dqkv_own, sum_a.far_in, pieces_f = together(dqkv_own, sum_a.far_in, pieces_f)
    g_own = grad_pack(net, pos, h1, da, dqkv_own, o_own, a_spans, 4 * width, True, (4, 4))
    sum_a.own(g_own)
    sum_a.turn()
    f_in = net.core(after(f_part[own_rows:], sum_a.sums))

    x_own = inputs.astype(F32)
    second_in = x_own + (branch[:own_rows].astype(F32) + branch_in[own_rows:].astype(F32))
    output = (second_in + (f_part[:own_rows].astype(F32) + f_in.astype(F32))).astype(BF)
    states_f = [w_gu, m_gu, v_gu, w_down.T, m_down.T, v_down.T]
    feed_new = adam_call(adam_feed_kernel, after(pieces_f, sum_a.sums), states_f, "adam_feed")
    output, feed_new, sum_a.near_in = together(output, feed_new, sum_a.near_in)
    pieces_a, mark_a = finish(net, [sum_a])

    dqkv_own, dqkv_last = after((dqkv_own, dqkv_other), mark_a)
    dh1 = (dot_nt(dqkv_own, wqkv_own) + dot_nt(dqkv_last, wqkv_other)).astype(BF)
    dh1_in = net.core(dh1[own_rows:])
    grad_first = dh1[:own_rows].astype(F32) + dh1_in.astype(F32)
    r_own = lax.rsqrt(jnp.mean(x_own * x_own, axis=1, keepdims=True) + NORM_EPS)
    n_own = x_own * r_own
    scaled = grad_first * gain_wide[0]
    center = jnp.mean(scaled * n_own, axis=1, keepdims=True)
    input_grad = dx2 + r_own * (scaled - n_own * center)

    states_a = [w_qkv, m_qkv, v_qkv, w_out, m_out, v_out]
    pieces_a = after(pieces_a, input_grad)
    attend_new = adam_call(adam_attend_kernel, pieces_a, states_a, "adam_attend")
    terms = jnp.concatenate([attend_new[-1][0:1], feed_new[-1][0:1]], axis=0)
    total = terms + net.core(terms) + net.x(terms) + net.cross(terms)
    gain_grad = total[:, :shard] / round_low(gains)
    new_gains, gain_moment, gain_second = gain_step(gains, m_gain, v_gain, gain_grad)
    return (
        (output, input_grad, new_gains, gain_moment, gain_second)
        + tuple(attend_new[:6])
        + tuple(feed_new[:3])
        + tuple(v.T for v in feed_new[3:6])
    )


def solution(mesh):
    net = Net(mesh.shape["dp"], mesh.shape["mp"])
    rows = P(("dp", "mp"), None)
    gain = P(None, "dp")
    wide = P(None, "dp", "mp")
    tall = P("mp", "dp")
    return jax.shard_map(
        functools.partial(body, net),
        mesh=mesh,
        in_specs=(rows, rows, P("dp"), gain) + (wide,) * 3 + (tall,) * 3 + (wide,) * 3 + (tall,) * 3 + (gain,) * 2,
        out_specs=(rows, rows) + (gain,) * 3 + (wide,) * 3 + (tall,) * 3 + (wide,) * 3 + (tall,) * 3,
        check_vma=False,
    )
```

```python
import functools
import math

import jax
import jax.numpy as jnp
from jax import lax
from jax.experimental import pallas as pl
from jax.experimental.pallas import tpu as pltpu
from jax.sharding import PartitionSpec as P

D = 768
DH = 64
FF = 2048
L = 1024
STEP = 10
HD = 768

NORM_EPS = 1e-06
MASK_FILL = -1e30
BETA_ONE = 0.5
BETA_TWO = 0.5
ADAM_EPS = 1e-08
DECAY_RATE = 0.01
GAIN_RATE = 0.5

AXES = ("dp", "mp")
BF = jnp.bfloat16
F32 = jnp.float32
SCALE = DH ** (-0.5)
SCALE2 = SCALE * math.log2(math.e)
VMEM_LIMIT = 24 * 1024 * 1024
TILE = 256
FEED_TILE = 512
COST_CUT = 1


def params(**kw):
    return pltpu.CompilerParams(vmem_limit_bytes=VMEM_LIMIT, **kw)


def cost(flops, nbytes, trans=0):
    return pl.CostEstimate(flops=int(flops) // COST_CUT, bytes_accessed=int(nbytes) // COST_CUT, transcendentals=0)


def round_low(value):
    return lax.reduce_precision(value, 8, 7)


def after(values, anchor):
    return lax.optimization_barrier((values, anchor))[0]


def dot_nn(a, b):
    return lax.dot_general(a, b, (((1,), (0,)), ((), ())), preferred_element_type=F32)


def dot_nt(a, b):
    return lax.dot_general(a, b, (((1,), (1,)), ((), ())), preferred_element_type=F32)


def dot_tn(a, b):
    return lax.dot_general(a, b, (((0,), (0,)), ((), ())), preferred_element_type=F32)


def together(*values):
    return lax.optimization_barrier(values)


def hbm(array):
    return pltpu.with_memory_space_constraint(array, pltpu.HBM)


SMEM_SPEC = pl.BlockSpec(memory_space=pltpu.SMEM)
VMEM_SPEC = pl.BlockSpec(memory_space=pltpu.VMEM)


def whole(shape):
    return pl.BlockSpec(shape, lambda *_: (0,) * len(shape))


def in_vmem(kernel, name, scalars, arrays, outs, scratch=(), flops=0):
    nbytes = sum(a.size * a.dtype.itemsize for a in arrays)
    return pl.pallas_call(
        kernel,
        in_specs=[SMEM_SPEC] * len(scalars) + [VMEM_SPEC] * len(arrays),
        out_specs=[VMEM_SPEC] * len(outs),
        out_shape=[pltpu.VMEM(shape, dtype) for shape, dtype in outs],
        scratch_shapes=[pltpu.VMEM(shape, dtype) for shape, dtype in scratch],
        compiler_params=params(),
        cost_estimate=cost(flops, nbytes),
        name=name,
    )(*scalars, *arrays)


class Net:
    def __init__(self, n_dp, n_mp):
        self.n_dp, self.n_mp = n_dp, n_mp
        self.n_y = 2
        self.n_z = n_dp // 2
        self.fast = n_dp == 8 and n_mp == 4 and (D // n_dp) % 16 == 0

    def perm(self, move):
        pairs = []
        for dp in range(self.n_dp):
            for mp in range(self.n_mp):
                z, y, x, c = dp // 2, dp % 2, mp // 2, mp % 2
                z2, y2, x2, c2 = move(z, y, x, c)
                pairs.append((dp * self.n_mp + mp, (z2 * 2 + y2) * self.n_mp + x2 * 2 + c2))
        return pairs

    def core(self, v):
        return lax.ppermute(v, AXES, self.perm(lambda z, y, x, c: (z, y, x, 1 - c)))

    def x(self, v):
        return lax.ppermute(v, AXES, self.perm(lambda z, y, x, c: (z, y, 1 - x, c)))

    def cross(self, v):
        return lax.ppermute(v, AXES, self.perm(lambda z, y, x, c: (z, y, 1 - x, 1 - c)))

    def y(self, v):
        return lax.ppermute(v, AXES, self.perm(lambda z, y, x, c: (z, 1 - y, x, c)))

    def z(self, v, r):
        return lax.ppermute(v, AXES, self.perm(lambda z, y, x, c: (z ^ r, y, x, c)))


def gather_line(net, shard):
    if not net.fast:
        return [shard]
    return [shard] + [net.z(shard, r) for r in range(1, net.n_z)]


def stacked(net, line):
    return jnp.stack(line) if net.fast else line[0]


class Plane:
    def __init__(self, net, line, near):
        self.net, self.line, self.near = net, line, near
        if net.fast:
            self.near_in = [net.y(line), net.x(line)]
        else:
            own = lax.all_gather(line, "dp", axis=0, tiled=True)[None]
            self.near_in = [own, net.x(own)]
        self.far_in, self.halves = [], ()

    def turn(self):
        if self.net.fast:
            y_all, x_all = self.near_in
            self.halves = (y_all[:2], x_all[2:])
            self.far_in = [self.net.x(self.halves[0]), self.net.y(self.halves[1])]

    def own(self):
        if not self.net.fast:
            return [(self.near_in[0], None, 0, 0)]
        return [(self.line, self.near, 0, 0), (self.near_in[0], self.near, 0, 1)]

    def other(self):
        if not self.net.fast:
            return [(self.near_in[1], None, 0, 0)]
        return [
            (self.near_in[1], self.near, 0, 0),
            (self.far_in[0], self.near, 0, 1),
            (self.far_in[1], self.near, 2, 1),
        ]


def block_row(net, pos, near, rank, flip):
    z = lax.bitwise_xor(pos[0], jnp.int32(rank)) if near else rank
    y = pos[1] if not flip else 1 - pos[1]
    return z * 2 + y


def assemble(net, target, pieces, metas, pos):
    for ref, (near, first, flip) in zip(pieces, metas):
        if near is None:
            target[...] = ref[0]
            continue
        rows = D // net.n_dp
        for index in range(ref.shape[0]):
            rank = first + index
            block = block_row(net, pos, near, rank, flip)
            start = pl.multiple_of(block * rows, 16)
            target[pl.ds(start, rows), :] = ref[index, 0:rows, :]


def ceil_to(n, m):
    return -(-n // m) * m


def turned(value):
    rows, cols = value.shape
    padded = jnp.pad(value, ((0, ceil_to(rows, 128) - rows), (0, ceil_to(cols, 128) - cols)))
    return padded.T[:cols, :rows]


def pack_attend_kernel(qkv_ref, out_ref, gain_ref, pack_ref):
    rows, width = qkv_ref.shape[1:]
    parts = [qkv_ref[member].astype(BF) for member in range(3)] + [turned(out_ref[...]).astype(BF)]
    for member, part in enumerate(parts):
        pack_ref[0:rows, member * width : (member + 1) * width] = part
    if pack_ref.shape[0] > rows:
        gains = jnp.pad(gain_ref[...], ((0, 6), (0, 4 * width - rows)))
        pack_ref[rows:, :] = gains.astype(BF)


def pack_attend(net, w_qkv, w_out, gains):
    _, rows, width = w_qkv.shape
    total = rows + 8 if net.fast else rows
    return pl.pallas_call(
        pack_attend_kernel,
        grid=(1,),
        in_specs=[whole(w_qkv.shape), whole(w_out.shape), whole(gains.shape)],
        out_specs=whole((total, 4 * width)),
        out_shape=jax.ShapeDtypeStruct((total, 4 * width), BF),
        compiler_params=params(),
        name="pack_attend",
    )(hbm(w_qkv), hbm(w_out), hbm(gains))


def pack_feed_kernel(gu_ref, down_ref, *pack_refs):
    units = gu_ref.shape[2] // 2
    for part, pack_ref in enumerate(pack_refs):
        span = slice(part * units, (part + 1) * units)
        pack_ref[:, 0:units] = gu_ref[0, :, span].astype(BF)
        pack_ref[:, units : 2 * units] = gu_ref[1, :, span].astype(BF)
        pack_ref[:, 2 * units : 3 * units] = down_ref[:, span].astype(BF)


def pack_feed(w_gu, w_down):
    _, rows, units = w_gu.shape
    shape = (rows, 3 * units // 2)
    return pl.pallas_call(
        pack_feed_kernel,
        grid=(1,),
        in_specs=[whole(w_gu.shape), whole(w_down.shape)],
        out_specs=[whole(shape)] * 2,
        out_shape=[jax.ShapeDtypeStruct(shape, BF)] * 2,
        compiler_params=params(),
        name="pack_feed",
    )(hbm(w_gu), hbm(w_down))


def spread_gains(net, gain_ref, pieces, pos):
    rows = D // net.n_dp
    for block in range(net.n_dp):
        rank = lax.bitwise_xor(pos[0], jnp.int32(block // 2))
        here = pieces[0][rank].astype(F32)[rows : rows + 8, :rows]
        there = pieces[1][rank].astype(F32)[rows : rows + 8, :rows]
        gain_ref[:, block * rows : (block + 1) * rows] = jnp.where(pos[1] == block % 2, here, there)


def row_tiles(rows, size):
    return [slice(start, start + size) for start in range(0, rows, size)]


def project_kernel(net, metas, first, pos, x_ref, *refs):
    if not net.fast and first:
        given, refs = refs[0], refs[1:]
    count = len(metas)
    pieces, refs = refs[:count], refs[count:]
    if first:
        h_ref, gain_ref, refs = refs[0], refs[1], refs[2:]
    qkv_ref, wqkv_ref, wout_ref, full = refs
    assemble(net, full, pieces, metas, pos)
    wqkv_ref[...] = full[:, : wqkv_ref.shape[1]]
    wout_ref[...] = full[:, wqkv_ref.shape[1] :]
    if first and net.fast:
        spread_gains(net, gain_ref, pieces, pos)
    elif first:
        gain_ref[...] = given[...]
    for tile in row_tiles(x_ref.shape[0], TILE):
        if first:
            value = x_ref[tile, :].astype(F32)
            inverse = lax.rsqrt(jnp.mean(value * value, axis=1, keepdims=True) + NORM_EPS)
            rows = (value * inverse * gain_ref[0:1, :]).astype(BF)
            h_ref[tile, :] = rows
        else:
            rows = x_ref[tile, :]
        qkv_ref[tile, :] = dot_nn(rows, wqkv_ref[...]).astype(BF)


def project(net, pos, x, pieces, head_width, gains=None, first=False):
    rows = x.shape[0]
    arrays = [x] + ([gains] if first and not net.fast else []) + [p[0] for p in pieces]
    metas = [p[1:] for p in pieces]
    outs = [((rows, 3 * head_width), BF), ((D, 3 * head_width), BF), ((D, head_width), BF)]
    if first:
        outs = [((rows, D), BF), ((8, D), F32)] + outs
    return in_vmem(
        functools.partial(project_kernel, net, metas, first),
        "project",
        [pos],
        arrays,
        outs,
        [((D, 4 * head_width), BF)],
        2 * rows * D * 3 * head_width,
    )


def key_valid(meta, seq, count, axis, shape, start):
    place = lax.broadcasted_iota(jnp.int32, shape, axis) + start + meta[count + seq]
    place = jnp.where(place >= L, place - L, place)
    return place < meta[seq]


def attend_kernel(heads, seqs, meta, qkv_ref, o_ref, lse_ref):
    width = heads * DH
    lane = lax.broadcasted_iota(jnp.int32, (TILE, 128), 1)

    def rows(seq, valid, step, carry):
        start = pl.multiple_of(seq * L + step * TILE, TILE)
        queries = qkv_ref[pl.ds(start, TILE), 0:width]
        logs = jnp.zeros((TILE, 128), F32)
        outs = []
        for head in range(heads):
            keys = qkv_ref[seq * L : (seq + 1) * L, width + head * DH : width + (head + 1) * DH]
            values = qkv_ref[seq * L : (seq + 1) * L, 2 * width + head * DH : 2 * width + (head + 1) * DH]
            scores = dot_nt(queries[:, head * DH : (head + 1) * DH], keys) * SCALE2
            scores = jnp.where(valid, scores, MASK_FILL)
            top = jnp.max(scores, axis=1, keepdims=True)
            expo = jnp.exp2(scores - top)
            total = jnp.sum(expo, axis=1, keepdims=True)
            mixed = dot_nn(expo.astype(BF), values)
            outs.append(mixed / total)
            logs = jnp.where(lane == head, top + jnp.log2(total), logs)
        o_ref[pl.ds(start, TILE), :] = jnp.concatenate(outs, axis=1).astype(BF)
        lse_ref[:, pl.ds(start, TILE)] = logs.T[0:8]
        return carry

    for seq in range(seqs):
        valid = key_valid(meta, seq, seqs, 1, (1, L), 0)
        lax.fori_loop(0, L // TILE, functools.partial(rows, seq, valid), 0)


def attend(meta, qkv, head_width, seqs):
    rows = qkv.shape[0]
    return in_vmem(
        functools.partial(attend_kernel, head_width // DH, seqs),
        "attend",
        [meta],
        [qkv],
        [((rows, head_width), BF), ((8, rows), F32)],
        flops=16 * rows * L * head_width,
    )


def attend_back_kernel(heads, seqs, block, meta, qkv_ref, do_ref, o_ref, lse_ref, out_ref, inner, dq_acc):
    width = heads * DH
    lane = lax.broadcasted_iota(jnp.int32, (TILE, 128), 1)

    def keys_of(seq, step, carry):
        span = slice(seq * L, (seq + 1) * L)
        offset = pl.multiple_of(step * block, block)
        start = pl.multiple_of(seq * L + step * block, block)
        valid = key_valid(meta, seq, seqs, 0, (block, 1), offset)
        for head in range(heads):
            cols = slice(head * DH, (head + 1) * DH)
            queries = qkv_ref[span, cols]
            grads = do_ref[span, cols]
            keys = qkv_ref[pl.ds(start, block), width + head * DH : width + (head + 1) * DH]
            values = qkv_ref[pl.ds(start, block), 2 * width + head * DH : 2 * width + (head + 1) * DH]
            scores = dot_nt(keys, queries) * SCALE2 - lse_ref[head : head + 1, span]
            probs = jnp.where(valid, jnp.exp2(scores), 0.0)
            grad_probs = dot_nt(values, grads)
            grad_scores = (probs * (grad_probs - inner[head : head + 1, :])).astype(BF)
            grad_values = dot_nn(probs.astype(BF), grads)
            grad_keys = dot_nn(grad_scores, queries) * SCALE
            out_ref[pl.ds(start, block), width + head * DH : width + (head + 1) * DH] = grad_keys.astype(BF)
            out_ref[pl.ds(start, block), 2 * width + head * DH : 2 * width + (head + 1) * DH] = (
                grad_values.astype(BF)
            )
            dq_acc[cols, :] += dot_tn(keys, grad_scores)
        return carry

    for seq in range(seqs):
        dq_acc[...] = jnp.zeros_like(dq_acc)
        for part in range(L // TILE):
            rows = slice(seq * L + part * TILE, seq * L + (part + 1) * TILE)
            product = do_ref[rows, :].astype(F32) * o_ref[rows, :].astype(F32)
            sums = jnp.zeros((TILE, 128), F32)
            for head in range(heads):
                one = jnp.sum(product[:, head * DH : (head + 1) * DH], axis=1, keepdims=True)
                sums = jnp.where(lane == head, one, sums)
            inner[:, part * TILE : (part + 1) * TILE] = sums.T[0:8]
        lax.fori_loop(0, L // block, functools.partial(keys_of, seq), 0)
        out_ref[seq * L : (seq + 1) * L, 0:width] = (dq_acc[...] * SCALE).T.astype(BF)


def attend_back(meta, qkv, grad, mixed, lse, head_width, seqs):
    rows = qkv.shape[0]
    return in_vmem(
        functools.partial(attend_back_kernel, head_width // DH, seqs, TILE),
        "attend_back",
        [meta],
        [qkv, grad, mixed, lse],
        [((rows, 3 * head_width), BF)],
        [((8, L), F32), ((head_width, L), F32)],
        40 * rows * L * head_width,
    )[0]


def feed_kernel(net, metas, units, first, pos, h_ref, dy_ref, *refs):
    groups = []
    for group in metas:
        groups.append(refs[: len(group)])
        refs = refs[len(group) :]
    if not first:
        f_prev, d_prev, refs = refs[0], refs[1], refs[2:]
    mid_refs, (f_ref, d_ref, full) = refs[:2], refs[2:]
    for index, group in enumerate(metas):
        assemble(net, full.at[index], groups[index], group, pos)
    root = math.sqrt(2.0 / math.pi)
    for tile in row_tiles(h_ref.shape[0], FEED_TILE):
        hidden_in, back_in = h_ref[tile, :], dy_ref[tile, :]
        f_part = d_part = 0.0
        for index in range(2):
            w_gate, w_up, w_down = (full[index, :, j * units : (j + 1) * units] for j in range(3))
            gate = dot_nn(hidden_in, w_gate)
            up = dot_nn(hidden_in, w_up)
            grad_hidden = dot_nn(back_in, w_down)
            square = gate * gate
            tanh = jnp.tanh(gate * (root + (root * 0.044715) * square))
            half = 0.5 * (1.0 + tanh)
            gelu = gate * half
            slope = half + (0.5 * gate) * (1.0 - tanh * tanh) * (root + (3.0 * root * 0.044715) * square)
            hidden = (gelu * up).astype(BF)
            grad_gate = (grad_hidden * up * slope).astype(BF)
            grad_up = (grad_hidden * gelu).astype(BF)
            mid_ref = mid_refs[index]
            mid_ref[tile, 0:units] = grad_gate
            mid_ref[tile, units : 2 * units] = grad_up
            mid_ref[tile, 2 * units : 3 * units] = hidden
            f_part += dot_nt(hidden, w_down)
            d_part += dot_nt(grad_gate, w_gate) + dot_nt(grad_up, w_up)
        if not first:
            f_part += f_prev[tile, :].astype(F32)
            d_part += d_prev[tile, :].astype(F32)
        f_ref[tile, :] = f_part.astype(BF)
        d_ref[tile, :] = d_part.astype(BF)


def feed(net, pos, h2, back, groups, units, previous):
    rows = h2.shape[0]
    arrays = [h2, back] + [p[0] for group in groups for p in group] + list(previous)
    metas = [[p[1:] for p in group] for group in groups]
    return in_vmem(
        functools.partial(feed_kernel, net, metas, units, not previous),
        "feed",
        [pos],
        arrays,
        [((rows, 3 * units), BF)] * 2 + [((rows, D), BF)] * 2,
        [((2, D, 3 * units), BF)],
        2 * rows * D * 12 * units,
    )


def second_kernel(x_ref, a_ref, b_ref, gain_ref, h_ref):
    tiles = row_tiles(x_ref.shape[0], TILE)
    for index, tile in enumerate(tiles):
        other = tiles[(index + len(tiles) // 2) % len(tiles)]
        value = x_ref[tile, :].astype(F32) + (a_ref[tile, :].astype(F32) + b_ref[other, :].astype(F32))
        inverse = lax.rsqrt(jnp.mean(value * value, axis=1, keepdims=True) + NORM_EPS)
        h_ref[tile, :] = (value * inverse * gain_ref[1:2, :]).astype(BF)


def second_norm(x, a_own, a_other, gain):
    return in_vmem(second_kernel, "second_norm", [], [x, a_own, a_other, gain], [(x.shape, BF)], (), 10 * x.size)[0]


def middle_kernel(x_ref, a_ref, b_ref, dy_ref, d_ref, e_ref, gain_ref, wo_ref, wx_ref,
                  da_ref, do_ref, dx_ref, dx2_ref):
    gain = gain_ref[1:2, :]
    tiles = row_tiles(x_ref.shape[0], TILE)
    for index, tile in enumerate(tiles):
        other = tiles[(index + len(tiles) // 2) % len(tiles)]
        second_in = x_ref[tile, :].astype(F32) + (a_ref[tile, :].astype(F32) + b_ref[other, :].astype(F32))
        inverse = lax.rsqrt(jnp.mean(second_in * second_in, axis=1, keepdims=True) + NORM_EPS)
        normed = second_in * inverse
        grad = d_ref[tile, :].astype(F32) + e_ref[other, :].astype(F32)
        scaled = grad * gain
        center = jnp.mean(scaled * normed, axis=1, keepdims=True)
        total = dy_ref[tile, :].astype(F32) + inverse * (scaled - normed * center)
        low = total.astype(BF)
        da_ref[tile, :] = low
        do_ref[tile, :] = dot_nn(low, wo_ref[...]).astype(BF)
        dx_ref[tile, :] = dot_nn(low, wx_ref[...]).astype(BF)
        if index < len(tiles) // 2:
            dx2_ref[tile, :] = total


def middle(x, a_own, a_other, back, d_own, d_other, gain, w_own, w_other):
    rows = x.shape[0]
    width = w_own.shape[1]
    return in_vmem(
        middle_kernel,
        "middle",
        [],
        [x, a_own, a_other, back, d_own, d_other, gain, w_own, w_other],
        [((rows, D), BF), ((rows, width), BF), ((rows, width), BF), ((rows // 2, D), F32)],
        (),
        4 * rows * D * width,
    )


def grad_kernel(net, near, spans, pos, left_ref, right_ref, mid_ref, tail_ref, *refs):
    outs, full = refs[:-1], refs[-1]
    for source, other, target, size in spans:
        left = (left_ref, right_ref)[source]
        values = (mid_ref, tail_ref)[other[0]][:, other[1] : other[1] + size]
        full[:, target : target + size] = dot_tn(left[...], values).astype(BF)
    if len(outs) == 1:
        outs[0][...] = full[...]
        return
    rows = D // net.n_dp
    slots = []
    for flip in range(2):
        for rank in range(net.n_z):
            slots.append((flip, rank))
    for out in outs:
        for index in range(out.shape[0]):
            flip, rank = slots.pop(0)
            block = block_row(net, pos, near, rank, flip)
            start = pl.multiple_of(block * rows, 16)
            out[index] = full[pl.ds(start, rows), :]


def grad_pack(net, pos, left, right, mid, tail, spans, width, near, split):
    rows = left.shape[0]
    outs = [((n, D // net.n_dp, width), BF) for n in split] if net.fast else [((D, width), BF)]
    return in_vmem(
        functools.partial(grad_kernel, net, near, spans),
        "weight_grad",
        [pos],
        [left, right, mid, tail],
        outs,
        [((D, width), BF)],
        2 * rows * D * width,
    )


def add_low(a, b):
    return (a.astype(F32) + b.astype(F32)).astype(BF)


def sum_kernel(paired, own_ref, across_ref, along_ref, *outs):
    for rank in range(own_ref.shape[0]):
        total = own_ref[rank].astype(F32) + (across_ref[rank].astype(F32) + along_ref[rank].astype(F32))
        if not paired:
            outs[rank][...] = total.astype(outs[rank].dtype)
        elif rank % 2:
            outs[2][rank // 2] = total.astype(BF)
        else:
            outs[rank // 2][...] = total


def sum_plane(parts, paired):
    _, rows, width = parts[0].shape
    shape = (rows, width)
    outs = [(shape, F32), (shape, F32), ((2, rows, width), BF)] if paired else [(shape, F32)] + [(shape, BF)] * 3
    return in_vmem(functools.partial(sum_kernel, paired), "sum_plane", [], parts, outs, (), 100 * rows * width)


def pair_kernel(own_ref, in_ref, out_ref):
    out_ref[...] = (own_ref[...] + in_ref[1].astype(F32)).astype(BF)


def turn_kernel(x_ref, y_ref, lo_ref, hi_ref, x_out, y_out):
    x_out[0:2] = x_ref[0:2]
    x_out[2:4] = (x_ref[2:4].astype(F32) + hi_ref[...].astype(F32)).astype(BF)
    y_out[0:2] = (y_ref[0:2].astype(F32) + lo_ref[...].astype(F32)).astype(BF)
    y_out[2:4] = y_ref[2:4]


class Scatter:
    def __init__(self, net, other):
        self.net = net
        self.other = other
        self.far_in = [net.x(other[1]), net.y(other[2])] if net.fast else []
        self.gate = ()

    def own(self, own):
        if self.net.fast:
            self.o_all, self.y_all = own
        else:
            total = own[0].astype(F32) + self.net.x(self.other[0]).astype(F32)
            self.pieces = lax.psum_scatter(total, "dp", scatter_dimension=0, tiled=True)

    def turn(self):
        self.sums, self.near_in = [], []
        if self.net.fast:
            x_all = self.other[0]
            parts = after([x_all, self.y_all] + list(self.far_in), self.gate)
            self.sums = in_vmem(turn_kernel, "turn", [], parts, [(x_all.shape, BF)] * 2, (), 2 * x_all.size)
            self.near_in = [self.net.x(self.sums[0]), self.net.y(self.sums[1])]


    def finish(self):
        if not self.net.fast:
            self.mark = ()
            return [self.pieces]
        sums = sum_plane([self.o_all] + list(self.near_in), False)
        self.mark = sums[0]
        return [sums[0]] + [self.net.z(sums[r], r) for r in range(1, self.net.n_z)]

    def pair(self):
        self.pair_in, self.mark = [], ()
        if self.net.fast:
            parts = after([self.o_all] + list(self.near_in), self.gate)
            self.kept, self.sent, out = sum_plane(parts, True)
            self.mark = self.kept
            self.pair_in = [self.net.z(out, 1)]

    def finish_pair(self):
        if not self.net.fast:
            self.last_sum = ()
            return [self.pieces]
        arrays = after([self.sent] + list(self.pair_in), self.gate)
        (out,) = in_vmem(pair_kernel, "sum_pair", [], arrays, [(self.sent.shape, BF)], (), 2 * self.sent.size)
        self.last_sum = out
        return [self.kept] + list(self.pair_in) + [self.net.z(out, 2)]


def adamw(outs, ins, place, gradient, rate, decay):
    weight, moment, second = (ref[place] for ref in ins)
    moment = BETA_ONE * moment + (1.0 - BETA_ONE) * gradient
    second = BETA_TWO * second + (1.0 - BETA_TWO) * gradient * gradient
    fix_one = 1.0 - BETA_ONE**STEP
    fix_two = 1.0 - BETA_TWO**STEP
    update = moment / fix_one / (jnp.sqrt(second / fix_two) + ADAM_EPS)
    outs[0][place] = weight - rate * (update + decay * weight)
    outs[1][place] = moment
    outs[2][place] = second


def total_of(refs, span):
    total = 0.0
    for ref in refs:
        total += (ref[0, :, span] if len(ref.shape) == 3 else ref[:, span]).astype(F32)
    return total


def put_row(out_ref, column):
    row = turned(column)
    out_ref[...] = jnp.zeros_like(out_ref)
    out_ref[0:1, 0 : row.shape[1]] = row


def total_kernel(count, *refs):
    pieces, (weight, total_ref, gain_ref) = refs[:count], refs[count:]
    width = weight.shape[2]
    total_ref[...] = total_of(pieces, slice(0, 4 * width))
    column = 0.0
    for member in range(3):
        low = weight[member].astype(BF).astype(F32)
        column += jnp.sum(low * total_ref[:, member * width : (member + 1) * width], axis=1, keepdims=True)
    put_row(gain_ref, column)


def total_attend(pieces, weight):
    _, rows, width = weight.shape
    outs = [((rows, 4 * width), F32), ((8, 128), F32)]
    return in_vmem(functools.partial(total_kernel, len(pieces)), "total_attend", [], list(pieces) + [weight], outs)


def adam_attend_kernel(count, *refs):
    total_ref, refs = refs[0], refs[1:]
    qkv, out, qkv_new, out_new = refs[0:3], refs[3:6], refs[6:9], refs[9:12]
    width = qkv[0].shape[2]
    for member in range(3):
        gradient = total_ref[:, member * width : (member + 1) * width]
        adamw(qkv_new, qkv, member, gradient, D ** (-0.5), DECAY_RATE)
    gradient = turned(total_ref[:, 3 * width : 4 * width])
    adamw(out_new, out, ..., gradient, max(1, 3 * HD // L) ** (-0.5), DECAY_RATE)


def adam_feed_kernel(count, *refs):
    groups, refs = (refs[: count // 2], refs[count // 2 : count]), refs[count:]
    gu, down, gu_new, down_new, gain_ref = refs[0:3], refs[3:6], refs[6:9], refs[9:12], refs[12]
    units = gu[0].shape[2] // 2
    column = 0.0
    for part in range(2):
        span = slice(part * units, (part + 1) * units)
        pieces = groups[part]
        for member in range(2):
            gradient = total_of(pieces, slice(member * units, (member + 1) * units))
            low = gu[0][member, :, span].astype(BF).astype(F32)
            column += jnp.sum(low * gradient, axis=1, keepdims=True)
            adamw(gu_new, gu, (member, slice(None), span), gradient, D ** (-0.5), DECAY_RATE)
        gradient = total_of(pieces, slice(2 * units, 3 * units))
        adamw(down_new, down, (slice(None), span), gradient, FF ** (-0.5), DECAY_RATE)
    put_row(gain_ref, column)


def adam_call(kernel, pieces, states, name, with_gain):
    shapes = [jax.ShapeDtypeStruct(s.shape, F32) for s in states]
    if with_gain:
        shapes.append(jax.ShapeDtypeStruct((8, 128), F32))
    return pl.pallas_call(
        functools.partial(kernel, len(pieces)),
        grid=(1,),
        in_specs=[whole(a.shape) for a in list(pieces) + list(states)],
        out_specs=[whole(s.shape) for s in shapes],
        out_shape=shapes,
        compiler_params=params(),
        cost_estimate=cost(0, 0),
        name=name,
    )(*pieces, *[hbm(a) for a in states])


def first_grad_kernel(own_ref, other_ref, wo_ref, wx_ref, f_ref, send_ref, keep_ref):
    half = own_ref.shape[0] // 2
    send_ref[0:half, :] = f_ref[half:, :]
    for tile in row_tiles(2 * half, TILE):
        total = (dot_nt(own_ref[tile, :], wo_ref[...]) + dot_nt(other_ref[tile, :], wx_ref[...])).astype(BF)
        if tile.start < half:
            keep_ref[tile, :] = total
        else:
            send_ref[tile, :] = total


def first_grad(own, other, w_own, w_other, f_part):
    rows = own.shape[0]
    return in_vmem(
        first_grad_kernel,
        "first_grad",
        [],
        [own, other, w_own, w_other, f_part],
        [((rows, D), BF), ((rows // 2, D), BF)],
        (),
        4 * rows * D * own.shape[1],
    )


def last_kernel(x_ref, a_ref, b_ref, f_ref, in_ref, d_ref, gain_ref, dx2_ref, out_ref, grad_ref):
    half = x_ref.shape[0]
    for tile in row_tiles(half, TILE):
        other = slice(half + tile.start, half + tile.stop)
        value = x_ref[tile, :].astype(F32)
        second_in = value + (a_ref[tile, :].astype(F32) + b_ref[other, :].astype(F32))
        out_ref[tile, :] = (second_in + (f_ref[tile, :].astype(F32) + in_ref[tile, :].astype(F32))).astype(BF)
        inverse = lax.rsqrt(jnp.mean(value * value, axis=1, keepdims=True) + NORM_EPS)
        normed = value * inverse
        scaled = (d_ref[tile, :].astype(F32) + in_ref[other, :].astype(F32)) * gain_ref[0:1, :]
        center = jnp.mean(scaled * normed, axis=1, keepdims=True)
        grad_ref[tile, :] = dx2_ref[tile, :] + inverse * (scaled - normed * center)


def last(x, *arrays):
    shapes = [jax.ShapeDtypeStruct(x.shape, BF), jax.ShapeDtypeStruct(x.shape, F32)]
    return pl.pallas_call(
        last_kernel,
        grid=(1,),
        in_specs=[whole(x.shape)] + [VMEM_SPEC] * len(arrays),
        out_specs=[whole(x.shape)] * 2,
        out_shape=shapes,
        compiler_params=params(),
        cost_estimate=cost(0, 0),
        name="last",
    )(x, *arrays)


def gain_step(weight, moment, second, gradient):
    moment_new = BETA_ONE * moment + (1.0 - BETA_ONE) * gradient
    second_new = BETA_TWO * second + (1.0 - BETA_TWO) * gradient * gradient
    fix_one = 1.0 - BETA_ONE**STEP
    fix_two = 1.0 - BETA_TWO**STEP
    update = moment_new / fix_one / (jnp.sqrt(second_new / fix_two) + ADAM_EPS)
    return (weight - GAIN_RATE * update, moment_new, second_new)


def body(
    net,
    inputs,
    cotangent,
    lengths,
    gains,
    w_qkv,
    m_qkv,
    v_qkv,
    w_out,
    m_out,
    v_out,
    w_gu,
    m_gu,
    v_gu,
    w_down,
    m_down,
    v_down,
    m_gain,
    v_gain,
):
    own_rows = inputs.shape[0]
    rows = 2 * own_rows
    shard = w_qkv.shape[1]
    width = w_qkv.shape[2]
    half_units = w_gu.shape[2] // 2
    dp, mp = lax.axis_index("dp"), lax.axis_index("mp")
    core = lax.rem(mp, 2)
    pos = jnp.stack([dp // 2, lax.rem(dp, 2)]).astype(jnp.int32)

    if own_rows % L == 0:
        each = own_rows // L
        seqs = 2 * each
        pair = mp + 1 - 2 * core
        own_len = lax.dynamic_slice(lengths, (mp * each,), (each,))
        other_len = lax.dynamic_slice(lengths, (pair * each,), (each,))
        meta = jnp.concatenate([own_len, other_len, jnp.zeros((seqs,), jnp.int32)])
    else:
        seqs = rows // L
        len_here = lax.dynamic_slice(lengths, ((mp // 2) * seqs,), (seqs,))
        meta = jnp.concatenate([len_here, jnp.full((seqs,), core * own_rows, jnp.int32)])

    x_in = net.core(inputs)
    back_in = net.core(cotangent)
    pack_a = pack_attend(net, w_qkv, w_out, gains)
    packs_f = pack_feed(after(w_gu, pack_a), w_down.T)
    stack_a = stacked(net, after(gather_line(net, pack_a), packs_f))
    pack_one, pack_two = after(packs_f, stack_a)
    line_one = gather_line(net, pack_one)
    plane_a = Plane(net, stack_a, True)
    gain_given = None
    if not net.fast:
        gain_all = lax.all_gather(gains.astype(BF), "dp", axis=1, tiled=True).astype(F32)
        gain_given = jnp.pad(gain_all, ((0, 6), (0, 0)))

    x_pair = jnp.concatenate([inputs, x_in], axis=0)
    back = jnp.concatenate([cotangent, back_in], axis=0)
    x_pair, back = together(x_pair, back)
    plane_a.turn()
    h1, gain_wide, qkv_own, wqkv_own, wout_own = project(net, pos, x_pair, plane_a.own(), width, gain_given, True)
    qkv_own, line_one, pack_two = together(qkv_own, line_one, pack_two)
    feed_one = Plane(net, stacked(net, line_one), True)
    two_in = [net.z(pack_two, 2)] if net.fast else []
    o_own, lse_own = attend(meta, qkv_own, width, seqs)
    o_own, plane_a.far_in, two_in = together(o_own, plane_a.far_in, two_in)
    two_last = [net.z(jnp.stack([pack_two] + two_in), 1)] if net.fast else []

    h1_late = after(h1, o_own)
    qkv_other, wqkv_other, wout_other = project(net, pos, h1_late, plane_a.other(), width)
    o_other, lse_other = attend(meta, qkv_other, width, seqs)
    o_other, feed_one.near_in, two_last = together(o_other, feed_one.near_in, two_last)
    feed_one.turn()

    o_other = after(o_other, feed_one.halves)
    branch = (dot_nt(o_own, wout_own) + dot_nt(o_other, wout_other)).astype(BF)
    branch_in = net.core(branch)
    line_two = [pack_two]
    if net.fast:
        line_two = [pack_two, two_last[0][0], two_in[0], two_last[0][1]]
    feed_two = Plane(net, stacked(net, line_two), True)
    h2 = second_norm(x_pair, branch, branch_in, gain_wide)

    pack_width = 3 * half_units
    f_spans = [(0, (0, 0), 0, 2 * half_units), (1, (0, 2 * half_units), 2 * half_units, half_units)]

    def feed_grads(mid_own, mid_other):
        g_other = grad_pack(net, pos, h2, back, mid_other, mid_other, f_spans, pack_width, True, (4, 2, 2))
        total = Scatter(net, g_other)
        g_own = grad_pack(net, pos, h2, back, mid_own, mid_own, f_spans, pack_width, True, (4, 4))
        total.own(g_own)
        return total, (g_own[0], g_other[0])

    groups = [feed_one.own(), feed_one.other()]
    mid_own, mid_other, f_part, d_part = feed(net, pos, h2, back, groups, half_units, [])
    mid_own, mid_other, f_part, d_part, feed_two.near_in = together(
        mid_own, mid_other, f_part, d_part, feed_two.near_in
    )
    feed_two.turn()
    sum_one, done_one = feed_grads(mid_own, mid_other)
    previous = after([f_part, d_part], done_one)
    groups = [feed_two.own(), feed_two.other()]
    mid_own, mid_other, f_part, d_part = feed(net, pos, h2, back, groups, half_units, previous)
    mid_own, mid_other, f_part, d_part, sum_one.far_in = together(
        mid_own, mid_other, f_part, d_part, sum_one.far_in
    )
    d_in = net.core(d_part)
    sum_one.turn()
    mid_own, mid_other = after((mid_own, mid_other), sum_one.sums)
    sum_two, done_two = feed_grads(mid_own, mid_other)
    d_in = after(d_in, done_two)

    da, do_own, do_other, dx2 = middle(
        x_pair, branch, branch_in, back, d_part, d_in, gain_wide, wout_own, wout_other
    )
    dqkv_other = attend_back(meta, qkv_other, do_other, o_other, lse_other, width, seqs)
    dqkv_other, sum_one.near_in, sum_two.far_in = together(dqkv_other, sum_one.near_in, sum_two.far_in)
    a_spans = [(0, (0, 0), 0, 3 * width), (1, (1, 0), 3 * width, width)]
    g_other = grad_pack(net, pos, h1, da, dqkv_other, o_other, a_spans, 4 * width, True, (4, 2, 2))
    sum_a = Scatter(net, g_other)
    sum_one.gate = sum_two.gate = g_other[0]
    sum_two.turn()
    sum_one.pair()
    do_own = after(do_own, (g_other, sum_one.mark, sum_two.sums))
    dqkv_own = attend_back(meta, qkv_own, do_own, o_own, lse_own, width, seqs)
    dqkv_own, sum_a.far_in, sum_one.pair_in = together(dqkv_own, sum_a.far_in, sum_one.pair_in)
    g_own = grad_pack(net, pos, h1, da, dqkv_own, o_own, a_spans, 4 * width, True, (4, 4))
    sum_a.own(g_own)
    sum_a.turn()
    sum_one.gate = sum_two.gate = sum_a.sums
    pieces_one = sum_one.finish_pair()
    sum_two.pair()
    dqkv_own, dqkv_last = after((dqkv_own, dqkv_other), sum_two.mark)
    send, dh1 = first_grad(dqkv_own, dqkv_last, wqkv_own, wqkv_other, f_part)
    send, sum_a.near_in, sum_two.pair_in, pieces_one = together(
        send, sum_a.near_in, sum_two.pair_in, pieces_one
    )
    sum_a.pair()
    sum_two.gate = sum_a.mark
    pieces_two = sum_two.finish_pair()
    last_in = net.core(after(send, sum_two.last_sum))
    sum_a.pair_in, last_in = together(sum_a.pair_in, last_in)
    pieces_a = sum_a.finish_pair()

    output, input_grad = last(
        after(inputs, sum_a.last_sum), branch, branch_in, f_part, last_in, dh1, gain_wide, dx2
    )
    states_f = [w_gu, m_gu, v_gu, w_down.T, m_down.T, v_down.T]
    feed_new = adam_call(adam_feed_kernel, after(pieces_one + pieces_two, output), states_f, "adam_feed", True)
    pieces_a = after(pieces_a, feed_new[-1])
    total_a, gain_one = total_attend(pieces_a, w_qkv)
    terms = jnp.concatenate([gain_one[0:1], feed_new[-1][0:1]], axis=0)
    states_a = [w_qkv, m_qkv, v_qkv, w_out, m_out, v_out]
    attend_new = adam_call(adam_attend_kernel, [total_a], states_a, "adam_attend", False)
    total = terms + net.core(terms) + net.x(terms) + net.cross(terms)
    gain_grad = total[:, :shard] / round_low(gains)
    new_gains, gain_moment, gain_second = gain_step(gains, m_gain, v_gain, gain_grad)
    return (
        (output, input_grad, new_gains, gain_moment, gain_second)
        + tuple(attend_new[:6])
        + tuple(feed_new[:3])
        + tuple(v.T for v in feed_new[3:6])
    )


def solution(mesh):
    net = Net(mesh.shape["dp"], mesh.shape["mp"])
    rows = P(("dp", "mp"), None)
    gain = P(None, "dp")
    wide = P(None, "dp", "mp")
    tall = P("mp", "dp")
    return jax.shard_map(
        functools.partial(body, net),
        mesh=mesh,
        in_specs=(rows, rows, P("dp"), gain) + (wide,) * 3 + (tall,) * 3 + (wide,) * 3 + (tall,) * 3 + (gain,) * 2,
        out_specs=(rows, rows) + (gain,) * 3 + (wide,) * 3 + (tall,) * 3 + (wide,) * 3 + (tall,) * 3,
        check_vma=False,
    )
```

```python
import functools
import math

import jax
import jax.numpy as jnp
from jax import lax
from jax.experimental import pallas as pl
from jax.experimental.pallas import tpu as pltpu
from jax.sharding import PartitionSpec as P

D = 768
DH = 64
FF = 2048
L = 1024
STEP = 10
HD = 768

NORM_EPS = 1e-06
MASK_FILL = -1e30
BETA_ONE = 0.5
BETA_TWO = 0.5
ADAM_EPS = 1e-08
DECAY_RATE = 0.01
GAIN_RATE = 0.5

AXES = ("dp", "mp")
BF = jnp.bfloat16
F32 = jnp.float32
SCALE = DH ** (-0.5)
SCALE2 = SCALE * math.log2(math.e)
VMEM_LIMIT = 24 * 1024 * 1024
TILE = 256
FEED_TILE = 512
COST_CUT = 1


def params(**kw):
    return pltpu.CompilerParams(vmem_limit_bytes=VMEM_LIMIT, **kw)


def cost(flops, nbytes, trans=0):
    return pl.CostEstimate(flops=int(flops) // COST_CUT, bytes_accessed=int(nbytes) // COST_CUT, transcendentals=0)


def round_low(value):
    return lax.reduce_precision(value, 8, 7)


def after(values, anchor):
    return lax.optimization_barrier((values, anchor))[0]


def dot_nn(a, b):
    return lax.dot_general(a, b, (((1,), (0,)), ((), ())), preferred_element_type=F32)


def dot_nt(a, b):
    return lax.dot_general(a, b, (((1,), (1,)), ((), ())), preferred_element_type=F32)


def dot_tn(a, b):
    return lax.dot_general(a, b, (((0,), (0,)), ((), ())), preferred_element_type=F32)


def together(*values):
    return lax.optimization_barrier(values)


def hbm(array):
    return pltpu.with_memory_space_constraint(array, pltpu.HBM)


SMEM_SPEC = pl.BlockSpec(memory_space=pltpu.SMEM)
VMEM_SPEC = pl.BlockSpec(memory_space=pltpu.VMEM)


def whole(shape):
    return pl.BlockSpec(shape, lambda *_: (0,) * len(shape))


def in_vmem(kernel, name, scalars, arrays, outs, scratch=(), flops=0, aliases=None):
    nbytes = sum(a.size * a.dtype.itemsize for a in arrays)
    return pl.pallas_call(
        kernel,
        in_specs=[SMEM_SPEC] * len(scalars) + [VMEM_SPEC] * len(arrays),
        out_specs=[VMEM_SPEC] * len(outs),
        out_shape=[pltpu.VMEM(shape, dtype) for shape, dtype in outs],
        scratch_shapes=[pltpu.VMEM(shape, dtype) for shape, dtype in scratch],
        input_output_aliases=aliases or {},
        compiler_params=params(),
        cost_estimate=cost(0, 0) if flops is None else cost(flops, nbytes),
        name=name,
    )(*scalars, *arrays)


class Net:
    def __init__(self, n_dp, n_mp):
        self.n_dp, self.n_mp = n_dp, n_mp
        self.n_y = 2
        self.n_z = n_dp // 2
        self.fast = n_dp == 8 and n_mp == 4 and (D // n_dp) % 16 == 0

    def perm(self, move):
        pairs = []
        for dp in range(self.n_dp):
            for mp in range(self.n_mp):
                z, y, x, c = dp // 2, dp % 2, mp // 2, mp % 2
                z2, y2, x2, c2 = move(z, y, x, c)
                pairs.append((dp * self.n_mp + mp, (z2 * 2 + y2) * self.n_mp + x2 * 2 + c2))
        return pairs

    def core(self, v):
        return lax.ppermute(v, AXES, self.perm(lambda z, y, x, c: (z, y, x, 1 - c)))

    def x(self, v):
        return lax.ppermute(v, AXES, self.perm(lambda z, y, x, c: (z, y, 1 - x, c)))

    def cross(self, v):
        return lax.ppermute(v, AXES, self.perm(lambda z, y, x, c: (z, y, 1 - x, 1 - c)))

    def y(self, v):
        return lax.ppermute(v, AXES, self.perm(lambda z, y, x, c: (z, 1 - y, x, c)))

    def z(self, v, r):
        return lax.ppermute(v, AXES, self.perm(lambda z, y, x, c: (z ^ r, y, x, c)))


def gather_line(net, shard):
    if not net.fast:
        return [shard]
    return [shard] + [net.z(shard, r) for r in range(1, net.n_z)]


def stacked(net, line):
    return jnp.stack(line) if net.fast else line[0]


class Plane:
    def __init__(self, net, line, near):
        self.net, self.line, self.near = net, line, near
        if net.fast:
            self.near_in = [net.y(line), net.x(line)]
        else:
            own = lax.all_gather(line, "dp", axis=0, tiled=True)[None]
            self.near_in = [own, net.x(own)]
        self.far_in, self.halves = [], ()

    def turn(self):
        if self.net.fast:
            y_all, x_all = self.near_in
            self.halves = (y_all[:2], x_all[2:])
            self.far_in = [self.net.x(self.halves[0]), self.net.y(self.halves[1])]

    def own(self):
        if not self.net.fast:
            return [(self.near_in[0], None, 0, 0)]
        return [(self.line, self.near, 0, 0), (self.near_in[0], self.near, 0, 1)]

    def other(self):
        if not self.net.fast:
            return [(self.near_in[1], None, 0, 0)]
        return [
            (self.near_in[1], self.near, 0, 0),
            (self.far_in[0], self.near, 0, 1),
            (self.far_in[1], self.near, 2, 1),
        ]


def block_row(net, pos, near, rank, flip):
    z = lax.bitwise_xor(pos[0], jnp.int32(rank)) if near else rank
    y = pos[1] if not flip else 1 - pos[1]
    return z * 2 + y


def assemble(net, target, pieces, metas, pos):
    for ref, (near, first, flip) in zip(pieces, metas):
        if near is None:
            target[...] = ref[0]
            continue
        rows = D // net.n_dp
        for index in range(ref.shape[0]):
            rank = first + index
            block = block_row(net, pos, near, rank, flip)
            start = pl.multiple_of(block * rows, 16)
            target[pl.ds(start, rows), :] = ref[index, 0:rows, :]


def ceil_to(n, m):
    return -(-n // m) * m


def turned(value):
    rows, cols = value.shape
    padded = jnp.pad(value, ((0, ceil_to(rows, 128) - rows), (0, ceil_to(cols, 128) - cols)))
    return padded.T[:cols, :rows]


def pack_attend_kernel(qkv_ref, out_ref, gain_ref, pack_ref):
    rows, width = qkv_ref.shape[1:]
    parts = [qkv_ref[member].astype(BF) for member in range(3)] + [turned(out_ref[...]).astype(BF)]
    for member, part in enumerate(parts):
        pack_ref[0:rows, member * width : (member + 1) * width] = part
    if pack_ref.shape[0] > rows:
        gains = jnp.pad(gain_ref[...], ((0, 6), (0, 4 * width - rows)))
        pack_ref[rows:, :] = gains.astype(BF)


def pack_attend(net, w_qkv, w_out, gains):
    _, rows, width = w_qkv.shape
    total = rows + 8 if net.fast else rows
    return pl.pallas_call(
        pack_attend_kernel,
        grid=(1,),
        in_specs=[whole(w_qkv.shape), whole(w_out.shape), whole(gains.shape)],
        out_specs=whole((total, 4 * width)),
        out_shape=jax.ShapeDtypeStruct((total, 4 * width), BF),
        compiler_params=params(),
        name="pack_attend",
    )(hbm(w_qkv), hbm(w_out), hbm(gains))


def pack_feed_kernel(gu_ref, down_ref, *pack_refs):
    units = gu_ref.shape[2] // 2
    for part, pack_ref in enumerate(pack_refs):
        span = slice(part * units, (part + 1) * units)
        pack_ref[:, 0:units] = gu_ref[0, :, span].astype(BF)
        pack_ref[:, units : 2 * units] = gu_ref[1, :, span].astype(BF)
        pack_ref[:, 2 * units : 3 * units] = down_ref[:, span].astype(BF)


def pack_feed(w_gu, w_down):
    _, rows, units = w_gu.shape
    shape = (rows, 3 * units // 2)
    return pl.pallas_call(
        pack_feed_kernel,
        grid=(1,),
        in_specs=[whole(w_gu.shape), whole(w_down.shape)],
        out_specs=[whole(shape)] * 2,
        out_shape=[jax.ShapeDtypeStruct(shape, BF)] * 2,
        compiler_params=params(),
        name="pack_feed",
    )(hbm(w_gu), hbm(w_down))


def spread_gains(net, gain_ref, pieces, pos):
    rows = D // net.n_dp
    for block in range(net.n_dp):
        rank = lax.bitwise_xor(pos[0], jnp.int32(block // 2))
        here = pieces[0][rank].astype(F32)[rows : rows + 8, :rows]
        there = pieces[1][rank].astype(F32)[rows : rows + 8, :rows]
        gain_ref[:, block * rows : (block + 1) * rows] = jnp.where(pos[1] == block % 2, here, there)


def row_tiles(rows, size):
    return [slice(start, start + size) for start in range(0, rows, size)]


def project_kernel(net, metas, first, pos, x_ref, *refs):
    if not net.fast and first:
        given, refs = refs[0], refs[1:]
    count = len(metas)
    pieces, refs = refs[:count], refs[count:]
    if first:
        h_ref, gain_ref, refs = refs[0], refs[1], refs[2:]
    qkv_ref, wqkv_ref, wout_ref, full = refs
    assemble(net, full, pieces, metas, pos)
    wqkv_ref[...] = full[:, : wqkv_ref.shape[1]]
    wout_ref[...] = full[:, wqkv_ref.shape[1] :]
    if first and net.fast:
        spread_gains(net, gain_ref, pieces, pos)
    elif first:
        gain_ref[...] = given[...]
    for tile in row_tiles(x_ref.shape[0], TILE):
        if first:
            value = x_ref[tile, :].astype(F32)
            inverse = lax.rsqrt(jnp.mean(value * value, axis=1, keepdims=True) + NORM_EPS)
            rows = (value * inverse * gain_ref[0:1, :]).astype(BF)
            h_ref[tile, :] = rows
        else:
            rows = x_ref[tile, :]
        qkv_ref[tile, :] = dot_nn(rows, wqkv_ref[...]).astype(BF)


def project(net, pos, x, pieces, head_width, gains=None, first=False):
    rows = x.shape[0]
    arrays = [x] + ([gains] if first and not net.fast else []) + [p[0] for p in pieces]
    metas = [p[1:] for p in pieces]
    outs = [((rows, 3 * head_width), BF), ((D, 3 * head_width), BF), ((D, head_width), BF)]
    if first:
        outs = [((rows, D), BF), ((8, D), F32)] + outs
    return in_vmem(
        functools.partial(project_kernel, net, metas, first),
        "project",
        [pos],
        arrays,
        outs,
        [((D, 4 * head_width), BF)],
        2 * rows * D * 3 * head_width,
    )


def key_valid(meta, seq, count, axis, shape, start):
    place = lax.broadcasted_iota(jnp.int32, shape, axis) + start + meta[count + seq]
    place = jnp.where(place >= L, place - L, place)
    return place < meta[seq]


def attend_kernel(heads, seqs, meta, qkv_ref, o_ref, lse_ref, key_wide, value_wide):
    width = heads * DH
    lane = lax.broadcasted_iota(jnp.int32, (TILE, 128), 1)
    column = lax.broadcasted_iota(jnp.int32, (L, DH), 1)
    one = jnp.where(column == 0, 1.0, 0.0).astype(BF)
    for seq in range(seqs):
        span = slice(seq * L, (seq + 1) * L)
        valid = key_valid(meta, seq, seqs, 0, (L, DH), 0)
        mask = jnp.where(column == 0, jnp.where(valid, 0.0, MASK_FILL), 0.0).astype(BF)
        for head in range(heads):
            keys = qkv_ref[span, width + head * DH : width + (head + 1) * DH]
            values = qkv_ref[span, 2 * width + head * DH : 2 * width + (head + 1) * DH]
            key_wide[head] = jnp.concatenate([keys, mask], axis=1)
            value_wide[head] = jnp.concatenate([values, one], axis=1)
        for tile in row_tiles(L, TILE):
            rows = slice(seq * L + tile.start, seq * L + tile.stop)
            scores = []
            for head in range(heads):
                queries = qkv_ref[rows, head * DH : (head + 1) * DH]
                queries = jnp.concatenate([queries, one[0:TILE]], axis=1)
                scores.append(dot_nt(queries, key_wide[head]))
            logs = jnp.zeros((TILE, 128), F32)
            outs = []
            for head in range(heads):
                top = jnp.max(scores[head], axis=1, keepdims=True)
                expo = jnp.exp2((scores[head] - top) * SCALE2)
                mixed = dot_nn(expo.astype(BF), value_wide[head])
                total = mixed[:, DH : DH + 1]
                outs.append(mixed[:, 0:DH] / total)
                logs = jnp.where(lane == head, top * SCALE2 + jnp.log2(total), logs)
            o_ref[rows, :] = jnp.concatenate(outs, axis=1).astype(BF)
            lse_ref[:, rows] = logs.T[0:8]


def attend(meta, qkv, head_width, seqs):
    rows = qkv.shape[0]
    heads = head_width // DH
    return in_vmem(
        functools.partial(attend_kernel, heads, seqs),
        "attend",
        [meta],
        [qkv],
        [((rows, head_width), BF), ((8, rows), F32)],
        [((heads, L, 2 * DH), BF)] * 2,
        16 * rows * L * head_width,
    )


def attend_back_kernel(heads, chosen, seqs, meta, qkv_ref, do_ref, o_ref, lse_ref, *refs):
    out_ref = refs[-1]
    width = heads * DH
    for seq in range(seqs):
        span = slice(seq * L, (seq + 1) * L)
        valid = key_valid(meta, seq, seqs, 0, (L, 1), 0)
        for head in chosen:
            cols = slice(head * DH, (head + 1) * DH)
            key_cols = slice(width + head * DH, width + (head + 1) * DH)
            value_cols = slice(2 * width + head * DH, 2 * width + (head + 1) * DH)
            product = do_ref[span, cols].astype(F32) * o_ref[span, cols].astype(F32)
            sums = jnp.broadcast_to(jnp.sum(product, axis=1, keepdims=True), (L, 128))
            inner = sums.T[0:1]
            scores = dot_nt(qkv_ref[span, key_cols], qkv_ref[span, cols]) * SCALE2 - lse_ref[head : head + 1, span]
            probs = jnp.where(valid, jnp.exp2(scores), 0.0)
            grad_probs = dot_nt(qkv_ref[span, value_cols], do_ref[span, cols])
            grad_scores = (probs * (grad_probs - inner)).astype(BF)
            grad_values = dot_nn(probs.astype(BF), do_ref[span, cols])
            grad_keys = dot_nn(grad_scores, qkv_ref[span, cols]) * SCALE
            grad_queries = dot_tn(qkv_ref[span, key_cols], grad_scores) * SCALE
            out_ref[span, key_cols] = grad_keys.astype(BF)
            out_ref[span, value_cols] = grad_values.astype(BF)
            out_ref[span, cols] = grad_queries.T.astype(BF)


def attend_back(meta, qkv, grad, mixed, lse, head_width, seqs, chosen, into=None):
    rows = qkv.shape[0]
    arrays = [qkv, grad, mixed, lse] + ([] if into is None else [into])
    return in_vmem(
        functools.partial(attend_back_kernel, head_width // DH, chosen, seqs),
        "attend_back",
        [meta],
        arrays,
        [((rows, 3 * head_width), BF)],
        (),
        14 * rows * L * DH * len(chosen),
        {} if into is None else {5: 0},
    )[0]


def feed_kernel(net, metas, units, first, pos, h_ref, dy_ref, *refs):
    pieces, refs = refs[: len(metas)], refs[len(metas) :]
    if not first:
        f_prev, d_prev, refs = refs[0], refs[1], refs[2:]
    mid_ref, f_ref, d_ref, full = refs
    assemble(net, full, pieces, metas, pos)
    root = math.sqrt(2.0 / math.pi)
    w_gate, w_up, w_down = (full[:, j * units : (j + 1) * units] for j in range(3))
    for tile in row_tiles(h_ref.shape[0], FEED_TILE):
        hidden_in, back_in = h_ref[tile, :], dy_ref[tile, :]
        gate = dot_nn(hidden_in, w_gate)
        up = dot_nn(hidden_in, w_up)
        grad_hidden = dot_nn(back_in, w_down)
        square = gate * gate
        tanh = jnp.tanh(gate * (root + (root * 0.044715) * square))
        half = 0.5 * (1.0 + tanh)
        gelu = gate * half
        slope = half + (0.5 * gate) * (1.0 - tanh * tanh) * (root + (3.0 * root * 0.044715) * square)
        hidden = (gelu * up).astype(BF)
        grad_gate = (grad_hidden * up * slope).astype(BF)
        grad_up = (grad_hidden * gelu).astype(BF)
        mid_ref[tile, 0:units] = grad_gate
        mid_ref[tile, units : 2 * units] = grad_up
        mid_ref[tile, 2 * units : 3 * units] = hidden
        f_part = dot_nt(hidden, w_down)
        d_part = dot_nt(grad_gate, w_gate) + dot_nt(grad_up, w_up)
        if not first:
            f_part += f_prev[tile, :].astype(F32)
            d_part += d_prev[tile, :].astype(F32)
        f_ref[tile, :] = f_part.astype(BF)
        d_ref[tile, :] = d_part.astype(BF)


def feed(net, pos, h2, back, pieces, units, previous):
    rows = h2.shape[0]
    arrays = [h2, back] + [p[0] for p in pieces] + list(previous)
    metas = [p[1:] for p in pieces]
    return in_vmem(
        functools.partial(feed_kernel, net, metas, units, not previous),
        "feed",
        [pos],
        arrays,
        [((rows, 3 * units), BF)] + [((rows, D), BF)] * 2,
        [((D, 3 * units), BF)],
        2 * rows * D * 6 * units,
    )


def second_kernel(x_ref, a_ref, b_ref, gain_ref, h_ref):
    tiles = row_tiles(x_ref.shape[0], TILE)
    for index, tile in enumerate(tiles):
        other = tiles[(index + len(tiles) // 2) % len(tiles)]
        value = x_ref[tile, :].astype(F32) + (a_ref[tile, :].astype(F32) + b_ref[other, :].astype(F32))
        inverse = lax.rsqrt(jnp.mean(value * value, axis=1, keepdims=True) + NORM_EPS)
        h_ref[tile, :] = (value * inverse * gain_ref[1:2, :]).astype(BF)


def second_norm(x, a_own, a_other, gain):
    return in_vmem(second_kernel, "second_norm", [], [x, a_own, a_other, gain], [(x.shape, BF)], (), 10 * x.size)[0]


def middle_kernel(x_ref, a_ref, b_ref, dy_ref, d_ref, e_ref, gain_ref, wo_ref, wx_ref,
                  da_ref, do_ref, dx_ref, dx2_ref):
    gain = gain_ref[1:2, :]
    tiles = row_tiles(x_ref.shape[0], TILE)
    for index, tile in enumerate(tiles):
        other = tiles[(index + len(tiles) // 2) % len(tiles)]
        second_in = x_ref[tile, :].astype(F32) + (a_ref[tile, :].astype(F32) + b_ref[other, :].astype(F32))
        inverse = lax.rsqrt(jnp.mean(second_in * second_in, axis=1, keepdims=True) + NORM_EPS)
        normed = second_in * inverse
        grad = d_ref[tile, :].astype(F32) + e_ref[other, :].astype(F32)
        scaled = grad * gain
        center = jnp.mean(scaled * normed, axis=1, keepdims=True)
        total = dy_ref[tile, :].astype(F32) + inverse * (scaled - normed * center)
        low = total.astype(BF)
        da_ref[tile, :] = low
        do_ref[tile, :] = dot_nn(low, wo_ref[...]).astype(BF)
        dx_ref[tile, :] = dot_nn(low, wx_ref[...]).astype(BF)
        if index < len(tiles) // 2:
            dx2_ref[tile, :] = total


def middle(x, a_own, a_other, back, d_own, d_other, gain, w_own, w_other):
    rows = x.shape[0]
    width = w_own.shape[1]
    return in_vmem(
        middle_kernel,
        "middle",
        [],
        [x, a_own, a_other, back, d_own, d_other, gain, w_own, w_other],
        [((rows, D), BF), ((rows, width), BF), ((rows, width), BF), ((rows // 2, D), F32)],
        (),
        4 * rows * D * width,
    )


def grad_kernel(net, spans, pos, left_ref, right_ref, mid_ref, tail_ref, full_ref, *outs):
    for source, other, target, size in spans:
        left = (left_ref, right_ref)[source]
        values = (mid_ref, tail_ref)[other[0]][:, other[1] : other[1] + size]
        full_ref[:, target : target + size] = dot_tn(left[...], values).astype(BF)
    for part, out in enumerate(outs):
        for index in range(2):
            out[index] = full_ref[block_rows(net, pos, 2 * part + index, 1), :]


def block_rows(net, pos, rank, flip):
    rows = D // net.n_dp
    return pl.ds(pl.multiple_of(block_row(net, pos, True, rank, flip) * rows, 16), rows)


def grad_pack(net, pos, left, right, mid, tail, spans, width, far):
    rows = left.shape[0]
    outs = [((D, width), BF)]
    if far and net.fast:
        outs += [((2, D // net.n_dp, width), BF)] * 2
    return in_vmem(
        functools.partial(grad_kernel, net, spans),
        "weight_grad",
        [pos],
        [left, right, mid, tail],
        outs,
        (),
        2 * rows * D * width,
    )


def sum_kernel(net, paired, pos, own_ref, across_ref, along_ref, *outs):
    for rank in range(net.n_z):
        own = own_ref[block_rows(net, pos, rank, 0), :].astype(F32)
        total = own + (across_ref[rank].astype(F32) + along_ref[rank].astype(F32))
        if not paired:
            outs[rank][...] = total.astype(outs[rank].dtype)
        elif rank % 2:
            outs[2][rank // 2] = total.astype(BF)
        else:
            outs[rank // 2][...] = total


def sum_plane(net, pos, own, near_in, paired):
    _, rows, width = near_in[0].shape
    shape = (rows, width)
    outs = [(shape, F32), (shape, F32), ((2, rows, width), BF)] if paired else [(shape, F32)] + [(shape, BF)] * 3
    kernel = functools.partial(sum_kernel, net, paired)
    return in_vmem(kernel, "sum_plane", [pos], [own] + list(near_in), outs, (), 100 * rows * width)


def pair_kernel(own_ref, in_ref, out_ref):
    out_ref[...] = (own_ref[...] + in_ref[1].astype(F32)).astype(BF)


def turn_kernel(net, pos, x_ref, y_ref, lo_ref, hi_ref, x_out, y_out):
    for rank in range(net.n_z):
        x_part = x_ref[block_rows(net, pos, rank, 0), :]
        y_part = y_ref[block_rows(net, pos, rank, 1), :]
        if rank < 2:
            y_part = (y_part.astype(F32) + lo_ref[rank].astype(F32)).astype(BF)
        else:
            x_part = (x_part.astype(F32) + hi_ref[rank - 2].astype(F32)).astype(BF)
        x_out[rank] = x_part
        y_out[rank] = y_part


class Scatter:
    def __init__(self, net, pos, other):
        self.net, self.pos = net, pos
        self.other = other
        self.far_in = [net.x(other[1]), net.y(other[2])] if net.fast else []
        self.gate = ()

    def own(self, own):
        self.own_full = own[0]
        if not self.net.fast:
            total = own[0].astype(F32) + self.net.x(self.other[0]).astype(F32)
            self.pieces = lax.psum_scatter(total, "dp", scatter_dimension=0, tiled=True)

    def turn(self):
        self.sums, self.near_in = [], []
        if self.net.fast:
            parts = after([self.other[0], self.own_full] + list(self.far_in), self.gate)
            shape = (self.net.n_z, D // self.net.n_dp, self.own_full.shape[1])
            kernel = functools.partial(turn_kernel, self.net)
            self.sums = in_vmem(kernel, "turn", [self.pos], parts, [(shape, BF)] * 2, (), 2 * self.own_full.size)
            self.near_in = [self.net.x(self.sums[0]), self.net.y(self.sums[1])]

    def marks(self):
        return self.sums

    def finish(self):
        if not self.net.fast:
            self.mark = ()
            return [self.pieces]
        sums = sum_plane(self.net, self.pos, self.own_full, self.near_in, False)
        self.mark = sums[0]
        return [sums[0]] + [self.net.z(sums[r], r) for r in range(1, self.net.n_z)]

    def pair(self):
        self.pair_in, self.mark = [], ()
        if self.net.fast:
            own, near_in = after((self.own_full, self.near_in), self.gate)
            self.kept, self.sent, out = sum_plane(self.net, self.pos, own, near_in, True)
            self.mark = self.kept
            self.pair_in = [self.net.z(out, 1)]

    def finish_pair(self):
        if not self.net.fast:
            self.last_sum = ()
            return [self.pieces]
        arrays = after([self.sent] + list(self.pair_in), self.gate)
        (out,) = in_vmem(pair_kernel, "sum_pair", [], arrays, [(self.sent.shape, BF)], (), None)
        self.last_sum = out
        return [self.kept] + list(self.pair_in) + [self.net.z(out, 2)]


def adamw(outs, ins, place, gradient, rate, decay):
    weight, moment, second = (ref[place] for ref in ins)
    moment = BETA_ONE * moment + (1.0 - BETA_ONE) * gradient
    second = BETA_TWO * second + (1.0 - BETA_TWO) * gradient * gradient
    fix_one = 1.0 - BETA_ONE**STEP
    fix_two = 1.0 - BETA_TWO**STEP
    update = moment / fix_one / (jnp.sqrt(second / fix_two) + ADAM_EPS)
    outs[0][place] = weight - rate * (update + decay * weight)
    outs[1][place] = moment
    outs[2][place] = second


def total_of(refs, span):
    total = 0.0
    for ref in refs:
        total += (ref[0, :, span] if len(ref.shape) == 3 else ref[:, span]).astype(F32)
    return total


def put_row(out_ref, column):
    row = turned(column)
    out_ref[...] = jnp.zeros_like(out_ref)
    out_ref[0:1, 0 : row.shape[1]] = row


def total_kernel(count, *refs):
    pieces, (weight, total_ref, gain_ref) = refs[:count], refs[count:]
    width = weight.shape[2]
    total_ref[...] = total_of(pieces, slice(0, 4 * width))
    column = 0.0
    for member in range(3):
        low = weight[member].astype(BF).astype(F32)
        column += jnp.sum(low * total_ref[:, member * width : (member + 1) * width], axis=1, keepdims=True)
    put_row(gain_ref, column)


def total_attend(pieces, weight):
    _, rows, width = weight.shape
    outs = [((rows, 4 * width), F32), ((8, 128), F32)]
    return in_vmem(functools.partial(total_kernel, len(pieces)), "total_attend", [], list(pieces) + [weight], outs)


def adam_attend_kernel(count, *refs):
    total_ref, refs = refs[0], refs[1:]
    qkv, out, qkv_new, out_new = refs[0:3], refs[3:6], refs[6:9], refs[9:12]
    width = qkv[0].shape[2]
    for member in range(3):
        gradient = total_ref[:, member * width : (member + 1) * width]
        adamw(qkv_new, qkv, member, gradient, D ** (-0.5), DECAY_RATE)
    gradient = turned(total_ref[:, 3 * width : 4 * width])
    adamw(out_new, out, ..., gradient, max(1, 3 * HD // L) ** (-0.5), DECAY_RATE)


def adam_feed_kernel(count, *refs):
    groups, refs = (refs[: count // 2], refs[count // 2 : count]), refs[count:]
    gu, down, gu_new, down_new, gain_ref = refs[0:3], refs[3:6], refs[6:9], refs[9:12], refs[12]
    units = gu[0].shape[2] // 2
    column = 0.0
    for part in range(2):
        span = slice(part * units, (part + 1) * units)
        pieces = groups[part]
        for member in range(2):
            gradient = total_of(pieces, slice(member * units, (member + 1) * units))
            low = gu[0][member, :, span].astype(BF).astype(F32)
            column += jnp.sum(low * gradient, axis=1, keepdims=True)
            adamw(gu_new, gu, (member, slice(None), span), gradient, D ** (-0.5), DECAY_RATE)
        gradient = total_of(pieces, slice(2 * units, 3 * units))
        adamw(down_new, down, (slice(None), span), gradient, FF ** (-0.5), DECAY_RATE)
    put_row(gain_ref, column)


def adam_call(kernel, pieces, states, name, with_gain):
    shapes = [jax.ShapeDtypeStruct(s.shape, F32) for s in states]
    if with_gain:
        shapes.append(jax.ShapeDtypeStruct((8, 128), F32))
    return pl.pallas_call(
        functools.partial(kernel, len(pieces)),
        grid=(1,),
        in_specs=[whole(a.shape) for a in list(pieces) + list(states)],
        out_specs=[whole(s.shape) for s in shapes],
        out_shape=shapes,
        compiler_params=params(),
        cost_estimate=cost(0, 0),
        name=name,
    )(*pieces, *[hbm(a) for a in states])


def first_grad_kernel(own_ref, other_ref, wo_ref, wx_ref, f_ref, send_ref, keep_ref):
    half = own_ref.shape[0] // 2
    send_ref[0:half, :] = f_ref[half:, :]
    for tile in row_tiles(2 * half, TILE):
        total = (dot_nt(own_ref[tile, :], wo_ref[...]) + dot_nt(other_ref[tile, :], wx_ref[...])).astype(BF)
        if tile.start < half:
            keep_ref[tile, :] = total
        else:
            send_ref[tile, :] = total


def first_grad(own, other, w_own, w_other, f_part):
    rows = own.shape[0]
    return in_vmem(
        first_grad_kernel,
        "first_grad",
        [],
        [own, other, w_own, w_other, f_part],
        [((rows, D), BF), ((rows // 2, D), BF)],
        (),
        4 * rows * D * own.shape[1],
    )


def last_kernel(x_ref, a_ref, b_ref, f_ref, in_ref, d_ref, gain_ref, dx2_ref, out_ref, grad_ref):
    half = x_ref.shape[0]
    for tile in row_tiles(half, TILE):
        other = slice(half + tile.start, half + tile.stop)
        value = x_ref[tile, :].astype(F32)
        second_in = value + (a_ref[tile, :].astype(F32) + b_ref[other, :].astype(F32))
        out_ref[tile, :] = (second_in + (f_ref[tile, :].astype(F32) + in_ref[tile, :].astype(F32))).astype(BF)
        inverse = lax.rsqrt(jnp.mean(value * value, axis=1, keepdims=True) + NORM_EPS)
        normed = value * inverse
        scaled = (d_ref[tile, :].astype(F32) + in_ref[other, :].astype(F32)) * gain_ref[0:1, :]
        center = jnp.mean(scaled * normed, axis=1, keepdims=True)
        grad_ref[tile, :] = dx2_ref[tile, :] + inverse * (scaled - normed * center)


def last(x, *arrays):
    shapes = [jax.ShapeDtypeStruct(x.shape, BF), jax.ShapeDtypeStruct(x.shape, F32)]
    return pl.pallas_call(
        last_kernel,
        grid=(1,),
        in_specs=[whole(x.shape)] + [VMEM_SPEC] * len(arrays),
        out_specs=[whole(x.shape)] * 2,
        out_shape=shapes,
        compiler_params=params(),
        cost_estimate=cost(0, 0),
        name="last",
    )(x, *arrays)


def gain_step(weight, moment, second, gradient):
    moment_new = BETA_ONE * moment + (1.0 - BETA_ONE) * gradient
    second_new = BETA_TWO * second + (1.0 - BETA_TWO) * gradient * gradient
    fix_one = 1.0 - BETA_ONE**STEP
    fix_two = 1.0 - BETA_TWO**STEP
    update = moment_new / fix_one / (jnp.sqrt(second_new / fix_two) + ADAM_EPS)
    return (weight - GAIN_RATE * update, moment_new, second_new)


def body(
    net,
    inputs,
    cotangent,
    lengths,
    gains,
    w_qkv,
    m_qkv,
    v_qkv,
    w_out,
    m_out,
    v_out,
    w_gu,
    m_gu,
    v_gu,
    w_down,
    m_down,
    v_down,
    m_gain,
    v_gain,
):
    own_rows = inputs.shape[0]
    rows = 2 * own_rows
    shard = w_qkv.shape[1]
    width = w_qkv.shape[2]
    half_units = w_gu.shape[2] // 2
    dp, mp = lax.axis_index("dp"), lax.axis_index("mp")
    core = lax.rem(mp, 2)
    pos = jnp.stack([dp // 2, lax.rem(dp, 2)]).astype(jnp.int32)

    if own_rows % L == 0:
        each = own_rows // L
        seqs = 2 * each
        pair = mp + 1 - 2 * core
        own_len = lax.dynamic_slice(lengths, (mp * each,), (each,))
        other_len = lax.dynamic_slice(lengths, (pair * each,), (each,))
        meta = jnp.concatenate([own_len, other_len, jnp.zeros((seqs,), jnp.int32)])
    else:
        seqs = rows // L
        len_here = lax.dynamic_slice(lengths, ((mp // 2) * seqs,), (seqs,))
        meta = jnp.concatenate([len_here, jnp.full((seqs,), core * own_rows, jnp.int32)])

    x_in = net.core(inputs)
    back_in = net.core(cotangent)
    pack_a = pack_attend(net, w_qkv, w_out, gains)
    packs_f = pack_feed(after(w_gu, pack_a), w_down.T)
    stack_a = stacked(net, after(gather_line(net, pack_a), packs_f))
    pack_one, pack_two = after(packs_f, stack_a)
    line_one = gather_line(net, pack_one)
    plane_a = Plane(net, stack_a, True)
    gain_given = None
    if not net.fast:
        gain_all = lax.all_gather(gains.astype(BF), "dp", axis=1, tiled=True).astype(F32)
        gain_given = jnp.pad(gain_all, ((0, 6), (0, 0)))

    x_pair = jnp.concatenate([inputs, x_in], axis=0)
    back = jnp.concatenate([cotangent, back_in], axis=0)
    x_pair, back = together(x_pair, back)
    h1, gain_wide, qkv_own, wqkv_own, wout_own = project(net, pos, x_pair, plane_a.own(), width, gain_given, True)
    plane_a.near_in = after(plane_a.near_in, qkv_own)
    plane_a.turn()
    qkv_own, line_one, pack_two = together(qkv_own, line_one, pack_two)
    feed_one = Plane(net, stacked(net, line_one), True)
    two_in = [net.z(pack_two, 2)] if net.fast else []
    o_own, lse_own = attend(meta, qkv_own, width, seqs)
    o_own, plane_a.far_in, two_in = together(o_own, plane_a.far_in, two_in)
    two_last = [net.z(jnp.stack([pack_two] + two_in), 1)] if net.fast else []

    h1_late = after(h1, o_own)
    qkv_other, wqkv_other, wout_other = project(net, pos, h1_late, plane_a.other(), width)
    o_other, lse_other = attend(meta, qkv_other, width, seqs)
    o_other, feed_one.near_in, two_last = together(o_other, feed_one.near_in, two_last)
    feed_one.turn()

    o_other = after(o_other, feed_one.halves)
    branch = (dot_nt(o_own, wout_own) + dot_nt(o_other, wout_other)).astype(BF)
    branch_in = net.core(branch)
    line_two = [pack_two]
    if net.fast:
        line_two = [pack_two, two_last[0][0], two_in[0], two_last[0][1]]
    feed_two = Plane(net, stacked(net, line_two), True)
    h2 = second_norm(x_pair, branch, branch_in, gain_wide)

    pack_width = 3 * half_units
    f_spans = [(0, (0, 0), 0, 2 * half_units), (1, (0, 2 * half_units), 2 * half_units, half_units)]

    def feed_grads(mid, far):
        return grad_pack(net, pos, h2, back, mid, mid, f_spans, pack_width, far)

    mid_own, f_part, d_part = feed(net, pos, h2, back, feed_one.own(), half_units, [])
    mid_other, f_part, d_part = feed(net, pos, h2, back, feed_one.other(), half_units, [f_part, d_part])
    one_other = feed_grads(mid_other, True)
    one_own = feed_grads(mid_own, False)
    f_part, d_part, feed_two.near_in = together(f_part, d_part, after(feed_two.near_in, (one_own, one_other)))
    feed_two.turn()
    mid_own, f_part, d_part = feed(net, pos, h2, back, feed_two.own(), half_units, [f_part, d_part])
    sum_one = Scatter(net, pos, after(one_other, d_part))
    sum_one.own(one_own)
    mid_other, f_part, d_part = feed(net, pos, h2, back, feed_two.other(), half_units, [f_part, d_part])
    mid_other, f_part, d_part, sum_one.far_in = together(mid_other, f_part, d_part, sum_one.far_in)
    d_in = net.core(d_part)
    g_other = feed_grads(after(mid_other, d_part), True)
    sum_two = Scatter(net, pos, g_other)
    g_own = feed_grads(after(mid_own, g_other), False)
    sum_two.own(g_own)
    sum_one.gate = g_own
    sum_one.turn()
    d_in = after(d_in, sum_one.marks())

    da, do_own, do_other, dx2 = middle(
        x_pair, branch, branch_in, back, d_part, d_in, gain_wide, wout_own, wout_other
    )
    heads = width // DH
    early, late = tuple(range(1)), tuple(range(1, heads))
    dqkv_other = attend_back(meta, qkv_other, do_other, o_other, lse_other, width, seqs, early)
    dqkv_other, sum_two.far_in = together(dqkv_other, sum_two.far_in)
    sum_two.gate = dqkv_other
    sum_two.turn()
    dqkv_other = after(dqkv_other, sum_two.marks())
    dqkv_other = attend_back(meta, qkv_other, do_other, o_other, lse_other, width, seqs, late, dqkv_other)
    a_spans = [(0, (0, 0), 0, 3 * width), (1, (1, 0), 3 * width, width)]
    g_other = grad_pack(net, pos, h1, da, dqkv_other, o_other, a_spans, 4 * width, True)
    sum_a = Scatter(net, pos, g_other)
    sum_one.gate = g_other[0]
    sum_one.pair()
    do_own = after(do_own, (g_other, sum_one.mark, sum_two.sums))
    dqkv_own = attend_back(meta, qkv_own, do_own, o_own, lse_own, width, seqs, early)
    sum_two.gate = dqkv_own
    sum_two.pair()
    dqkv_own = after(dqkv_own, sum_two.mark)
    dqkv_own = attend_back(meta, qkv_own, do_own, o_own, lse_own, width, seqs, late, dqkv_own)
    dqkv_own, sum_a.far_in, sum_one.pair_in, sum_two.pair_in = together(
        dqkv_own, sum_a.far_in, sum_one.pair_in, sum_two.pair_in
    )
    g_own = grad_pack(net, pos, h1, da, dqkv_own, o_own, a_spans, 4 * width, False)
    sum_a.own(g_own)
    sum_a.turn()
    sum_one.gate = sum_two.gate = sum_a.sums
    pieces_one = sum_one.finish_pair()
    pieces_two = sum_two.finish_pair()
    dqkv_own, dqkv_last = after((dqkv_own, dqkv_other), (sum_one.last_sum, sum_two.last_sum))
    send, dh1 = first_grad(dqkv_own, dqkv_last, wqkv_own, wqkv_other, f_part)
    send, sum_a.near_in, pieces_two, pieces_one = together(send, sum_a.near_in, pieces_two, pieces_one)
    pieces_a = sum_a.finish()
    last_in = net.core(after(send, sum_a.mark))

    output, input_grad = last(inputs, branch, branch_in, f_part, last_in, dh1, gain_wide, dx2)
    states_f = [w_gu, m_gu, v_gu, w_down.T, m_down.T, v_down.T]
    feed_new = adam_call(adam_feed_kernel, after(pieces_one + pieces_two, output), states_f, "adam_feed", True)
    pieces_a = after(pieces_a, feed_new[-1])
    total_a, gain_one = total_attend(pieces_a, w_qkv)
    terms = jnp.concatenate([gain_one[0:1], feed_new[-1][0:1]], axis=0)
    states_a = [w_qkv, m_qkv, v_qkv, w_out, m_out, v_out]
    attend_new = adam_call(adam_attend_kernel, [total_a], states_a, "adam_attend", False)
    total = terms + net.core(terms) + net.x(terms) + net.cross(terms)
    gain_grad = total[:, :shard] / round_low(gains)
    new_gains, gain_moment, gain_second = gain_step(gains, m_gain, v_gain, gain_grad)
    return (
        (output, input_grad, new_gains, gain_moment, gain_second)
        + tuple(attend_new[:6])
        + tuple(feed_new[:3])
        + tuple(v.T for v in feed_new[3:6])
    )


def solution(mesh):
    net = Net(mesh.shape["dp"], mesh.shape["mp"])
    rows = P(("dp", "mp"), None)
    gain = P(None, "dp")
    wide = P(None, "dp", "mp")
    tall = P("mp", "dp")
    return jax.shard_map(
        functools.partial(body, net),
        mesh=mesh,
        in_specs=(rows, rows, P("dp"), gain) + (wide,) * 3 + (tall,) * 3 + (wide,) * 3 + (tall,) * 3 + (gain,) * 2,
        out_specs=(rows, rows) + (gain,) * 3 + (wide,) * 3 + (tall,) * 3 + (wide,) * 3 + (tall,) * 3,
        check_vma=False,
    )
```

```python
import functools
import math

import jax
import jax.numpy as jnp
from jax import lax
from jax.experimental import pallas as pl
from jax.experimental.pallas import tpu as pltpu
from jax.sharding import PartitionSpec as P

D = 768
DH = 64
FF = 2048
L = 1024
STEP = 10
HD = 768

NORM_EPS = 1e-06
MASK_FILL = -1e30
BETA_ONE = 0.5
BETA_TWO = 0.5
ADAM_EPS = 1e-08
DECAY_RATE = 0.01
GAIN_RATE = 0.5

AXES = ("dp", "mp")
BF = jnp.bfloat16
F32 = jnp.float32
SCALE = DH ** (-0.5)
SCALE2 = SCALE * math.log2(math.e)
VMEM_LIMIT = 12 * 1024 * 1024
TILE = 256
FEED_TILE = 512
COST_CUT = 1


def params(**kw):
    return pltpu.CompilerParams(vmem_limit_bytes=VMEM_LIMIT, **kw)


def cost(flops, nbytes, trans=0):
    return pl.CostEstimate(flops=int(flops) // COST_CUT, bytes_accessed=int(nbytes) // COST_CUT, transcendentals=0)


def round_low(value):
    return lax.reduce_precision(value, 8, 7)


def after(values, anchor):
    return lax.optimization_barrier((values, anchor))[0]


def dot_nn(a, b):
    return lax.dot_general(a, b, (((1,), (0,)), ((), ())), preferred_element_type=F32)


def dot_nt(a, b):
    return lax.dot_general(a, b, (((1,), (1,)), ((), ())), preferred_element_type=F32)


def dot_tn(a, b):
    return lax.dot_general(a, b, (((0,), (0,)), ((), ())), preferred_element_type=F32)


def together(*values):
    return lax.optimization_barrier(values)


def hbm(array):
    return pltpu.with_memory_space_constraint(array, pltpu.HBM)


SMEM_SPEC = pl.BlockSpec(memory_space=pltpu.SMEM)
VMEM_SPEC = pl.BlockSpec(memory_space=pltpu.VMEM)


def whole(shape):
    return pl.BlockSpec(shape, lambda *_: (0,) * len(shape))


def in_vmem(kernel, name, scalars, arrays, outs, scratch=(), flops=0, aliases=None):
    nbytes = sum(a.size * a.dtype.itemsize for a in arrays)
    return pl.pallas_call(
        kernel,
        in_specs=[SMEM_SPEC] * len(scalars) + [VMEM_SPEC] * len(arrays),
        out_specs=[VMEM_SPEC] * len(outs),
        out_shape=[pltpu.VMEM(shape, dtype) for shape, dtype in outs],
        scratch_shapes=[pltpu.VMEM(shape, dtype) for shape, dtype in scratch],
        input_output_aliases=aliases or {},
        compiler_params=params(),
        cost_estimate=cost(0, 0) if flops is None else cost(flops, nbytes),
        name=name,
    )(*scalars, *arrays)


class Net:
    def __init__(self, n_dp, n_mp):
        self.n_dp, self.n_mp = n_dp, n_mp
        self.n_y = 2
        self.n_z = n_dp // 2
        self.fast = n_dp == 8 and n_mp == 4 and (D // n_dp) % 16 == 0

    def perm(self, move):
        pairs = []
        for dp in range(self.n_dp):
            for mp in range(self.n_mp):
                z, y, x, c = dp // 2, dp % 2, mp // 2, mp % 2
                z2, y2, x2, c2 = move(z, y, x, c)
                pairs.append((dp * self.n_mp + mp, (z2 * 2 + y2) * self.n_mp + x2 * 2 + c2))
        return pairs

    def core(self, v):
        return lax.ppermute(v, AXES, self.perm(lambda z, y, x, c: (z, y, x, 1 - c)))

    def x(self, v):
        return lax.ppermute(v, AXES, self.perm(lambda z, y, x, c: (z, y, 1 - x, c)))

    def cross(self, v):
        return lax.ppermute(v, AXES, self.perm(lambda z, y, x, c: (z, y, 1 - x, 1 - c)))

    def y(self, v):
        return lax.ppermute(v, AXES, self.perm(lambda z, y, x, c: (z, 1 - y, x, c)))

    def z(self, v, r):
        return lax.ppermute(v, AXES, self.perm(lambda z, y, x, c: (z ^ r, y, x, c)))


def gather_line(net, shard):
    if not net.fast:
        return [shard]
    return [shard] + [net.z(shard, r) for r in range(1, net.n_z)]


def stacked(net, line):
    return jnp.stack(line) if net.fast else line[0]


class Plane:
    def __init__(self, net, line, near):
        self.net, self.line, self.near = net, line, near
        if net.fast:
            self.near_in = [net.y(line), net.x(line)]
        else:
            own = lax.all_gather(line, "dp", axis=0, tiled=True)[None]
            self.near_in = [own, net.x(own)]
        self.far_in, self.halves = [], ()

    def turn(self):
        if self.net.fast:
            y_all, x_all = self.near_in
            self.halves = (y_all[:2], x_all[2:])
            self.far_in = [self.net.x(self.halves[0]), self.net.y(self.halves[1])]

    def own(self):
        if not self.net.fast:
            return [(self.near_in[0], None, 0, 0)]
        return [(self.line, self.near, 0, 0), (self.near_in[0], self.near, 0, 1)]

    def other(self):
        if not self.net.fast:
            return [(self.near_in[1], None, 0, 0)]
        return [
            (self.near_in[1], self.near, 0, 0),
            (self.far_in[0], self.near, 0, 1),
            (self.far_in[1], self.near, 2, 1),
        ]


def block_row(net, pos, near, rank, flip):
    z = lax.bitwise_xor(pos[0], jnp.int32(rank)) if near else rank
    y = pos[1] if not flip else 1 - pos[1]
    return z * 2 + y


def assemble(net, target, pieces, metas, pos):
    for ref, (near, first, flip) in zip(pieces, metas):
        if near is None:
            target[...] = ref[0]
            continue
        rows = D // net.n_dp
        for index in range(ref.shape[0]):
            rank = first + index
            block = block_row(net, pos, near, rank, flip)
            start = pl.multiple_of(block * rows, 16)
            target[pl.ds(start, rows), :] = ref[index, 0:rows, :]


def ceil_to(n, m):
    return -(-n // m) * m


def turned(value):
    rows, cols = value.shape
    padded = jnp.pad(value, ((0, ceil_to(rows, 128) - rows), (0, ceil_to(cols, 128) - cols)))
    return padded.T[:cols, :rows]


def pack_attend_kernel(qkv_ref, out_ref, gain_ref, pack_ref):
    rows, width = qkv_ref.shape[1:]
    parts = [qkv_ref[member].astype(BF) for member in range(3)] + [turned(out_ref[...]).astype(BF)]
    for member, part in enumerate(parts):
        pack_ref[0:rows, member * width : (member + 1) * width] = part
    if pack_ref.shape[0] > rows:
        gains = jnp.pad(gain_ref[...], ((0, 6), (0, 4 * width - rows)))
        pack_ref[rows:, :] = gains.astype(BF)


def pack_attend(net, w_qkv, w_out, gains):
    _, rows, width = w_qkv.shape
    total = rows + 8 if net.fast else rows
    return pl.pallas_call(
        pack_attend_kernel,
        grid=(1,),
        in_specs=[whole(w_qkv.shape), whole(w_out.shape), whole(gains.shape)],
        out_specs=whole((total, 4 * width)),
        out_shape=jax.ShapeDtypeStruct((total, 4 * width), BF),
        compiler_params=params(),
        name="pack_attend",
    )(hbm(w_qkv), hbm(w_out), hbm(gains))


def pack_feed_kernel(gu_ref, down_ref, *pack_refs):
    units = gu_ref.shape[2] // 2
    for part, pack_ref in enumerate(pack_refs):
        span = slice(part * units, (part + 1) * units)
        pack_ref[:, 0:units] = gu_ref[0, :, span].astype(BF)
        pack_ref[:, units : 2 * units] = gu_ref[1, :, span].astype(BF)
        pack_ref[:, 2 * units : 3 * units] = down_ref[:, span].astype(BF)


def pack_feed(w_gu, w_down):
    _, rows, units = w_gu.shape
    shape = (rows, 3 * units // 2)
    return pl.pallas_call(
        pack_feed_kernel,
        grid=(1,),
        in_specs=[whole(w_gu.shape), whole(w_down.shape)],
        out_specs=[whole(shape)] * 2,
        out_shape=[jax.ShapeDtypeStruct(shape, BF)] * 2,
        compiler_params=params(),
        name="pack_feed",
    )(hbm(w_gu), hbm(w_down))


def spread_gains(net, gain_ref, pieces, pos):
    rows = D // net.n_dp
    for block in range(net.n_dp):
        rank = lax.bitwise_xor(pos[0], jnp.int32(block // 2))
        here = pieces[0][rank].astype(F32)[rows : rows + 8, :rows]
        there = pieces[1][rank].astype(F32)[rows : rows + 8, :rows]
        gain_ref[:, block * rows : (block + 1) * rows] = jnp.where(pos[1] == block % 2, here, there)


def row_tiles(rows, size):
    return [slice(start, start + size) for start in range(0, rows, size)]


def project_kernel(net, metas, first, pos, x_ref, *refs):
    if not net.fast and first:
        given, refs = refs[0], refs[1:]
    count = len(metas)
    pieces, refs = refs[:count], refs[count:]
    if first:
        h_ref, gain_ref, refs = refs[0], refs[1], refs[2:]
    qkv_ref, wqkv_ref, wout_ref, full = refs
    assemble(net, full, pieces, metas, pos)
    wqkv_ref[...] = full[:, : wqkv_ref.shape[1]]
    wout_ref[...] = full[:, wqkv_ref.shape[1] :]
    if first and net.fast:
        spread_gains(net, gain_ref, pieces, pos)
    elif first:
        gain_ref[...] = given[...]
    for tile in row_tiles(x_ref.shape[0], TILE):
        if first:
            value = x_ref[tile, :].astype(F32)
            inverse = lax.rsqrt(jnp.mean(value * value, axis=1, keepdims=True) + NORM_EPS)
            rows = (value * inverse * gain_ref[0:1, :]).astype(BF)
            h_ref[tile, :] = rows
        else:
            rows = x_ref[tile, :]
        qkv_ref[tile, :] = dot_nn(rows, wqkv_ref[...]).astype(BF)


def project(net, pos, x, pieces, head_width, gains=None, first=False):
    rows = x.shape[0]
    arrays = [x] + ([gains] if first and not net.fast else []) + [p[0] for p in pieces]
    metas = [p[1:] for p in pieces]
    outs = [((rows, 3 * head_width), BF), ((D, 3 * head_width), BF), ((D, head_width), BF)]
    if first:
        outs = [((rows, D), BF), ((8, D), F32)] + outs
    return in_vmem(
        functools.partial(project_kernel, net, metas, first),
        "project",
        [pos],
        arrays,
        outs,
        [((D, 4 * head_width), BF)],
        2 * rows * D * 3 * head_width,
    )


def key_valid(meta, seq, count, axis, shape, start):
    place = lax.broadcasted_iota(jnp.int32, shape, axis) + start + meta[count + seq]
    place = jnp.where(place >= L, place - L, place)
    return place < meta[seq]


def attend_kernel(heads, seqs, meta, qkv_ref, o_ref, inverse_ref, expo_ref, key_wide, value_wide):
    width = heads * DH
    lane = lax.broadcasted_iota(jnp.int32, (TILE, 128), 1)
    column = lax.broadcasted_iota(jnp.int32, (L, DH), 1)
    one = jnp.where(column == 0, 1.0, 0.0).astype(BF)
    for seq in range(seqs):
        span = slice(seq * L, (seq + 1) * L)
        valid = key_valid(meta, seq, seqs, 0, (L, DH), 0)
        mask = jnp.where(column == 0, jnp.where(valid, 0.0, MASK_FILL), 0.0).astype(BF)
        for head in range(heads):
            keys = qkv_ref[span, width + head * DH : width + (head + 1) * DH]
            values = qkv_ref[span, 2 * width + head * DH : 2 * width + (head + 1) * DH]
            key_wide[head] = jnp.concatenate([keys, mask], axis=1)
            value_wide[head] = jnp.concatenate([values, one], axis=1)
        for tile in row_tiles(L, TILE):
            rows = slice(seq * L + tile.start, seq * L + tile.stop)
            scores = []
            for head in range(heads):
                queries = qkv_ref[rows, head * DH : (head + 1) * DH]
                queries = jnp.concatenate([queries, one[0:TILE]], axis=1)
                scores.append(dot_nt(queries, key_wide[head]))
            inverses = jnp.zeros((TILE, 128), F32)
            outs = []
            for head in range(heads):
                top = jnp.max(scores[head], axis=1, keepdims=True)
                expo = jnp.exp2((scores[head] - top) * SCALE2).astype(BF)
                expo_ref[head, rows, :] = expo
                mixed = dot_nn(expo, value_wide[head])
                inverse = 1.0 / mixed[:, DH : DH + 1]
                outs.append(mixed[:, 0:DH] * inverse)
                inverses = jnp.where(lane == head, inverse, inverses)
            o_ref[rows, :] = jnp.concatenate(outs, axis=1).astype(BF)
            inverse_ref[rows, :] = inverses


def attend(meta, qkv, head_width, seqs):
    rows = qkv.shape[0]
    heads = head_width // DH
    return in_vmem(
        functools.partial(attend_kernel, heads, seqs),
        "attend",
        [meta],
        [qkv],
        [((rows, head_width), BF), ((rows, 128), F32), ((heads, rows, L), BF)],
        [((heads, L, 2 * DH), BF)] * 2,
        16 * rows * L * head_width,
    )


def attend_back_kernel(heads, chosen, seqs, qkv_ref, do_ref, o_ref, inverse_ref, expo_ref, *refs):
    out_ref = refs[-1]
    width = heads * DH
    for seq in range(seqs):
        span = slice(seq * L, (seq + 1) * L)
        for head in chosen:
            cols = slice(head * DH, (head + 1) * DH)
            key_cols = slice(width + head * DH, width + (head + 1) * DH)
            value_cols = slice(2 * width + head * DH, 2 * width + (head + 1) * DH)
            inverse = inverse_ref[span, head : head + 1]
            grads = do_ref[span, cols].astype(F32) * inverse
            inner = jnp.sum(grads * o_ref[span, cols].astype(F32), axis=1, keepdims=True)
            grads = grads.astype(BF)
            expo = expo_ref[head, span, :]
            grad_probs = dot_nt(grads, qkv_ref[span, value_cols])
            grad_scores = (expo.astype(F32) * (grad_probs - inner)).astype(BF)
            grad_values = dot_tn(grads, expo)
            grad_keys = dot_tn(qkv_ref[span, cols], grad_scores) * SCALE
            grad_queries = dot_nn(grad_scores, qkv_ref[span, key_cols]) * SCALE
            out_ref[span, key_cols] = grad_keys.T.astype(BF)
            out_ref[span, value_cols] = grad_values.T.astype(BF)
            out_ref[span, cols] = grad_queries.astype(BF)


def attend_back(qkv, grad, mixed, saved, head_width, seqs, chosen, into=None, light=False):
    rows = qkv.shape[0]
    arrays = [qkv, grad, mixed] + list(saved) + ([] if into is None else [into])
    return in_vmem(
        functools.partial(attend_back_kernel, head_width // DH, chosen, seqs),
        "attend_back",
        [],
        arrays,
        [((rows, 3 * head_width), BF)],
        (),
        None if light else 10 * rows * L * DH * len(chosen),
        {} if into is None else {5: 0},
    )[0]


def feed_kernel(net, metas, units, first, pos, h_ref, dy_ref, *refs):
    pieces, refs = refs[: len(metas)], refs[len(metas) :]
    if not first:
        f_prev, d_prev, refs = refs[0], refs[1], refs[2:]
    mid_ref, f_ref, d_ref, full = refs
    assemble(net, full, pieces, metas, pos)
    root = math.sqrt(2.0 / math.pi)
    w_gate, w_up, w_down = (full[:, j * units : (j + 1) * units] for j in range(3))
    for tile in row_tiles(h_ref.shape[0], FEED_TILE):
        hidden_in, back_in = h_ref[tile, :], dy_ref[tile, :]
        gate = dot_nn(hidden_in, w_gate)
        up = dot_nn(hidden_in, w_up)
        grad_hidden = dot_nn(back_in, w_down)
        square = gate * gate
        tanh = jnp.tanh(gate * (root + (root * 0.044715) * square))
        half = 0.5 * (1.0 + tanh)
        gelu = gate * half
        slope = half + (0.5 * gate) * (1.0 - tanh * tanh) * (root + (3.0 * root * 0.044715) * square)
        hidden = (gelu * up).astype(BF)
        grad_gate = (grad_hidden * up * slope).astype(BF)
        grad_up = (grad_hidden * gelu).astype(BF)
        mid_ref[tile, 0:units] = grad_gate
        mid_ref[tile, units : 2 * units] = grad_up
        mid_ref[tile, 2 * units : 3 * units] = hidden
        f_part = dot_nt(hidden, w_down)
        d_part = dot_nt(grad_gate, w_gate) + dot_nt(grad_up, w_up)
        if not first:
            f_part += f_prev[tile, :].astype(F32)
            d_part += d_prev[tile, :].astype(F32)
        f_ref[tile, :] = f_part.astype(BF)
        d_ref[tile, :] = d_part.astype(BF)


def feed(net, pos, h2, back, pieces, units, previous):
    rows = h2.shape[0]
    arrays = [h2, back] + [p[0] for p in pieces] + list(previous)
    metas = [p[1:] for p in pieces]
    return in_vmem(
        functools.partial(feed_kernel, net, metas, units, not previous),
        "feed",
        [pos],
        arrays,
        [((rows, 3 * units), BF)] + [((rows, D), BF)] * 2,
        [((D, 3 * units), BF)],
        2 * rows * D * 6 * units,
    )


def second_kernel(x_ref, a_ref, b_ref, gain_ref, h_ref):
    tiles = row_tiles(x_ref.shape[0], TILE)
    for index, tile in enumerate(tiles):
        other = tiles[(index + len(tiles) // 2) % len(tiles)]
        value = x_ref[tile, :].astype(F32) + (a_ref[tile, :].astype(F32) + b_ref[other, :].astype(F32))
        inverse = lax.rsqrt(jnp.mean(value * value, axis=1, keepdims=True) + NORM_EPS)
        h_ref[tile, :] = (value * inverse * gain_ref[1:2, :]).astype(BF)


def second_norm(x, a_own, a_other, gain):
    return in_vmem(second_kernel, "second_norm", [], [x, a_own, a_other, gain], [(x.shape, BF)], (), 10 * x.size)[0]


def middle_kernel(x_ref, a_ref, b_ref, dy_ref, d_ref, e_ref, gain_ref, wo_ref, wx_ref,
                  da_ref, do_ref, dx_ref, dx2_ref):
    gain = gain_ref[1:2, :]
    tiles = row_tiles(x_ref.shape[0], TILE)
    for index, tile in enumerate(tiles):
        other = tiles[(index + len(tiles) // 2) % len(tiles)]
        second_in = x_ref[tile, :].astype(F32) + (a_ref[tile, :].astype(F32) + b_ref[other, :].astype(F32))
        inverse = lax.rsqrt(jnp.mean(second_in * second_in, axis=1, keepdims=True) + NORM_EPS)
        normed = second_in * inverse
        grad = d_ref[tile, :].astype(F32) + e_ref[other, :].astype(F32)
        scaled = grad * gain
        center = jnp.mean(scaled * normed, axis=1, keepdims=True)
        total = dy_ref[tile, :].astype(F32) + inverse * (scaled - normed * center)
        low = total.astype(BF)
        da_ref[tile, :] = low
        do_ref[tile, :] = dot_nn(low, wo_ref[...]).astype(BF)
        dx_ref[tile, :] = dot_nn(low, wx_ref[...]).astype(BF)
        if index < len(tiles) // 2:
            dx2_ref[tile, :] = total


def middle(x, a_own, a_other, back, d_own, d_other, gain, w_own, w_other):
    rows = x.shape[0]
    width = w_own.shape[1]
    return in_vmem(
        middle_kernel,
        "middle",
        [],
        [x, a_own, a_other, back, d_own, d_other, gain, w_own, w_other],
        [((rows, D), BF), ((rows, width), BF), ((rows, width), BF), ((rows // 2, D), F32)],
        (),
        4 * rows * D * width,
    )


def grad_kernel(net, spans, pos, left_ref, right_ref, mid_ref, tail_ref, full_ref, *outs):
    for source, other, target, size in spans:
        left = (left_ref, right_ref)[source]
        values = (mid_ref, tail_ref)[other[0]][:, other[1] : other[1] + size]
        full_ref[:, target : target + size] = dot_tn(left[...], values).astype(BF)
    for part, out in enumerate(outs):
        for index in range(2):
            out[index] = full_ref[block_rows(net, pos, 2 * part + index, 1), :]


def block_rows(net, pos, rank, flip):
    rows = D // net.n_dp
    return pl.ds(pl.multiple_of(block_row(net, pos, True, rank, flip) * rows, 16), rows)


def grad_pack(net, pos, left, right, mid, tail, spans, width, far):
    rows = left.shape[0]
    outs = [((D, width), BF)]
    if far and net.fast:
        outs += [((2, D // net.n_dp, width), BF)] * 2
    return in_vmem(
        functools.partial(grad_kernel, net, spans),
        "weight_grad",
        [pos],
        [left, right, mid, tail],
        outs,
        (),
        2 * rows * D * width,
    )


def sum_kernel(net, paired, pos, own_ref, across_ref, along_ref, *outs):
    for rank in range(net.n_z):
        own = own_ref[block_rows(net, pos, rank, 0), :].astype(F32)
        total = own + (across_ref[rank].astype(F32) + along_ref[rank].astype(F32))
        if not paired:
            outs[rank][...] = total.astype(outs[rank].dtype)
        elif rank % 2:
            outs[2][rank // 2] = total.astype(BF)
        else:
            outs[rank // 2][...] = total


def sum_plane(net, pos, own, near_in, paired):
    _, rows, width = near_in[0].shape
    shape = (rows, width)
    outs = [(shape, F32), (shape, F32), ((2, rows, width), BF)] if paired else [(shape, F32)] + [(shape, BF)] * 3
    kernel = functools.partial(sum_kernel, net, paired)
    return in_vmem(kernel, "sum_plane", [pos], [own] + list(near_in), outs, (), 100 * rows * width)


def pair_kernel(own_ref, in_ref, out_ref):
    out_ref[...] = (own_ref[...] + in_ref[1].astype(F32)).astype(BF)


def turn_kernel(net, pos, x_ref, y_ref, lo_ref, hi_ref, x_out, y_out):
    for rank in range(net.n_z):
        x_part = x_ref[block_rows(net, pos, rank, 0), :]
        y_part = y_ref[block_rows(net, pos, rank, 1), :]
        if rank < 2:
            y_part = (y_part.astype(F32) + lo_ref[rank].astype(F32)).astype(BF)
        else:
            x_part = (x_part.astype(F32) + hi_ref[rank - 2].astype(F32)).astype(BF)
        x_out[rank] = x_part
        y_out[rank] = y_part


class Scatter:
    def __init__(self, net, pos, other):
        self.net, self.pos = net, pos
        self.other = other
        self.far_in = [net.x(other[1]), net.y(other[2])] if net.fast else []
        self.gate = ()

    def own(self, own):
        self.own_full = own[0]
        if not self.net.fast:
            total = own[0].astype(F32) + self.net.x(self.other[0]).astype(F32)
            self.pieces = lax.psum_scatter(total, "dp", scatter_dimension=0, tiled=True)

    def turn(self):
        self.sums, self.near_in = [], []
        if self.net.fast:
            parts = after([self.other[0], self.own_full] + list(self.far_in), self.gate)
            shape = (self.net.n_z, D // self.net.n_dp, self.own_full.shape[1])
            kernel = functools.partial(turn_kernel, self.net)
            self.sums = in_vmem(kernel, "turn", [self.pos], parts, [(shape, BF)] * 2, (), 2 * self.own_full.size)
            self.near_in = [self.net.x(self.sums[0]), self.net.y(self.sums[1])]

    def marks(self):
        return self.sums

    def finish(self):
        if not self.net.fast:
            self.mark = ()
            return [self.pieces]
        sums = sum_plane(self.net, self.pos, self.own_full, self.near_in, False)
        self.mark = sums[0]
        return [sums[0]] + [self.net.z(sums[r], r) for r in range(1, self.net.n_z)]

    def pair(self):
        self.pair_in, self.mark = [], ()
        if self.net.fast:
            own, near_in = after((self.own_full, self.near_in), self.gate)
            self.kept, self.sent, out = sum_plane(self.net, self.pos, own, near_in, True)
            self.mark = self.kept
            self.pair_in = [self.net.z(out, 1)]

    def finish_pair(self):
        if not self.net.fast:
            self.last_sum = ()
            return [self.pieces]
        arrays = after([self.sent] + list(self.pair_in), self.gate)
        (out,) = in_vmem(pair_kernel, "sum_pair", [], arrays, [(self.sent.shape, BF)], (), None)
        self.last_sum = out
        return [self.kept] + list(self.pair_in) + [self.net.z(out, 2)]


def adamw(outs, ins, place, gradient, rate, decay):
    weight, moment, second = (ref[place] for ref in ins)
    moment = BETA_ONE * moment + (1.0 - BETA_ONE) * gradient
    second = BETA_TWO * second + (1.0 - BETA_TWO) * gradient * gradient
    fix_one = 1.0 - BETA_ONE**STEP
    fix_two = 1.0 - BETA_TWO**STEP
    update = moment / fix_one / (jnp.sqrt(second / fix_two) + ADAM_EPS)
    outs[0][place] = weight - rate * (update + decay * weight)
    outs[1][place] = moment
    outs[2][place] = second


def total_of(refs, span):
    total = 0.0
    for ref in refs:
        total += (ref[0, :, span] if len(ref.shape) == 3 else ref[:, span]).astype(F32)
    return total


def put_row(out_ref, column):
    row = turned(column)
    out_ref[...] = jnp.zeros_like(out_ref)
    out_ref[0:1, 0 : row.shape[1]] = row


def total_kernel(count, *refs):
    pieces, (weight, total_ref, gain_ref) = refs[:count], refs[count:]
    width = weight.shape[2]
    total_ref[...] = total_of(pieces, slice(0, 4 * width))
    column = 0.0
    for member in range(3):
        low = weight[member].astype(BF).astype(F32)
        column += jnp.sum(low * total_ref[:, member * width : (member + 1) * width], axis=1, keepdims=True)
    put_row(gain_ref, column)


def total_attend(pieces, weight):
    _, rows, width = weight.shape
    outs = [((rows, 4 * width), F32), ((8, 128), F32)]
    return in_vmem(functools.partial(total_kernel, len(pieces)), "total_attend", [], list(pieces) + [weight], outs)


def adam_attend_kernel(count, *refs):
    total_ref, refs = refs[0], refs[1:]
    qkv, out, qkv_new, out_new = refs[0:3], refs[3:6], refs[6:9], refs[9:12]
    width = qkv[0].shape[2]
    for member in range(3):
        gradient = total_ref[:, member * width : (member + 1) * width]
        adamw(qkv_new, qkv, member, gradient, D ** (-0.5), DECAY_RATE)
    gradient = turned(total_ref[:, 3 * width : 4 * width])
    adamw(out_new, out, ..., gradient, max(1, 3 * HD // L) ** (-0.5), DECAY_RATE)


def adam_feed_kernel(count, *refs):
    groups, refs = (refs[: count // 2], refs[count // 2 : count]), refs[count:]
    gu, down, gu_new, down_new, gain_ref = refs[0:3], refs[3:6], refs[6:9], refs[9:12], refs[12]
    units = gu[0].shape[2] // 2
    column = 0.0
    for part in range(2):
        span = slice(part * units, (part + 1) * units)
        pieces = groups[part]
        for member in range(2):
            gradient = total_of(pieces, slice(member * units, (member + 1) * units))
            low = gu[0][member, :, span].astype(BF).astype(F32)
            column += jnp.sum(low * gradient, axis=1, keepdims=True)
            adamw(gu_new, gu, (member, slice(None), span), gradient, D ** (-0.5), DECAY_RATE)
        gradient = total_of(pieces, slice(2 * units, 3 * units))
        adamw(down_new, down, (slice(None), span), gradient, FF ** (-0.5), DECAY_RATE)
    put_row(gain_ref, column)


def adam_call(kernel, pieces, states, name, with_gain):
    shapes = [jax.ShapeDtypeStruct(s.shape, F32) for s in states]
    if with_gain:
        shapes.append(jax.ShapeDtypeStruct((8, 128), F32))
    return pl.pallas_call(
        functools.partial(kernel, len(pieces)),
        grid=(1,),
        in_specs=[whole(a.shape) for a in list(pieces) + list(states)],
        out_specs=[whole(s.shape) for s in shapes],
        out_shape=shapes,
        compiler_params=params(),
        cost_estimate=cost(0, 0),
        name=name,
    )(*pieces, *[hbm(a) for a in states])


def first_grad_kernel(own_ref, other_ref, wo_ref, wx_ref, f_ref, send_ref, keep_ref):
    half = own_ref.shape[0] // 2
    send_ref[0:half, :] = f_ref[half:, :]
    for tile in row_tiles(2 * half, TILE):
        total = (dot_nt(own_ref[tile, :], wo_ref[...]) + dot_nt(other_ref[tile, :], wx_ref[...])).astype(BF)
        if tile.start < half:
            keep_ref[tile, :] = total
        else:
            send_ref[tile, :] = total


def first_grad(own, other, w_own, w_other, f_part):
    rows = own.shape[0]
    return in_vmem(
        first_grad_kernel,
        "first_grad",
        [],
        [own, other, w_own, w_other, f_part],
        [((rows, D), BF), ((rows // 2, D), BF)],
        (),
        4 * rows * D * own.shape[1],
    )


def last_kernel(x_ref, a_ref, b_ref, f_ref, in_ref, d_ref, gain_ref, dx2_ref, out_ref, grad_ref):
    half = x_ref.shape[0]
    for tile in row_tiles(half, TILE):
        other = slice(half + tile.start, half + tile.stop)
        value = x_ref[tile, :].astype(F32)
        second_in = value + (a_ref[tile, :].astype(F32) + b_ref[other, :].astype(F32))
        out_ref[tile, :] = (second_in + (f_ref[tile, :].astype(F32) + in_ref[tile, :].astype(F32))).astype(BF)
        inverse = lax.rsqrt(jnp.mean(value * value, axis=1, keepdims=True) + NORM_EPS)
        normed = value * inverse
        scaled = (d_ref[tile, :].astype(F32) + in_ref[other, :].astype(F32)) * gain_ref[0:1, :]
        center = jnp.mean(scaled * normed, axis=1, keepdims=True)
        grad_ref[tile, :] = dx2_ref[tile, :] + inverse * (scaled - normed * center)


def last(x, *arrays):
    shapes = [jax.ShapeDtypeStruct(x.shape, BF), jax.ShapeDtypeStruct(x.shape, F32)]
    return pl.pallas_call(
        last_kernel,
        grid=(1,),
        in_specs=[whole(x.shape)] + [VMEM_SPEC] * len(arrays),
        out_specs=[whole(x.shape)] * 2,
        out_shape=shapes,
        compiler_params=params(),
        cost_estimate=cost(0, 0),
        name="last",
    )(x, *arrays)


def gain_step(weight, moment, second, gradient):
    moment_new = BETA_ONE * moment + (1.0 - BETA_ONE) * gradient
    second_new = BETA_TWO * second + (1.0 - BETA_TWO) * gradient * gradient
    fix_one = 1.0 - BETA_ONE**STEP
    fix_two = 1.0 - BETA_TWO**STEP
    update = moment_new / fix_one / (jnp.sqrt(second_new / fix_two) + ADAM_EPS)
    return (weight - GAIN_RATE * update, moment_new, second_new)


def body(
    net,
    inputs,
    cotangent,
    lengths,
    gains,
    w_qkv,
    m_qkv,
    v_qkv,
    w_out,
    m_out,
    v_out,
    w_gu,
    m_gu,
    v_gu,
    w_down,
    m_down,
    v_down,
    m_gain,
    v_gain,
):
    own_rows = inputs.shape[0]
    rows = 2 * own_rows
    shard = w_qkv.shape[1]
    width = w_qkv.shape[2]
    half_units = w_gu.shape[2] // 2
    dp, mp = lax.axis_index("dp"), lax.axis_index("mp")
    core = lax.rem(mp, 2)
    pos = jnp.stack([dp // 2, lax.rem(dp, 2)]).astype(jnp.int32)

    if own_rows % L == 0:
        each = own_rows // L
        seqs = 2 * each
        pair = mp + 1 - 2 * core
        own_len = lax.dynamic_slice(lengths, (mp * each,), (each,))
        other_len = lax.dynamic_slice(lengths, (pair * each,), (each,))
        meta = jnp.concatenate([own_len, other_len, jnp.zeros((seqs,), jnp.int32)])
    else:
        seqs = rows // L
        len_here = lax.dynamic_slice(lengths, ((mp // 2) * seqs,), (seqs,))
        meta = jnp.concatenate([len_here, jnp.full((seqs,), core * own_rows, jnp.int32)])

    x_in = net.core(inputs)
    back_in = net.core(cotangent)
    pack_a = pack_attend(net, w_qkv, w_out, gains)
    packs_f = pack_feed(after(w_gu, pack_a), w_down.T)
    stack_a = stacked(net, after(gather_line(net, pack_a), packs_f))
    pack_one, pack_two = after(packs_f, stack_a)
    line_one = gather_line(net, pack_one)
    plane_a = Plane(net, stack_a, True)
    gain_given = None
    if not net.fast:
        gain_all = lax.all_gather(gains.astype(BF), "dp", axis=1, tiled=True).astype(F32)
        gain_given = jnp.pad(gain_all, ((0, 6), (0, 0)))

    x_pair = jnp.concatenate([inputs, x_in], axis=0)
    back = jnp.concatenate([cotangent, back_in], axis=0)
    x_pair, back = together(x_pair, back)
    h1, gain_wide, qkv_own, wqkv_own, wout_own = project(net, pos, x_pair, plane_a.own(), width, gain_given, True)
    plane_a.near_in = after(plane_a.near_in, qkv_own)
    plane_a.turn()
    qkv_own, line_one, pack_two = together(qkv_own, line_one, pack_two)
    feed_one = Plane(net, stacked(net, line_one), True)
    two_in = [net.z(pack_two, 2)] if net.fast else []
    o_own, *saved_own = attend(meta, qkv_own, width, seqs)
    o_own, plane_a.far_in, two_in = together(o_own, plane_a.far_in, two_in)
    two_last = [net.z(jnp.stack([pack_two] + two_in), 1)] if net.fast else []

    h1_late = after(h1, o_own)
    qkv_other, wqkv_other, wout_other = project(net, pos, h1_late, plane_a.other(), width)
    o_other, *saved_other = attend(meta, qkv_other, width, seqs)
    o_other, feed_one.near_in, two_last = together(o_other, feed_one.near_in, two_last)
    feed_one.turn()

    o_other = after(o_other, feed_one.halves)
    branch = (dot_nt(o_own, wout_own) + dot_nt(o_other, wout_other)).astype(BF)
    branch_in = net.core(branch)
    line_two = [pack_two]
    if net.fast:
        line_two = [pack_two, two_last[0][0], two_in[0], two_last[0][1]]
    feed_two = Plane(net, stacked(net, line_two), True)
    h2 = second_norm(x_pair, branch, branch_in, gain_wide)

    pack_width = 3 * half_units
    f_spans = [(0, (0, 0), 0, 2 * half_units), (1, (0, 2 * half_units), 2 * half_units, half_units)]

    def feed_grads(mid, far):
        return grad_pack(net, pos, h2, back, mid, mid, f_spans, pack_width, far)

    mid_own, f_part, d_part = feed(net, pos, h2, back, feed_one.own(), half_units, [])
    mid_other, f_part, d_part = feed(net, pos, h2, back, feed_one.other(), half_units, [f_part, d_part])
    one_other = feed_grads(mid_other, True)
    one_own = feed_grads(mid_own, False)
    f_part, d_part, feed_two.near_in = together(f_part, d_part, after(feed_two.near_in, (one_own, one_other)))
    feed_two.turn()
    mid_own, f_part, d_part = feed(net, pos, h2, back, feed_two.own(), half_units, [f_part, d_part])
    sum_one = Scatter(net, pos, after(one_other, d_part))
    sum_one.own(one_own)
    mid_other, f_part, d_part = feed(net, pos, h2, back, feed_two.other(), half_units, [f_part, d_part])
    mid_other, f_part, d_part, sum_one.far_in = together(mid_other, f_part, d_part, sum_one.far_in)
    d_in = net.core(d_part)
    g_other = feed_grads(after(mid_other, d_part), True)
    sum_two = Scatter(net, pos, g_other)
    g_own = feed_grads(after(mid_own, g_other), False)
    sum_two.own(g_own)
    sum_one.gate = g_own
    sum_one.turn()
    d_in = after(d_in, sum_one.marks())

    da, do_own, do_other, dx2 = middle(
        x_pair, branch, branch_in, back, d_part, d_in, gain_wide, wout_own, wout_other
    )
    da, do_own, do_other, dx2, sum_two.far_in = together(da, do_own, do_other, dx2, sum_two.far_in)
    heads = tuple(range(width // DH))
    dqkv_other = attend_back(qkv_other, do_other, o_other, saved_other, width, seqs, heads)
    a_spans = [(0, (0, 0), 0, 3 * width), (1, (1, 0), 3 * width, width)]
    g_other = grad_pack(net, pos, h1, da, dqkv_other, o_other, a_spans, 4 * width, True)
    sum_a = Scatter(net, pos, g_other)
    sum_one.gate = g_other[0]
    sum_one.pair()
    sum_two.gate = sum_one.mark
    sum_two.turn()
    do_own = after(do_own, (g_other, sum_one.mark, sum_two.marks()))
    dqkv_own = attend_back(qkv_own, do_own, o_own, saved_own, width, seqs, heads[:2], light=True)
    dqkv_own, sum_a.far_in = together(dqkv_own, sum_a.far_in)
    dqkv_own = attend_back(qkv_own, do_own, o_own, saved_own, width, seqs, heads[2:], dqkv_own)
    dqkv_own, sum_one.pair_in = together(dqkv_own, sum_one.pair_in)
    g_own = grad_pack(net, pos, h1, da, dqkv_own, o_own, a_spans, 4 * width, False)
    sum_a.own(g_own)
    sum_a.turn()
    sum_one.gate = sum_two.gate = sum_a.sums
    pieces_one = sum_one.finish_pair()
    sum_two.pair()
    dqkv_own, dqkv_last = after((dqkv_own, dqkv_other), (sum_one.last_sum, sum_two.mark))
    send, dh1 = first_grad(dqkv_own, dqkv_last, wqkv_own, wqkv_other, f_part)
    send, sum_two.pair_in, pieces_one = together(send, sum_two.pair_in, pieces_one)
    sum_two.gate = send
    pieces_two = sum_two.finish_pair()
    sum_a.near_in = after(sum_a.near_in, sum_two.last_sum)
    pieces_a = sum_a.finish()
    last_in = net.core(after(send, sum_a.mark))

    output, input_grad = last(inputs, branch, branch_in, f_part, last_in, dh1, gain_wide, dx2)
    states_f = [w_gu, m_gu, v_gu, w_down.T, m_down.T, v_down.T]
    feed_new = adam_call(adam_feed_kernel, after(pieces_one + pieces_two, output), states_f, "adam_feed", True)
    pieces_a = after(pieces_a, feed_new[-1])
    total_a, gain_one = total_attend(pieces_a, w_qkv)
    terms = jnp.concatenate([gain_one[0:1], feed_new[-1][0:1]], axis=0)
    states_a = [w_qkv, m_qkv, v_qkv, w_out, m_out, v_out]
    attend_new = adam_call(adam_attend_kernel, [total_a], states_a, "adam_attend", False)
    total = terms + net.core(terms) + net.x(terms) + net.cross(terms)
    gain_grad = total[:, :shard] / round_low(gains)
    new_gains, gain_moment, gain_second = gain_step(gains, m_gain, v_gain, gain_grad)
    return (
        (output, input_grad, new_gains, gain_moment, gain_second)
        + tuple(attend_new[:6])
        + tuple(feed_new[:3])
        + tuple(v.T for v in feed_new[3:6])
    )


def solution(mesh):
    net = Net(mesh.shape["dp"], mesh.shape["mp"])
    rows = P(("dp", "mp"), None)
    gain = P(None, "dp")
    wide = P(None, "dp", "mp")
    tall = P("mp", "dp")
    return jax.shard_map(
        functools.partial(body, net),
        mesh=mesh,
        in_specs=(rows, rows, P("dp"), gain) + (wide,) * 3 + (tall,) * 3 + (wide,) * 3 + (tall,) * 3 + (gain,) * 2,
        out_specs=(rows, rows) + (gain,) * 3 + (wide,) * 3 + (tall,) * 3 + (wide,) * 3 + (tall,) * 3,
        check_vma=False,
    )
```

```python
import functools
import math

import jax
import jax.numpy as jnp
from jax import lax
from jax.experimental import pallas as pl
from jax.experimental.pallas import tpu as pltpu
from jax.sharding import PartitionSpec as P

D = 768
DH = 64
FF = 2048
L = 1024
STEP = 10
HD = 768

NORM_EPS = 1e-06
MASK_FILL = -1e30
BETA_ONE = 0.5
BETA_TWO = 0.5
ADAM_EPS = 1e-08
DECAY_RATE = 0.01
GAIN_RATE = 0.5

AXES = ("dp", "mp")
BF = jnp.bfloat16
F32 = jnp.float32
SCALE = DH ** (-0.5)
SCALE2 = SCALE * math.log2(math.e)
VMEM_LIMIT = 12 * 1024 * 1024
TILE = 256
FEED_TILE = 512
COST_CUT = 1


def params(**kw):
    return pltpu.CompilerParams(vmem_limit_bytes=VMEM_LIMIT, **kw)


def cost(flops, nbytes, trans=0):
    return pl.CostEstimate(flops=int(flops) // COST_CUT, bytes_accessed=int(nbytes) // COST_CUT, transcendentals=0)


def round_low(value):
    return lax.reduce_precision(value, 8, 7)


def after(values, anchor):
    return lax.optimization_barrier((values, anchor))[0]


def dot_nn(a, b):
    return lax.dot_general(a, b, (((1,), (0,)), ((), ())), preferred_element_type=F32)


def dot_nt(a, b):
    return lax.dot_general(a, b, (((1,), (1,)), ((), ())), preferred_element_type=F32)


def dot_tn(a, b):
    return lax.dot_general(a, b, (((0,), (0,)), ((), ())), preferred_element_type=F32)


def together(*values):
    return lax.optimization_barrier(values)


def hbm(array):
    return pltpu.with_memory_space_constraint(array, pltpu.HBM)


SMEM_SPEC = pl.BlockSpec(memory_space=pltpu.SMEM)
VMEM_SPEC = pl.BlockSpec(memory_space=pltpu.VMEM)


def whole(shape):
    return pl.BlockSpec(shape, lambda *_: (0,) * len(shape))


def in_vmem(kernel, name, scalars, arrays, outs, scratch=(), flops=0, aliases=None):
    nbytes = sum(a.size * a.dtype.itemsize for a in arrays)
    return pl.pallas_call(
        kernel,
        in_specs=[SMEM_SPEC] * len(scalars) + [VMEM_SPEC] * len(arrays),
        out_specs=[VMEM_SPEC] * len(outs),
        out_shape=[pltpu.VMEM(shape, dtype) for shape, dtype in outs],
        scratch_shapes=[pltpu.VMEM(shape, dtype) for shape, dtype in scratch],
        input_output_aliases=aliases or {},
        compiler_params=params(),
        cost_estimate=cost(0, 0) if flops is None else cost(flops, nbytes),
        name=name,
    )(*scalars, *arrays)


class Net:
    def __init__(self, n_dp, n_mp):
        self.n_dp, self.n_mp = n_dp, n_mp
        self.n_y = 2
        self.n_z = n_dp // 2
        self.fast = n_dp == 8 and n_mp == 4 and (D // n_dp) % 16 == 0

    def perm(self, move):
        pairs = []
        for dp in range(self.n_dp):
            for mp in range(self.n_mp):
                z, y, x, c = dp // 2, dp % 2, mp // 2, mp % 2
                z2, y2, x2, c2 = move(z, y, x, c)
                pairs.append((dp * self.n_mp + mp, (z2 * 2 + y2) * self.n_mp + x2 * 2 + c2))
        return pairs

    def core(self, v):
        return lax.ppermute(v, AXES, self.perm(lambda z, y, x, c: (z, y, x, 1 - c)))

    def x(self, v):
        return lax.ppermute(v, AXES, self.perm(lambda z, y, x, c: (z, y, 1 - x, c)))

    def cross(self, v):
        return lax.ppermute(v, AXES, self.perm(lambda z, y, x, c: (z, y, 1 - x, 1 - c)))

    def y(self, v):
        return lax.ppermute(v, AXES, self.perm(lambda z, y, x, c: (z, 1 - y, x, c)))

    def z(self, v, r):
        return lax.ppermute(v, AXES, self.perm(lambda z, y, x, c: (z ^ r, y, x, c)))


def gather_line(net, shard):
    if not net.fast:
        return [shard]
    return [shard] + [net.z(shard, r) for r in range(1, net.n_z)]


def stacked(net, line):
    return jnp.stack(line) if net.fast else line[0]


class Plane:
    def __init__(self, net, line, near):
        self.net, self.line, self.near = net, line, near
        if net.fast:
            self.near_in = [net.y(line), net.x(line)]
        else:
            own = lax.all_gather(line, "dp", axis=0, tiled=True)[None]
            self.near_in = [own, net.x(own)]
        self.far_in, self.halves = [], ()

    def turn(self):
        if self.net.fast:
            y_all, x_all = self.near_in
            self.halves = (y_all[:2], x_all[2:])
            self.far_in = [self.net.x(self.halves[0]), self.net.y(self.halves[1])]

    def own(self):
        if not self.net.fast:
            return [(self.near_in[0], None, 0, 0)]
        return [(self.line, self.near, 0, 0), (self.near_in[0], self.near, 0, 1)]

    def other(self):
        if not self.net.fast:
            return [(self.near_in[1], None, 0, 0)]
        return [
            (self.near_in[1], self.near, 0, 0),
            (self.far_in[0], self.near, 0, 1),
            (self.far_in[1], self.near, 2, 1),
        ]


def block_row(net, pos, near, rank, flip):
    z = lax.bitwise_xor(pos[0], jnp.int32(rank)) if near else rank
    y = pos[1] if not flip else 1 - pos[1]
    return z * 2 + y


def assemble(net, target, pieces, metas, pos):
    for ref, (near, first, flip) in zip(pieces, metas):
        if near is None:
            target[...] = ref[0]
            continue
        rows = D // net.n_dp
        for index in range(ref.shape[0]):
            rank = first + index
            block = block_row(net, pos, near, rank, flip)
            start = pl.multiple_of(block * rows, 16)
            target[pl.ds(start, rows), :] = ref[index, 0:rows, :]


def ceil_to(n, m):
    return -(-n // m) * m


def turned(value):
    rows, cols = value.shape
    padded = jnp.pad(value, ((0, ceil_to(rows, 128) - rows), (0, ceil_to(cols, 128) - cols)))
    return padded.T[:cols, :rows]


def pack_attend_kernel(qkv_ref, out_ref, gain_ref, pack_ref):
    rows, width = qkv_ref.shape[1:]
    parts = [qkv_ref[member].astype(BF) for member in range(3)] + [turned(out_ref[...]).astype(BF)]
    for member, part in enumerate(parts):
        pack_ref[0:rows, member * width : (member + 1) * width] = part
    if pack_ref.shape[0] > rows:
        gains = jnp.pad(gain_ref[...], ((0, 6), (0, 4 * width - rows)))
        pack_ref[rows:, :] = gains.astype(BF)


def pack_attend(net, w_qkv, w_out, gains):
    _, rows, width = w_qkv.shape
    total = rows + 8 if net.fast else rows
    return pl.pallas_call(
        pack_attend_kernel,
        grid=(1,),
        in_specs=[whole(w_qkv.shape), whole(w_out.shape), whole(gains.shape)],
        out_specs=whole((total, 4 * width)),
        out_shape=jax.ShapeDtypeStruct((total, 4 * width), BF),
        compiler_params=params(),
        name="pack_attend",
    )(hbm(w_qkv), hbm(w_out), hbm(gains))


def pack_feed_kernel(gu_ref, down_ref, *pack_refs):
    units = gu_ref.shape[2] // 2
    for part, pack_ref in enumerate(pack_refs):
        span = slice(part * units, (part + 1) * units)
        pack_ref[:, 0:units] = gu_ref[0, :, span].astype(BF)
        pack_ref[:, units : 2 * units] = gu_ref[1, :, span].astype(BF)
        pack_ref[:, 2 * units : 3 * units] = down_ref[:, span].astype(BF)


def pack_feed(w_gu, w_down):
    _, rows, units = w_gu.shape
    shape = (rows, 3 * units // 2)
    return pl.pallas_call(
        pack_feed_kernel,
        grid=(1,),
        in_specs=[whole(w_gu.shape), whole(w_down.shape)],
        out_specs=[whole(shape)] * 2,
        out_shape=[jax.ShapeDtypeStruct(shape, BF)] * 2,
        compiler_params=params(),
        name="pack_feed",
    )(hbm(w_gu), hbm(w_down))


def spread_gains(net, gain_ref, pieces, pos):
    rows = D // net.n_dp
    for block in range(net.n_dp):
        rank = lax.bitwise_xor(pos[0], jnp.int32(block // 2))
        here = pieces[0][rank].astype(F32)[rows : rows + 8, :rows]
        there = pieces[1][rank].astype(F32)[rows : rows + 8, :rows]
        gain_ref[:, block * rows : (block + 1) * rows] = jnp.where(pos[1] == block % 2, here, there)


def row_tiles(rows, size):
    return [slice(start, start + size) for start in range(0, rows, size)]


def project_kernel(net, metas, first, pos, x_ref, *refs):
    if not net.fast and first:
        given, refs = refs[0], refs[1:]
    count = len(metas)
    pieces, refs = refs[:count], refs[count:]
    if first:
        h_ref, gain_ref, refs = refs[0], refs[1], refs[2:]
    qkv_ref, wqkv_ref, wout_ref, full = refs
    assemble(net, full, pieces, metas, pos)
    wqkv_ref[...] = full[:, : wqkv_ref.shape[1]]
    wout_ref[...] = full[:, wqkv_ref.shape[1] :]
    if first and net.fast:
        spread_gains(net, gain_ref, pieces, pos)
    elif first:
        gain_ref[...] = given[...]
    for tile in row_tiles(x_ref.shape[0], TILE):
        if first:
            value = x_ref[tile, :].astype(F32)
            inverse = lax.rsqrt(jnp.mean(value * value, axis=1, keepdims=True) + NORM_EPS)
            rows = (value * inverse * gain_ref[0:1, :]).astype(BF)
            h_ref[tile, :] = rows
        else:
            rows = x_ref[tile, :]
        qkv_ref[tile, :] = dot_nn(rows, wqkv_ref[...]).astype(BF)


def project(net, pos, x, pieces, head_width, gains=None, first=False):
    rows = x.shape[0]
    arrays = [x] + ([gains] if first and not net.fast else []) + [p[0] for p in pieces]
    metas = [p[1:] for p in pieces]
    outs = [((rows, 3 * head_width), BF), ((D, 3 * head_width), BF), ((D, head_width), BF)]
    if first:
        outs = [((rows, D), BF), ((8, D), F32)] + outs
    return in_vmem(
        functools.partial(project_kernel, net, metas, first),
        "project",
        [pos],
        arrays,
        outs,
        [((D, 4 * head_width), BF)],
        2 * rows * D * 3 * head_width,
    )


def key_valid(meta, seq, count, axis, shape, start):
    place = lax.broadcasted_iota(jnp.int32, shape, axis) + start + meta[count + seq]
    place = jnp.where(place >= L, place - L, place)
    return place < meta[seq]


def attend_kernel(heads, seqs, meta, qkv_ref, o_ref, inverse_ref, expo_ref, key_wide, value_wide):
    width = heads * DH
    lane = lax.broadcasted_iota(jnp.int32, (TILE, 128), 1)
    column = lax.broadcasted_iota(jnp.int32, (L, DH), 1)
    one = jnp.where(column == 0, 1.0, 0.0).astype(BF)
    for seq in range(seqs):
        span = slice(seq * L, (seq + 1) * L)
        valid = key_valid(meta, seq, seqs, 0, (L, DH), 0)
        mask = jnp.where(column == 0, jnp.where(valid, 0.0, MASK_FILL), 0.0).astype(BF)
        for head in range(heads):
            keys = qkv_ref[span, width + head * DH : width + (head + 1) * DH]
            values = qkv_ref[span, 2 * width + head * DH : 2 * width + (head + 1) * DH]
            key_wide[head] = jnp.concatenate([keys, mask], axis=1)
            value_wide[head] = jnp.concatenate([values, one], axis=1)
        for tile in row_tiles(L, TILE):
            rows = slice(seq * L + tile.start, seq * L + tile.stop)
            scores = []
            for head in range(heads):
                queries = qkv_ref[rows, head * DH : (head + 1) * DH]
                queries = jnp.concatenate([queries, one[0:TILE]], axis=1)
                scores.append(dot_nt(queries, key_wide[head]))
            inverses = jnp.zeros((TILE, 128), F32)
            outs = []
            for head in range(heads):
                top = jnp.max(scores[head], axis=1, keepdims=True)
                expo = jnp.exp2((scores[head] - top) * SCALE2).astype(BF)
                expo_ref[head, rows, :] = expo
                mixed = dot_nn(expo, value_wide[head])
                inverse = 1.0 / mixed[:, DH : DH + 1]
                outs.append(mixed[:, 0:DH] * inverse)
                inverses = jnp.where(lane == head, inverse, inverses)
            o_ref[rows, :] = jnp.concatenate(outs, axis=1).astype(BF)
            inverse_ref[rows, :] = inverses


def attend(meta, qkv, head_width, seqs):
    rows = qkv.shape[0]
    heads = head_width // DH
    return in_vmem(
        functools.partial(attend_kernel, heads, seqs),
        "attend",
        [meta],
        [qkv],
        [((rows, head_width), BF), ((rows, 128), F32), ((heads, rows, L), BF)],
        [((heads, L, 2 * DH), BF)] * 2,
        16 * rows * L * head_width,
    )


def attend_back_kernel(heads, chosen, seqs, qkv_ref, do_ref, o_ref, inverse_ref, expo_ref, *refs):
    out_ref = refs[-1]
    width = heads * DH
    for seq in range(seqs):
        span = slice(seq * L, (seq + 1) * L)
        for head in chosen:
            cols = slice(head * DH, (head + 1) * DH)
            key_cols = slice(width + head * DH, width + (head + 1) * DH)
            value_cols = slice(2 * width + head * DH, 2 * width + (head + 1) * DH)
            inverse = inverse_ref[span, head : head + 1]
            grads = do_ref[span, cols].astype(F32) * inverse
            inner = jnp.sum(grads * o_ref[span, cols].astype(F32), axis=1, keepdims=True)
            grads = grads.astype(BF)
            expo = expo_ref[head, span, :]
            grad_probs = dot_nt(grads, qkv_ref[span, value_cols])
            grad_scores = (expo.astype(F32) * (grad_probs - inner)).astype(BF)
            grad_values = dot_tn(grads, expo)
            grad_keys = dot_tn(qkv_ref[span, cols], grad_scores) * SCALE
            grad_queries = dot_nn(grad_scores, qkv_ref[span, key_cols]) * SCALE
            out_ref[span, key_cols] = grad_keys.T.astype(BF)
            out_ref[span, value_cols] = grad_values.T.astype(BF)
            out_ref[span, cols] = grad_queries.astype(BF)


def attend_back(qkv, grad, mixed, saved, head_width, seqs, chosen, into=None, light=False):
    rows = qkv.shape[0]
    arrays = [qkv, grad, mixed] + list(saved) + ([] if into is None else [into])
    return in_vmem(
        functools.partial(attend_back_kernel, head_width // DH, chosen, seqs),
        "attend_back",
        [],
        arrays,
        [((rows, 3 * head_width), BF)],
        (),
        None if light else 10 * rows * L * DH * len(chosen),
        {} if into is None else {5: 0},
    )[0]


def feed_kernel(net, metas, units, first, pos, h_ref, dy_ref, *refs):
    pieces, refs = refs[: len(metas)], refs[len(metas) :]
    if not first:
        f_prev, d_prev, refs = refs[0], refs[1], refs[2:]
    mid_ref, f_ref, d_ref, full = refs
    assemble(net, full, pieces, metas, pos)
    root = math.sqrt(2.0 / math.pi)
    w_gate, w_up, w_down = (full[:, j * units : (j + 1) * units] for j in range(3))
    for tile in row_tiles(h_ref.shape[0], FEED_TILE):
        hidden_in, back_in = h_ref[tile, :], dy_ref[tile, :]
        gate = dot_nn(hidden_in, w_gate)
        up = dot_nn(hidden_in, w_up)
        grad_hidden = dot_nn(back_in, w_down)
        square = gate * gate
        tanh = jnp.tanh(gate * (root + (root * 0.044715) * square))
        half = 0.5 * (1.0 + tanh)
        gelu = gate * half
        slope = half + (0.5 * gate) * (1.0 - tanh * tanh) * (root + (3.0 * root * 0.044715) * square)
        hidden = (gelu * up).astype(BF)
        grad_gate = (grad_hidden * up * slope).astype(BF)
        grad_up = (grad_hidden * gelu).astype(BF)
        mid_ref[tile, 0:units] = grad_gate
        mid_ref[tile, units : 2 * units] = grad_up
        mid_ref[tile, 2 * units : 3 * units] = hidden
        f_part = dot_nt(hidden, w_down)
        d_part = dot_nt(grad_gate, w_gate) + dot_nt(grad_up, w_up)
        if not first:
            f_part += f_prev[tile, :].astype(F32)
            d_part += d_prev[tile, :].astype(F32)
        f_ref[tile, :] = f_part.astype(BF)
        d_ref[tile, :] = d_part.astype(BF)


def feed(net, pos, h2, back, pieces, units, previous):
    rows = h2.shape[0]
    arrays = [h2, back] + [p[0] for p in pieces] + list(previous)
    metas = [p[1:] for p in pieces]
    return in_vmem(
        functools.partial(feed_kernel, net, metas, units, not previous),
        "feed",
        [pos],
        arrays,
        [((rows, 3 * units), BF)] + [((rows, D), BF)] * 2,
        [((D, 3 * units), BF)],
        2 * rows * D * 6 * units,
    )


def second_kernel(x_ref, a_ref, b_ref, gain_ref, h_ref):
    tiles = row_tiles(x_ref.shape[0], TILE)
    for index, tile in enumerate(tiles):
        other = tiles[(index + len(tiles) // 2) % len(tiles)]
        value = x_ref[tile, :].astype(F32) + (a_ref[tile, :].astype(F32) + b_ref[other, :].astype(F32))
        inverse = lax.rsqrt(jnp.mean(value * value, axis=1, keepdims=True) + NORM_EPS)
        h_ref[tile, :] = (value * inverse * gain_ref[1:2, :]).astype(BF)


def second_norm(x, a_own, a_other, gain):
    return in_vmem(second_kernel, "second_norm", [], [x, a_own, a_other, gain], [(x.shape, BF)], (), 10 * x.size)[0]


def middle_kernel(x_ref, a_ref, b_ref, dy_ref, d_ref, e_ref, gain_ref, wo_ref, wx_ref,
                  da_ref, do_ref, dx_ref, dx2_ref):
    gain = gain_ref[1:2, :]
    tiles = row_tiles(x_ref.shape[0], TILE)
    for index, tile in enumerate(tiles):
        other = tiles[(index + len(tiles) // 2) % len(tiles)]
        second_in = x_ref[tile, :].astype(F32) + (a_ref[tile, :].astype(F32) + b_ref[other, :].astype(F32))
        inverse = lax.rsqrt(jnp.mean(second_in * second_in, axis=1, keepdims=True) + NORM_EPS)
        normed = second_in * inverse
        grad = d_ref[tile, :].astype(F32) + e_ref[other, :].astype(F32)
        scaled = grad * gain
        center = jnp.mean(scaled * normed, axis=1, keepdims=True)
        total = dy_ref[tile, :].astype(F32) + inverse * (scaled - normed * center)
        low = total.astype(BF)
        da_ref[tile, :] = low
        do_ref[tile, :] = dot_nn(low, wo_ref[...]).astype(BF)
        dx_ref[tile, :] = dot_nn(low, wx_ref[...]).astype(BF)
        if index < len(tiles) // 2:
            dx2_ref[tile, :] = total


def middle(x, a_own, a_other, back, d_own, d_other, gain, w_own, w_other):
    rows = x.shape[0]
    width = w_own.shape[1]
    return in_vmem(
        middle_kernel,
        "middle",
        [],
        [x, a_own, a_other, back, d_own, d_other, gain, w_own, w_other],
        [((rows, D), BF), ((rows, width), BF), ((rows, width), BF), ((rows // 2, D), F32)],
        (),
        4 * rows * D * width,
    )


def grad_kernel(net, spans, pos, left_ref, right_ref, mid_ref, tail_ref, full_ref, *outs):
    for source, other, target, size in spans:
        left = (left_ref, right_ref)[source]
        values = (mid_ref, tail_ref)[other[0]][:, other[1] : other[1] + size]
        full_ref[:, target : target + size] = dot_tn(left[...], values).astype(BF)
    for part, out in enumerate(outs):
        for index in range(2):
            out[index] = full_ref[block_rows(net, pos, 2 * part + index, 1), :]


def block_rows(net, pos, rank, flip):
    rows = D // net.n_dp
    return pl.ds(pl.multiple_of(block_row(net, pos, True, rank, flip) * rows, 16), rows)


def grad_pack(net, pos, left, right, mid, tail, spans, width, far):
    rows = left.shape[0]
    outs = [((D, width), BF)]
    if far and net.fast:
        outs += [((2, D // net.n_dp, width), BF)] * 2
    return in_vmem(
        functools.partial(grad_kernel, net, spans),
        "weight_grad",
        [pos],
        [left, right, mid, tail],
        outs,
        (),
        2 * rows * D * width,
    )


def sum_kernel(net, paired, pos, own_ref, across_ref, along_ref, *outs):
    for rank in range(net.n_z):
        own = own_ref[block_rows(net, pos, rank, 0), :].astype(F32)
        total = own + (across_ref[rank].astype(F32) + along_ref[rank].astype(F32))
        if not paired:
            outs[rank][...] = total.astype(outs[rank].dtype)
        elif rank % 2:
            outs[2][rank // 2] = total.astype(BF)
        else:
            outs[rank // 2][...] = total


def sum_plane(net, pos, own, near_in, paired):
    _, rows, width = near_in[0].shape
    shape = (rows, width)
    outs = [(shape, F32), (shape, F32), ((2, rows, width), BF)] if paired else [(shape, F32)] + [(shape, BF)] * 3
    kernel = functools.partial(sum_kernel, net, paired)
    return in_vmem(kernel, "sum_plane", [pos], [own] + list(near_in), outs, (), 100 * rows * width)


def pair_kernel(own_ref, in_ref, out_ref):
    out_ref[...] = (own_ref[...] + in_ref[1].astype(F32)).astype(BF)


def turn_kernel(net, pos, x_ref, y_ref, lo_ref, hi_ref, x_out, y_out):
    for rank in range(net.n_z):
        x_part = x_ref[block_rows(net, pos, rank, 0), :]
        y_part = y_ref[block_rows(net, pos, rank, 1), :]
        if rank < 2:
            y_part = (y_part.astype(F32) + lo_ref[rank].astype(F32)).astype(BF)
        else:
            x_part = (x_part.astype(F32) + hi_ref[rank - 2].astype(F32)).astype(BF)
        x_out[rank] = x_part
        y_out[rank] = y_part


class Scatter:
    def __init__(self, net, pos, other):
        self.net, self.pos = net, pos
        self.other = other
        self.far_in = [net.x(other[1]), net.y(other[2])] if net.fast else []
        self.gate = ()

    def own(self, own):
        self.own_full = own[0]
        if not self.net.fast:
            total = own[0].astype(F32) + self.net.x(self.other[0]).astype(F32)
            self.pieces = lax.psum_scatter(total, "dp", scatter_dimension=0, tiled=True)

    def turn(self):
        self.sums, self.near_in = [], []
        if self.net.fast:
            parts = after([self.other[0], self.own_full] + list(self.far_in), self.gate)
            shape = (self.net.n_z, D // self.net.n_dp, self.own_full.shape[1])
            kernel = functools.partial(turn_kernel, self.net)
            self.sums = in_vmem(kernel, "turn", [self.pos], parts, [(shape, BF)] * 2, (), 2 * self.own_full.size)
            self.near_in = [self.net.x(self.sums[0]), self.net.y(self.sums[1])]

    def marks(self):
        return self.sums

    def finish(self):
        if not self.net.fast:
            self.mark = ()
            return [self.pieces]
        sums = sum_plane(self.net, self.pos, self.own_full, self.near_in, False)
        self.mark = sums[0]
        return [sums[0]] + [self.net.z(sums[r], r) for r in range(1, self.net.n_z)]

    def pair(self):
        self.pair_in, self.mark = [], ()
        if self.net.fast:
            own, near_in = after((self.own_full, self.near_in), self.gate)
            self.kept, self.sent, out = sum_plane(self.net, self.pos, own, near_in, True)
            self.mark = self.kept
            self.pair_in = [self.net.z(out, 1)]

    def finish_pair(self):
        if not self.net.fast:
            self.last_sum = ()
            return [self.pieces]
        arrays = after([self.sent] + list(self.pair_in), self.gate)
        (out,) = in_vmem(pair_kernel, "sum_pair", [], arrays, [(self.sent.shape, BF)], (), None)
        self.last_sum = out
        return [self.kept] + list(self.pair_in) + [self.net.z(out, 2)]


def adamw(outs, ins, place, gradient, rate, decay):
    weight, moment, second = (ref[place] for ref in ins)
    moment = BETA_ONE * moment + (1.0 - BETA_ONE) * gradient
    second = BETA_TWO * second + (1.0 - BETA_TWO) * gradient * gradient
    fix_one = 1.0 - BETA_ONE**STEP
    fix_two = 1.0 - BETA_TWO**STEP
    update = moment / fix_one / (jnp.sqrt(second / fix_two) + ADAM_EPS)
    outs[0][place] = weight - rate * (update + decay * weight)
    outs[1][place] = moment
    outs[2][place] = second


def total_of(refs, span):
    total = 0.0
    for ref in refs:
        total += (ref[0, :, span] if len(ref.shape) == 3 else ref[:, span]).astype(F32)
    return total


def put_row(out_ref, column):
    row = turned(column)
    out_ref[...] = jnp.zeros_like(out_ref)
    out_ref[0:1, 0 : row.shape[1]] = row


def total_kernel(count, *refs):
    pieces, (weight, total_ref, gain_ref) = refs[:count], refs[count:]
    width = weight.shape[2]
    total_ref[...] = total_of(pieces, slice(0, 4 * width))
    column = 0.0
    for member in range(3):
        low = weight[member].astype(BF).astype(F32)
        column += jnp.sum(low * total_ref[:, member * width : (member + 1) * width], axis=1, keepdims=True)
    put_row(gain_ref, column)


def total_attend(pieces, weight):
    _, rows, width = weight.shape
    outs = [((rows, 4 * width), F32), ((8, 128), F32)]
    return in_vmem(functools.partial(total_kernel, len(pieces)), "total_attend", [], list(pieces) + [weight], outs)


def adam_attend_kernel(count, *refs):
    total_ref, refs = refs[0], refs[1:]
    qkv, out, qkv_new, out_new = refs[0:3], refs[3:6], refs[6:9], refs[9:12]
    width = qkv[0].shape[2]
    for member in range(3):
        gradient = total_ref[:, member * width : (member + 1) * width]
        adamw(qkv_new, qkv, member, gradient, D ** (-0.5), DECAY_RATE)
    gradient = turned(total_ref[:, 3 * width : 4 * width])
    adamw(out_new, out, ..., gradient, max(1, 3 * HD // L) ** (-0.5), DECAY_RATE)


def adam_feed_kernel(count, *refs):
    groups, refs = (refs[: count // 2], refs[count // 2 : count]), refs[count:]
    gu, down, gu_new, down_new, gain_ref = refs[0:3], refs[3:6], refs[6:9], refs[9:12], refs[12]
    units = gu[0].shape[2] // 2
    column = 0.0
    for part in range(2):
        span = slice(part * units, (part + 1) * units)
        pieces = groups[part]
        for member in range(2):
            gradient = total_of(pieces, slice(member * units, (member + 1) * units))
            low = gu[0][member, :, span].astype(BF).astype(F32)
            column += jnp.sum(low * gradient, axis=1, keepdims=True)
            adamw(gu_new, gu, (member, slice(None), span), gradient, D ** (-0.5), DECAY_RATE)
        gradient = total_of(pieces, slice(2 * units, 3 * units))
        adamw(down_new, down, (slice(None), span), gradient, FF ** (-0.5), DECAY_RATE)
    put_row(gain_ref, column)


def adam_call(kernel, pieces, states, name, with_gain):
    shapes = [jax.ShapeDtypeStruct(s.shape, F32) for s in states]
    if with_gain:
        shapes.append(jax.ShapeDtypeStruct((8, 128), F32))
    return pl.pallas_call(
        functools.partial(kernel, len(pieces)),
        grid=(1,),
        in_specs=[whole(a.shape) for a in list(pieces) + list(states)],
        out_specs=[whole(s.shape) for s in shapes],
        out_shape=shapes,
        compiler_params=params(),
        cost_estimate=cost(0, 0),
        name=name,
    )(*pieces, *states)


def first_grad_kernel(own_ref, other_ref, wo_ref, wx_ref, f_ref, send_ref, keep_ref):
    half = own_ref.shape[0] // 2
    send_ref[0:half, :] = f_ref[half:, :]
    for tile in row_tiles(2 * half, TILE):
        total = (dot_nt(own_ref[tile, :], wo_ref[...]) + dot_nt(other_ref[tile, :], wx_ref[...])).astype(BF)
        if tile.start < half:
            keep_ref[tile, :] = total
        else:
            send_ref[tile, :] = total


def first_grad(own, other, w_own, w_other, f_part):
    rows = own.shape[0]
    return in_vmem(
        first_grad_kernel,
        "first_grad",
        [],
        [own, other, w_own, w_other, f_part],
        [((rows, D), BF), ((rows // 2, D), BF)],
        (),
        4 * rows * D * own.shape[1],
    )


def last_kernel(x_ref, a_ref, b_ref, f_ref, in_ref, d_ref, gain_ref, dx2_ref, out_ref, grad_ref):
    half = x_ref.shape[0]
    for tile in row_tiles(half, TILE):
        other = slice(half + tile.start, half + tile.stop)
        value = x_ref[tile, :].astype(F32)
        second_in = value + (a_ref[tile, :].astype(F32) + b_ref[other, :].astype(F32))
        out_ref[tile, :] = (second_in + (f_ref[tile, :].astype(F32) + in_ref[tile, :].astype(F32))).astype(BF)
        inverse = lax.rsqrt(jnp.mean(value * value, axis=1, keepdims=True) + NORM_EPS)
        normed = value * inverse
        scaled = (d_ref[tile, :].astype(F32) + in_ref[other, :].astype(F32)) * gain_ref[0:1, :]
        center = jnp.mean(scaled * normed, axis=1, keepdims=True)
        grad_ref[tile, :] = dx2_ref[tile, :] + inverse * (scaled - normed * center)


def last(x, *arrays):
    shapes = [jax.ShapeDtypeStruct(x.shape, BF), jax.ShapeDtypeStruct(x.shape, F32)]
    return pl.pallas_call(
        last_kernel,
        grid=(1,),
        in_specs=[whole(x.shape)] + [VMEM_SPEC] * len(arrays),
        out_specs=[whole(x.shape)] * 2,
        out_shape=shapes,
        compiler_params=params(),
        cost_estimate=cost(0, 0),
        name="last",
    )(x, *arrays)


def gain_step(weight, moment, second, gradient):
    moment_new = BETA_ONE * moment + (1.0 - BETA_ONE) * gradient
    second_new = BETA_TWO * second + (1.0 - BETA_TWO) * gradient * gradient
    fix_one = 1.0 - BETA_ONE**STEP
    fix_two = 1.0 - BETA_TWO**STEP
    update = moment_new / fix_one / (jnp.sqrt(second_new / fix_two) + ADAM_EPS)
    return (weight - GAIN_RATE * update, moment_new, second_new)


def body(
    net,
    inputs,
    cotangent,
    lengths,
    gains,
    w_qkv,
    m_qkv,
    v_qkv,
    w_out,
    m_out,
    v_out,
    w_gu,
    m_gu,
    v_gu,
    w_down,
    m_down,
    v_down,
    m_gain,
    v_gain,
):
    own_rows = inputs.shape[0]
    rows = 2 * own_rows
    shard = w_qkv.shape[1]
    width = w_qkv.shape[2]
    half_units = w_gu.shape[2] // 2
    dp, mp = lax.axis_index("dp"), lax.axis_index("mp")
    core = lax.rem(mp, 2)
    pos = jnp.stack([dp // 2, lax.rem(dp, 2)]).astype(jnp.int32)

    if own_rows % L == 0:
        each = own_rows // L
        seqs = 2 * each
        pair = mp + 1 - 2 * core
        own_len = lax.dynamic_slice(lengths, (mp * each,), (each,))
        other_len = lax.dynamic_slice(lengths, (pair * each,), (each,))
        meta = jnp.concatenate([own_len, other_len, jnp.zeros((seqs,), jnp.int32)])
    else:
        seqs = rows // L
        len_here = lax.dynamic_slice(lengths, ((mp // 2) * seqs,), (seqs,))
        meta = jnp.concatenate([len_here, jnp.full((seqs,), core * own_rows, jnp.int32)])

    x_in = net.core(inputs)
    back_in = net.core(cotangent)
    pack_a = pack_attend(net, w_qkv, w_out, gains)
    packs_f = pack_feed(after(w_gu, pack_a), w_down.T)
    stack_a = stacked(net, after(gather_line(net, pack_a), packs_f))
    pack_one, pack_two = after(packs_f, stack_a)
    line_one = gather_line(net, pack_one)
    plane_a = Plane(net, stack_a, True)
    gain_given = None
    if not net.fast:
        gain_all = lax.all_gather(gains.astype(BF), "dp", axis=1, tiled=True).astype(F32)
        gain_given = jnp.pad(gain_all, ((0, 6), (0, 0)))

    x_pair = jnp.concatenate([inputs, x_in], axis=0)
    back = jnp.concatenate([cotangent, back_in], axis=0)
    x_pair, back = together(x_pair, back)
    h1, gain_wide, qkv_own, wqkv_own, wout_own = project(net, pos, x_pair, plane_a.own(), width, gain_given, True)
    plane_a.near_in = after(plane_a.near_in, qkv_own)
    plane_a.turn()
    qkv_own, line_one, pack_two = together(qkv_own, line_one, pack_two)
    feed_one = Plane(net, stacked(net, line_one), True)
    two_in = [net.z(pack_two, 2)] if net.fast else []
    o_own, *saved_own = attend(meta, qkv_own, width, seqs)
    o_own, plane_a.far_in, two_in = together(o_own, plane_a.far_in, two_in)
    two_last = [net.z(jnp.stack([pack_two] + two_in), 1)] if net.fast else []

    h1_late = after(h1, o_own)
    qkv_other, wqkv_other, wout_other = project(net, pos, h1_late, plane_a.other(), width)
    o_other, *saved_other = attend(meta, qkv_other, width, seqs)
    o_other, feed_one.near_in, two_last = together(o_other, feed_one.near_in, two_last)
    feed_one.turn()

    o_other = after(o_other, feed_one.halves)
    branch = (dot_nt(o_own, wout_own) + dot_nt(o_other, wout_other)).astype(BF)
    branch_in = net.core(branch)
    line_two = [pack_two]
    if net.fast:
        line_two = [pack_two, two_last[0][0], two_in[0], two_last[0][1]]
    feed_two = Plane(net, stacked(net, line_two), True)
    h2 = second_norm(x_pair, branch, branch_in, gain_wide)

    pack_width = 3 * half_units
    f_spans = [(0, (0, 0), 0, 2 * half_units), (1, (0, 2 * half_units), 2 * half_units, half_units)]

    def feed_grads(mid, far):
        return grad_pack(net, pos, h2, back, mid, mid, f_spans, pack_width, far)

    mid_own, f_part, d_part = feed(net, pos, h2, back, feed_one.own(), half_units, [])
    mid_other, f_part, d_part = feed(net, pos, h2, back, feed_one.other(), half_units, [f_part, d_part])
    one_other = feed_grads(mid_other, True)
    one_own = feed_grads(mid_own, False)
    f_part, d_part, feed_two.near_in = together(f_part, d_part, after(feed_two.near_in, (one_own, one_other)))
    feed_two.turn()
    mid_own, f_part, d_part = feed(net, pos, h2, back, feed_two.own(), half_units, [f_part, d_part])
    sum_one = Scatter(net, pos, after(one_other, d_part))
    sum_one.own(one_own)
    mid_other, f_part, d_part = feed(net, pos, h2, back, feed_two.other(), half_units, [f_part, d_part])
    mid_other, f_part, d_part, sum_one.far_in = together(mid_other, f_part, d_part, sum_one.far_in)
    d_in = net.core(d_part)
    g_other = feed_grads(after(mid_other, d_part), True)
    sum_two = Scatter(net, pos, g_other)
    g_own = feed_grads(after(mid_own, g_other), False)
    sum_two.own(g_own)
    sum_one.gate = g_own
    sum_one.turn()
    d_in = after(d_in, sum_one.marks())

    da, do_own, do_other, dx2 = middle(
        x_pair, branch, branch_in, back, d_part, d_in, gain_wide, wout_own, wout_other
    )
    da, do_own, do_other, dx2, sum_two.far_in = together(da, do_own, do_other, dx2, sum_two.far_in)
    heads = tuple(range(width // DH))
    dqkv_other = attend_back(qkv_other, do_other, o_other, saved_other, width, seqs, heads)
    a_spans = [(0, (0, 0), 0, 3 * width), (1, (1, 0), 3 * width, width)]
    g_other = grad_pack(net, pos, h1, da, dqkv_other, o_other, a_spans, 4 * width, True)
    sum_a = Scatter(net, pos, g_other)
    sum_one.gate = g_other[0]
    sum_one.pair()
    sum_two.gate = sum_one.mark
    sum_two.turn()
    do_own = after(do_own, (g_other, sum_one.mark, sum_two.marks()))
    dqkv_own = attend_back(qkv_own, do_own, o_own, saved_own, width, seqs, heads[:2], light=True)
    dqkv_own, sum_a.far_in = together(dqkv_own, sum_a.far_in)
    dqkv_own = attend_back(qkv_own, do_own, o_own, saved_own, width, seqs, heads[2:], dqkv_own)
    dqkv_own, sum_one.pair_in = together(dqkv_own, sum_one.pair_in)
    g_own = grad_pack(net, pos, h1, da, dqkv_own, o_own, a_spans, 4 * width, False)
    sum_a.own(g_own)
    sum_a.turn()
    sum_one.gate = sum_two.gate = sum_a.sums
    pieces_one = sum_one.finish_pair()
    sum_two.pair()
    dqkv_own, dqkv_last = after((dqkv_own, dqkv_other), (sum_one.last_sum, sum_two.mark))
    send, dh1 = first_grad(dqkv_own, dqkv_last, wqkv_own, wqkv_other, f_part)
    send, sum_two.pair_in, pieces_one = together(send, sum_two.pair_in, pieces_one)
    sum_two.gate = send
    pieces_two = sum_two.finish_pair()
    sum_a.near_in = after(sum_a.near_in, sum_two.last_sum)
    pieces_a = sum_a.finish()
    last_in = net.core(after(send, sum_a.mark))

    output, input_grad = last(inputs, branch, branch_in, f_part, last_in, dh1, gain_wide, dx2)
    states_f = [w_gu, m_gu, v_gu, w_down.T, m_down.T, v_down.T]
    feed_new = adam_call(adam_feed_kernel, after(pieces_one + pieces_two, output), states_f, "adam_feed", True)
    pieces_a = after(pieces_a, feed_new[-1])
    total_a, gain_one = total_attend(pieces_a, w_qkv)
    terms = jnp.concatenate([gain_one[0:1], feed_new[-1][0:1]], axis=0)
    states_a = [w_qkv, m_qkv, v_qkv, w_out, m_out, v_out]
    attend_new = adam_call(adam_attend_kernel, [total_a], states_a, "adam_attend", False)
    total = terms + net.core(terms) + net.x(terms) + net.cross(terms)
    gain_grad = total[:, :shard] / round_low(gains)
    new_gains, gain_moment, gain_second = gain_step(gains, m_gain, v_gain, gain_grad)
    return (
        (output, input_grad, new_gains, gain_moment, gain_second)
        + tuple(attend_new[:6])
        + tuple(feed_new[:3])
        + tuple(v.T for v in feed_new[3:6])
    )


def solution(mesh):
    net = Net(mesh.shape["dp"], mesh.shape["mp"])
    rows = P(("dp", "mp"), None)
    gain = P(None, "dp")
    wide = P(None, "dp", "mp")
    tall = P("mp", "dp")
    return jax.shard_map(
        functools.partial(body, net),
        mesh=mesh,
        in_specs=(rows, rows, P("dp"), gain) + (wide,) * 3 + (tall,) * 3 + (wide,) * 3 + (tall,) * 3 + (gain,) * 2,
        out_specs=(rows, rows) + (gain,) * 3 + (wide,) * 3 + (tall,) * 3 + (wide,) * 3 + (tall,) * 3,
        check_vma=False,
    )
```

```python
import functools
import math

import jax
import jax.numpy as jnp
from jax import lax
from jax.experimental import pallas as pl
from jax.experimental.pallas import tpu as pltpu
from jax.sharding import PartitionSpec as P

D = 768
DH = 64
FF = 2048
L = 1024
STEP = 10
HD = 768

NORM_EPS = 1e-06
MASK_FILL = -1e30
BETA_ONE = 0.5
BETA_TWO = 0.5
ADAM_EPS = 1e-08
DECAY_RATE = 0.01
GAIN_RATE = 0.5

AXES = ("dp", "mp")
BF = jnp.bfloat16
F32 = jnp.float32
SCALE = DH ** (-0.5)
SCALE2 = SCALE * math.log2(math.e)
VMEM_LIMIT = 12 * 1024 * 1024
TILE = 256
FEED_TILE = 512
COST_CUT = 1


def params(**kw):
    return pltpu.CompilerParams(vmem_limit_bytes=VMEM_LIMIT, **kw)


def cost(flops, nbytes, trans=0):
    return pl.CostEstimate(flops=int(flops) // COST_CUT, bytes_accessed=int(nbytes) // COST_CUT, transcendentals=0)


def round_low(value):
    return lax.reduce_precision(value, 8, 7)


def after(values, anchor):
    return lax.optimization_barrier((values, anchor))[0]


def dot_nn(a, b):
    return lax.dot_general(a, b, (((1,), (0,)), ((), ())), preferred_element_type=F32)


def dot_nt(a, b):
    return lax.dot_general(a, b, (((1,), (1,)), ((), ())), preferred_element_type=F32)


def dot_tn(a, b):
    return lax.dot_general(a, b, (((0,), (0,)), ((), ())), preferred_element_type=F32)


def together(*values):
    return lax.optimization_barrier(values)


def hbm(array):
    return pltpu.with_memory_space_constraint(array, pltpu.HBM)


SMEM_SPEC = pl.BlockSpec(memory_space=pltpu.SMEM)
VMEM_SPEC = pl.BlockSpec(memory_space=pltpu.VMEM)


def whole(shape):
    return pl.BlockSpec(shape, lambda *_: (0,) * len(shape))


def in_vmem(kernel, name, scalars, arrays, outs, scratch=(), flops=0, aliases=None):
    nbytes = sum(a.size * a.dtype.itemsize for a in arrays)
    return pl.pallas_call(
        kernel,
        in_specs=[SMEM_SPEC] * len(scalars) + [VMEM_SPEC] * len(arrays),
        out_specs=[VMEM_SPEC] * len(outs),
        out_shape=[pltpu.VMEM(shape, dtype) for shape, dtype in outs],
        scratch_shapes=[pltpu.VMEM(shape, dtype) for shape, dtype in scratch],
        input_output_aliases=aliases or {},
        compiler_params=params(),
        cost_estimate=cost(0, 0) if flops is None else cost(flops, nbytes),
        name=name,
    )(*scalars, *arrays)


class Net:
    def __init__(self, n_dp, n_mp):
        self.n_dp, self.n_mp = n_dp, n_mp
        self.n_y = 2
        self.n_z = n_dp // 2
        self.fast = n_dp == 8 and n_mp == 4 and (D // n_dp) % 16 == 0

    def perm(self, move):
        pairs = []
        for dp in range(self.n_dp):
            for mp in range(self.n_mp):
                z, y, x, c = dp // 2, dp % 2, mp // 2, mp % 2
                z2, y2, x2, c2 = move(z, y, x, c)
                pairs.append((dp * self.n_mp + mp, (z2 * 2 + y2) * self.n_mp + x2 * 2 + c2))
        return pairs

    def core(self, v):
        return lax.ppermute(v, AXES, self.perm(lambda z, y, x, c: (z, y, x, 1 - c)))

    def x(self, v):
        return lax.ppermute(v, AXES, self.perm(lambda z, y, x, c: (z, y, 1 - x, c)))

    def cross(self, v):
        return lax.ppermute(v, AXES, self.perm(lambda z, y, x, c: (z, y, 1 - x, 1 - c)))

    def y(self, v):
        return lax.ppermute(v, AXES, self.perm(lambda z, y, x, c: (z, 1 - y, x, c)))

    def z(self, v, r):
        return lax.ppermute(v, AXES, self.perm(lambda z, y, x, c: (z ^ r, y, x, c)))


def gather_line(net, shard):
    if not net.fast:
        return [shard]
    return [shard] + [net.z(shard, r) for r in range(1, net.n_z)]


def stacked(net, line):
    return jnp.stack(line) if net.fast else line[0]


class Plane:
    def __init__(self, net, line, near):
        self.net, self.line, self.near = net, line, near
        if net.fast:
            self.near_in = [net.y(line), net.x(line)]
        else:
            own = lax.all_gather(line, "dp", axis=0, tiled=True)[None]
            self.near_in = [own, net.x(own)]
        self.far_in, self.halves = [], ()

    def turn(self):
        if self.net.fast:
            y_all, x_all = self.near_in
            self.halves = (y_all[:2], x_all[2:])
            self.far_in = [self.net.x(self.halves[0]), self.net.y(self.halves[1])]

    def own(self):
        if not self.net.fast:
            return [(self.near_in[0], None, 0, 0)]
        return [(self.line, self.near, 0, 0), (self.near_in[0], self.near, 0, 1)]

    def other(self):
        if not self.net.fast:
            return [(self.near_in[1], None, 0, 0)]
        return [
            (self.near_in[1], self.near, 0, 0),
            (self.far_in[0], self.near, 0, 1),
            (self.far_in[1], self.near, 2, 1),
        ]


def block_row(net, pos, near, rank, flip):
    z = lax.bitwise_xor(pos[0], jnp.int32(rank)) if near else rank
    y = pos[1] if not flip else 1 - pos[1]
    return z * 2 + y


def assemble(net, target, pieces, metas, pos):
    for ref, (near, first, flip) in zip(pieces, metas):
        if near is None:
            target[...] = ref[0]
            continue
        rows = D // net.n_dp
        for index in range(ref.shape[0]):
            rank = first + index
            block = block_row(net, pos, near, rank, flip)
            start = pl.multiple_of(block * rows, 16)
            target[pl.ds(start, rows), :] = ref[index, 0:rows, :]


def ceil_to(n, m):
    return -(-n // m) * m


def turned(value):
    rows, cols = value.shape
    padded = jnp.pad(value, ((0, ceil_to(rows, 128) - rows), (0, ceil_to(cols, 128) - cols)))
    return padded.T[:cols, :rows]


def pack_attend_kernel(qkv_ref, out_ref, gain_ref, pack_ref):
    rows, width = qkv_ref.shape[1:]
    parts = [qkv_ref[member].astype(BF) for member in range(3)] + [turned(out_ref[...]).astype(BF)]
    for member, part in enumerate(parts):
        pack_ref[0:rows, member * width : (member + 1) * width] = part
    if pack_ref.shape[0] > rows:
        gains = jnp.pad(gain_ref[...], ((0, 6), (0, 4 * width - rows)))
        pack_ref[rows:, :] = gains.astype(BF)


def pack_attend(net, w_qkv, w_out, gains):
    _, rows, width = w_qkv.shape
    total = rows + 8 if net.fast else rows
    return pl.pallas_call(
        pack_attend_kernel,
        grid=(1,),
        in_specs=[whole(w_qkv.shape), whole(w_out.shape), whole(gains.shape)],
        out_specs=whole((total, 4 * width)),
        out_shape=jax.ShapeDtypeStruct((total, 4 * width), BF),
        compiler_params=params(),
        name="pack_attend",
    )(hbm(w_qkv), hbm(w_out), hbm(gains))


def pack_feed_kernel(gu_ref, down_ref, *pack_refs):
    units = gu_ref.shape[2] // 2
    for part, pack_ref in enumerate(pack_refs):
        span = slice(part * units, (part + 1) * units)
        pack_ref[:, 0:units] = gu_ref[0, :, span].astype(BF)
        pack_ref[:, units : 2 * units] = gu_ref[1, :, span].astype(BF)
        pack_ref[:, 2 * units : 3 * units] = down_ref[:, span].astype(BF)


def pack_feed(w_gu, w_down):
    _, rows, units = w_gu.shape
    shape = (rows, 3 * units // 2)
    return pl.pallas_call(
        pack_feed_kernel,
        grid=(1,),
        in_specs=[whole(w_gu.shape), whole(w_down.shape)],
        out_specs=[whole(shape)] * 2,
        out_shape=[jax.ShapeDtypeStruct(shape, BF)] * 2,
        compiler_params=params(),
        name="pack_feed",
    )(hbm(w_gu), hbm(w_down))


def spread_gains(net, gain_ref, pieces, pos):
    rows = D // net.n_dp
    for block in range(net.n_dp):
        rank = lax.bitwise_xor(pos[0], jnp.int32(block // 2))
        here = pieces[0][rank].astype(F32)[rows : rows + 8, :rows]
        there = pieces[1][rank].astype(F32)[rows : rows + 8, :rows]
        gain_ref[:, block * rows : (block + 1) * rows] = jnp.where(pos[1] == block % 2, here, there)


def row_tiles(rows, size):
    return [slice(start, start + size) for start in range(0, rows, size)]


def project_kernel(net, metas, first, pos, x_ref, *refs):
    if not net.fast and first:
        given, refs = refs[0], refs[1:]
    count = len(metas)
    pieces, refs = refs[:count], refs[count:]
    if first:
        h_ref, gain_ref, refs = refs[0], refs[1], refs[2:]
    qkv_ref, wqkv_ref, wout_ref, full = refs
    assemble(net, full, pieces, metas, pos)
    wqkv_ref[...] = full[:, : wqkv_ref.shape[1]]
    wout_ref[...] = full[:, wqkv_ref.shape[1] :]
    if first and net.fast:
        spread_gains(net, gain_ref, pieces, pos)
    elif first:
        gain_ref[...] = given[...]
    for tile in row_tiles(x_ref.shape[0], TILE):
        if first:
            value = x_ref[tile, :].astype(F32)
            inverse = lax.rsqrt(jnp.mean(value * value, axis=1, keepdims=True) + NORM_EPS)
            rows = (value * inverse * gain_ref[0:1, :]).astype(BF)
            h_ref[tile, :] = rows
        else:
            rows = x_ref[tile, :]
        qkv_ref[tile, :] = dot_nn(rows, wqkv_ref[...]).astype(BF)


def project(net, pos, x, pieces, head_width, gains=None, first=False):
    rows = x.shape[0]
    arrays = [x] + ([gains] if first and not net.fast else []) + [p[0] for p in pieces]
    metas = [p[1:] for p in pieces]
    outs = [((rows, 3 * head_width), BF), ((D, 3 * head_width), BF), ((D, head_width), BF)]
    if first:
        outs = [((rows, D), BF), ((8, D), F32)] + outs
    return in_vmem(
        functools.partial(project_kernel, net, metas, first),
        "project",
        [pos],
        arrays,
        outs,
        [((D, 4 * head_width), BF)],
        2 * rows * D * 3 * head_width,
    )


def key_valid(meta, seq, count, axis, shape, start):
    place = lax.broadcasted_iota(jnp.int32, shape, axis) + start + meta[count + seq]
    place = jnp.where(place >= L, place - L, place)
    return place < meta[seq]


def attend_kernel(heads, seqs, meta, qkv_ref, o_ref, inverse_ref, expo_ref, key_wide, value_wide):
    width = heads * DH
    lane = lax.broadcasted_iota(jnp.int32, (TILE, 128), 1)
    column = lax.broadcasted_iota(jnp.int32, (L, DH), 1)
    one = jnp.where(column == 0, 1.0, 0.0).astype(BF)
    for seq in range(seqs):
        span = slice(seq * L, (seq + 1) * L)
        valid = key_valid(meta, seq, seqs, 0, (L, DH), 0)
        mask = jnp.where(column == 0, jnp.where(valid, 0.0, MASK_FILL), 0.0).astype(BF)
        for head in range(heads):
            keys = qkv_ref[span, width + head * DH : width + (head + 1) * DH]
            values = qkv_ref[span, 2 * width + head * DH : 2 * width + (head + 1) * DH]
            key_wide[head] = jnp.concatenate([keys, mask], axis=1)
            value_wide[head] = jnp.concatenate([values, one], axis=1)
        for tile in row_tiles(L, TILE):
            rows = slice(seq * L + tile.start, seq * L + tile.stop)
            scores = []
            for head in range(heads):
                queries = qkv_ref[rows, head * DH : (head + 1) * DH]
                queries = jnp.concatenate([queries, one[0:TILE]], axis=1)
                scores.append(dot_nt(queries, key_wide[head]))
            inverses = jnp.zeros((TILE, 128), F32)
            outs = []
            for head in range(heads):
                top = jnp.max(scores[head], axis=1, keepdims=True)
                expo = jnp.exp2((scores[head] - top) * SCALE2).astype(BF)
                expo_ref[head, rows, :] = expo
                mixed = dot_nn(expo, value_wide[head])
                inverse = 1.0 / mixed[:, DH : DH + 1]
                outs.append(mixed[:, 0:DH] * inverse)
                inverses = jnp.where(lane == head, inverse, inverses)
            o_ref[rows, :] = jnp.concatenate(outs, axis=1).astype(BF)
            inverse_ref[rows, :] = inverses


def attend(meta, qkv, head_width, seqs):
    rows = qkv.shape[0]
    heads = head_width // DH
    return in_vmem(
        functools.partial(attend_kernel, heads, seqs),
        "attend",
        [meta],
        [qkv],
        [((rows, head_width), BF), ((rows, 128), F32), ((heads, rows, L), BF)],
        [((heads, L, 2 * DH), BF)] * 2,
        16 * rows * L * head_width,
    )


def attend_back_kernel(heads, chosen, seqs, qkv_ref, do_ref, o_ref, inverse_ref, expo_ref, *refs):
    out_ref = refs[-1]
    width = heads * DH
    for seq in range(seqs):
        span = slice(seq * L, (seq + 1) * L)
        for head in chosen:
            cols = slice(head * DH, (head + 1) * DH)
            key_cols = slice(width + head * DH, width + (head + 1) * DH)
            value_cols = slice(2 * width + head * DH, 2 * width + (head + 1) * DH)
            inverse = inverse_ref[span, head : head + 1]
            grads = do_ref[span, cols].astype(F32) * inverse
            inner = jnp.sum(grads * o_ref[span, cols].astype(F32), axis=1, keepdims=True)
            grads = grads.astype(BF)
            expo = expo_ref[head, span, :]
            grad_probs = dot_nt(grads, qkv_ref[span, value_cols])
            grad_scores = (expo.astype(F32) * (grad_probs - inner)).astype(BF)
            grad_values = dot_tn(grads, expo)
            grad_keys = dot_tn(qkv_ref[span, cols], grad_scores) * SCALE
            grad_queries = dot_nn(grad_scores, qkv_ref[span, key_cols]) * SCALE
            out_ref[span, key_cols] = grad_keys.T.astype(BF)
            out_ref[span, value_cols] = grad_values.T.astype(BF)
            out_ref[span, cols] = grad_queries.astype(BF)


def attend_back(qkv, grad, mixed, saved, head_width, seqs, chosen, into=None, light=False):
    rows = qkv.shape[0]
    arrays = [qkv, grad, mixed] + list(saved) + ([] if into is None else [into])
    return in_vmem(
        functools.partial(attend_back_kernel, head_width // DH, chosen, seqs),
        "attend_back",
        [],
        arrays,
        [((rows, 3 * head_width), BF)],
        (),
        None if light else 10 * rows * L * DH * len(chosen),
        {} if into is None else {5: 0},
    )[0]


def feed_kernel(net, metas, units, first, pos, h_ref, dy_ref, *refs):
    pieces, refs = refs[: len(metas)], refs[len(metas) :]
    if not first:
        f_prev, d_prev, refs = refs[0], refs[1], refs[2:]
    mid_ref, f_ref, d_ref, full = refs
    assemble(net, full, pieces, metas, pos)
    root = math.sqrt(2.0 / math.pi)
    w_gate, w_up, w_down = (full[:, j * units : (j + 1) * units] for j in range(3))
    for tile in row_tiles(h_ref.shape[0], FEED_TILE):
        hidden_in, back_in = h_ref[tile, :], dy_ref[tile, :]
        gate = dot_nn(hidden_in, w_gate)
        up = dot_nn(hidden_in, w_up)
        grad_hidden = dot_nn(back_in, w_down)
        square = gate * gate
        tanh = jnp.tanh(gate * (root + (root * 0.044715) * square))
        half = 0.5 * (1.0 + tanh)
        gelu = gate * half
        slope = half + (0.5 * gate) * (1.0 - tanh * tanh) * (root + (3.0 * root * 0.044715) * square)
        hidden = (gelu * up).astype(BF)
        grad_gate = (grad_hidden * up * slope).astype(BF)
        grad_up = (grad_hidden * gelu).astype(BF)
        mid_ref[tile, 0:units] = grad_gate
        mid_ref[tile, units : 2 * units] = grad_up
        mid_ref[tile, 2 * units : 3 * units] = hidden
        f_part = dot_nt(hidden, w_down)
        d_part = dot_nt(grad_gate, w_gate) + dot_nt(grad_up, w_up)
        if not first:
            f_part += f_prev[tile, :].astype(F32)
            d_part += d_prev[tile, :].astype(F32)
        f_ref[tile, :] = f_part.astype(BF)
        d_ref[tile, :] = d_part.astype(BF)


def feed(net, pos, h2, back, pieces, units, previous):
    rows = h2.shape[0]
    arrays = [h2, back] + [p[0] for p in pieces] + list(previous)
    metas = [p[1:] for p in pieces]
    return in_vmem(
        functools.partial(feed_kernel, net, metas, units, not previous),
        "feed",
        [pos],
        arrays,
        [((rows, 3 * units), BF)] + [((rows, D), BF)] * 2,
        [((D, 3 * units), BF)],
        2 * rows * D * 6 * units,
    )


def second_kernel(x_ref, a_ref, b_ref, gain_ref, h_ref):
    tiles = row_tiles(x_ref.shape[0], TILE)
    for index, tile in enumerate(tiles):
        other = tiles[(index + len(tiles) // 2) % len(tiles)]
        value = x_ref[tile, :].astype(F32) + (a_ref[tile, :].astype(F32) + b_ref[other, :].astype(F32))
        inverse = lax.rsqrt(jnp.mean(value * value, axis=1, keepdims=True) + NORM_EPS)
        h_ref[tile, :] = (value * inverse * gain_ref[1:2, :]).astype(BF)


def second_norm(x, a_own, a_other, gain):
    return in_vmem(second_kernel, "second_norm", [], [x, a_own, a_other, gain], [(x.shape, BF)], (), 10 * x.size)[0]


def middle_kernel(x_ref, a_ref, b_ref, dy_ref, d_ref, e_ref, gain_ref, wo_ref, wx_ref,
                  da_ref, do_ref, dx_ref, dx2_ref):
    gain = gain_ref[1:2, :]
    tiles = row_tiles(x_ref.shape[0], TILE)
    for index, tile in enumerate(tiles):
        other = tiles[(index + len(tiles) // 2) % len(tiles)]
        second_in = x_ref[tile, :].astype(F32) + (a_ref[tile, :].astype(F32) + b_ref[other, :].astype(F32))
        inverse = lax.rsqrt(jnp.mean(second_in * second_in, axis=1, keepdims=True) + NORM_EPS)
        normed = second_in * inverse
        grad = d_ref[tile, :].astype(F32) + e_ref[other, :].astype(F32)
        scaled = grad * gain
        center = jnp.mean(scaled * normed, axis=1, keepdims=True)
        total = dy_ref[tile, :].astype(F32) + inverse * (scaled - normed * center)
        low = total.astype(BF)
        da_ref[tile, :] = low
        do_ref[tile, :] = dot_nn(low, wo_ref[...]).astype(BF)
        dx_ref[tile, :] = dot_nn(low, wx_ref[...]).astype(BF)
        if index < len(tiles) // 2:
            dx2_ref[tile, :] = total


def middle(x, a_own, a_other, back, d_own, d_other, gain, w_own, w_other):
    rows = x.shape[0]
    width = w_own.shape[1]
    return in_vmem(
        middle_kernel,
        "middle",
        [],
        [x, a_own, a_other, back, d_own, d_other, gain, w_own, w_other],
        [((rows, D), BF), ((rows, width), BF), ((rows, width), BF), ((rows // 2, D), F32)],
        (),
        4 * rows * D * width,
    )


def grad_kernel(net, spans, pos, left_ref, right_ref, mid_ref, tail_ref, full_ref, *outs):
    for source, other, target, size in spans:
        left = (left_ref, right_ref)[source]
        values = (mid_ref, tail_ref)[other[0]][:, other[1] : other[1] + size]
        full_ref[:, target : target + size] = dot_tn(left[...], values).astype(BF)
    for part, out in enumerate(outs):
        for index in range(2):
            out[index] = full_ref[block_rows(net, pos, 2 * part + index, 1), :]


def block_rows(net, pos, rank, flip):
    rows = D // net.n_dp
    return pl.ds(pl.multiple_of(block_row(net, pos, True, rank, flip) * rows, 16), rows)


def grad_pack(net, pos, left, right, mid, tail, spans, width, far):
    rows = left.shape[0]
    outs = [((D, width), BF)]
    if far and net.fast:
        outs += [((2, D // net.n_dp, width), BF)] * 2
    return in_vmem(
        functools.partial(grad_kernel, net, spans),
        "weight_grad",
        [pos],
        [left, right, mid, tail],
        outs,
        (),
        2 * rows * D * width,
    )


def sum_kernel(net, paired, pos, own_ref, across_ref, along_ref, *outs):
    for rank in range(net.n_z):
        own = own_ref[block_rows(net, pos, rank, 0), :].astype(F32)
        total = own + (across_ref[rank].astype(F32) + along_ref[rank].astype(F32))
        if not paired:
            outs[rank][...] = total.astype(outs[rank].dtype)
        elif rank % 2:
            outs[2][rank // 2] = total.astype(BF)
        else:
            outs[rank // 2][...] = total


def sum_plane(net, pos, own, near_in, paired):
    _, rows, width = near_in[0].shape
    shape = (rows, width)
    outs = [(shape, F32), (shape, F32), ((2, rows, width), BF)] if paired else [(shape, F32)] + [(shape, BF)] * 3
    kernel = functools.partial(sum_kernel, net, paired)
    return in_vmem(kernel, "sum_plane", [pos], [own] + list(near_in), outs, (), 100 * rows * width)


def pair_kernel(own_ref, in_ref, out_ref):
    out_ref[...] = (own_ref[...] + in_ref[1].astype(F32)).astype(BF)


def turn_kernel(net, pos, x_ref, y_ref, lo_ref, hi_ref, x_out, y_out):
    for rank in range(net.n_z):
        x_part = x_ref[block_rows(net, pos, rank, 0), :]
        y_part = y_ref[block_rows(net, pos, rank, 1), :]
        if rank < 2:
            y_part = (y_part.astype(F32) + lo_ref[rank].astype(F32)).astype(BF)
        else:
            x_part = (x_part.astype(F32) + hi_ref[rank - 2].astype(F32)).astype(BF)
        x_out[rank] = x_part
        y_out[rank] = y_part


class Scatter:
    def __init__(self, net, pos, other):
        self.net, self.pos = net, pos
        self.other = other
        self.far_in = [net.x(other[1]), net.y(other[2])] if net.fast else []
        self.gate = ()

    def own(self, own):
        self.own_full = own[0]
        if not self.net.fast:
            total = own[0].astype(F32) + self.net.x(self.other[0]).astype(F32)
            self.pieces = lax.psum_scatter(total, "dp", scatter_dimension=0, tiled=True)

    def turn(self):
        self.sums, self.near_in = [], []
        if self.net.fast:
            parts = after([self.other[0], self.own_full] + list(self.far_in), self.gate)
            shape = (self.net.n_z, D // self.net.n_dp, self.own_full.shape[1])
            kernel = functools.partial(turn_kernel, self.net)
            self.sums = in_vmem(kernel, "turn", [self.pos], parts, [(shape, BF)] * 2, (), 2 * self.own_full.size)
            self.near_in = [self.net.x(self.sums[0]), self.net.y(self.sums[1])]

    def marks(self):
        return self.sums

    def finish(self):
        if not self.net.fast:
            self.mark = ()
            return [self.pieces]
        sums = sum_plane(self.net, self.pos, self.own_full, self.near_in, False)
        self.mark = sums[0]
        return [sums[0]] + [self.net.z(sums[r], r) for r in range(1, self.net.n_z)]

    def pair(self):
        self.pair_in, self.mark = [], ()
        if self.net.fast:
            own, near_in = after((self.own_full, self.near_in), self.gate)
            self.kept, self.sent, out = sum_plane(self.net, self.pos, own, near_in, True)
            self.mark = self.kept
            self.pair_in = [self.net.z(out, 1)]

    def finish_pair(self):
        if not self.net.fast:
            self.last_sum = ()
            return [self.pieces]
        arrays = after([self.sent] + list(self.pair_in), self.gate)
        (out,) = in_vmem(pair_kernel, "sum_pair", [], arrays, [(self.sent.shape, BF)], (), None)
        self.last_sum = out
        return [self.kept] + list(self.pair_in) + [self.net.z(out, 2)]


def adamw(outs, ins, place, gradient, rate, decay):
    weight, moment, second = (ref[place] for ref in ins)
    moment = BETA_ONE * moment + (1.0 - BETA_ONE) * gradient
    second = BETA_TWO * second + (1.0 - BETA_TWO) * gradient * gradient
    fix_one = 1.0 - BETA_ONE**STEP
    fix_two = 1.0 - BETA_TWO**STEP
    update = moment / fix_one / (jnp.sqrt(second / fix_two) + ADAM_EPS)
    outs[0][place] = weight - rate * (update + decay * weight)
    outs[1][place] = moment
    outs[2][place] = second


def total_of(refs, span):
    total = 0.0
    for ref in refs:
        total += (ref[0, :, span] if len(ref.shape) == 3 else ref[:, span]).astype(F32)
    return total


def put_row(out_ref, column):
    row = turned(column)
    out_ref[...] = jnp.zeros_like(out_ref)
    out_ref[0:1, 0 : row.shape[1]] = row


def total_kernel(count, *refs):
    pieces, (weight, total_ref, gain_ref) = refs[:count], refs[count:]
    width = weight.shape[2]
    total_ref[...] = total_of(pieces, slice(0, 4 * width))
    column = 0.0
    for member in range(3):
        low = weight[member].astype(BF).astype(F32)
        column += jnp.sum(low * total_ref[:, member * width : (member + 1) * width], axis=1, keepdims=True)
    put_row(gain_ref, column)


def total_attend(pieces, weight):
    _, rows, width = weight.shape
    outs = [((rows, 4 * width), F32), ((8, 128), F32)]
    return in_vmem(functools.partial(total_kernel, len(pieces)), "total_attend", [], list(pieces) + [weight], outs)


def adam_attend_kernel(count, *refs):
    total_ref, refs = refs[0], refs[1:]
    qkv, out, qkv_new, out_new = refs[0:3], refs[3:6], refs[6:9], refs[9:12]
    width = qkv[0].shape[2]
    for member in range(3):
        gradient = total_ref[:, member * width : (member + 1) * width]
        adamw(qkv_new, qkv, member, gradient, D ** (-0.5), DECAY_RATE)
    gradient = turned(total_ref[:, 3 * width : 4 * width])
    adamw(out_new, out, ..., gradient, max(1, 3 * HD // L) ** (-0.5), DECAY_RATE)


def adam_feed_kernel(count, *refs):
    groups, refs = (refs[: count // 2], refs[count // 2 : count]), refs[count:]
    gu, down, gu_new, down_new, gain_ref = refs[0:3], refs[3:6], refs[6:9], refs[9:12], refs[12]
    units = gu[0].shape[2] // 2
    column = 0.0
    for part in range(2):
        span = slice(part * units, (part + 1) * units)
        pieces = groups[part]
        for member in range(2):
            gradient = total_of(pieces, slice(member * units, (member + 1) * units))
            low = gu[0][member, :, span].astype(BF).astype(F32)
            column += jnp.sum(low * gradient, axis=1, keepdims=True)
            adamw(gu_new, gu, (member, slice(None), span), gradient, D ** (-0.5), DECAY_RATE)
        gradient = total_of(pieces, slice(2 * units, 3 * units))
        adamw(down_new, down, (slice(None), span), gradient, FF ** (-0.5), DECAY_RATE)
    put_row(gain_ref, column)


def adam_call(kernel, pieces, states, name, with_gain):
    shapes = [jax.ShapeDtypeStruct(s.shape, F32) for s in states]
    if with_gain:
        shapes.append(jax.ShapeDtypeStruct((8, 128), F32))
    return pl.pallas_call(
        functools.partial(kernel, len(pieces)),
        grid=(1,),
        in_specs=[whole(a.shape) for a in list(pieces) + list(states)],
        out_specs=[whole(s.shape) for s in shapes],
        out_shape=shapes,
        compiler_params=params(),
        cost_estimate=cost(0, 0),
        name=name,
    )(*pieces, *states)


def first_grad_kernel(own_ref, other_ref, wo_ref, wx_ref, f_ref, send_ref, keep_ref):
    half = own_ref.shape[0] // 2
    send_ref[0:half, :] = f_ref[half:, :]
    for tile in row_tiles(2 * half, TILE):
        total = (dot_nt(own_ref[tile, :], wo_ref[...]) + dot_nt(other_ref[tile, :], wx_ref[...])).astype(BF)
        if tile.start < half:
            keep_ref[tile, :] = total
        else:
            send_ref[tile, :] = total


def first_grad(own, other, w_own, w_other, f_part):
    rows = own.shape[0]
    return in_vmem(
        first_grad_kernel,
        "first_grad",
        [],
        [own, other, w_own, w_other, f_part],
        [((rows, D), BF), ((rows // 2, D), BF)],
        (),
        4 * rows * D * own.shape[1],
    )


def last_kernel(x_ref, a_ref, b_ref, f_ref, in_ref, d_ref, gain_ref, dx2_ref, out_ref, grad_ref):
    half = x_ref.shape[0]
    for tile in row_tiles(half, TILE):
        other = slice(half + tile.start, half + tile.stop)
        value = x_ref[tile, :].astype(F32)
        second_in = value + (a_ref[tile, :].astype(F32) + b_ref[other, :].astype(F32))
        out_ref[tile, :] = (second_in + (f_ref[tile, :].astype(F32) + in_ref[tile, :].astype(F32))).astype(BF)
        inverse = lax.rsqrt(jnp.mean(value * value, axis=1, keepdims=True) + NORM_EPS)
        normed = value * inverse
        scaled = (d_ref[tile, :].astype(F32) + in_ref[other, :].astype(F32)) * gain_ref[0:1, :]
        center = jnp.mean(scaled * normed, axis=1, keepdims=True)
        grad_ref[tile, :] = dx2_ref[tile, :] + inverse * (scaled - normed * center)


def last(x, *arrays):
    shapes = [jax.ShapeDtypeStruct(x.shape, BF), jax.ShapeDtypeStruct(x.shape, F32)]
    return pl.pallas_call(
        last_kernel,
        grid=(1,),
        in_specs=[whole(x.shape)] + [VMEM_SPEC] * len(arrays),
        out_specs=[whole(x.shape)] * 2,
        out_shape=shapes,
        compiler_params=params(),
        cost_estimate=cost(0, 0),
        name="last",
    )(x, *arrays)


def gain_step(weight, moment, second, gradient):
    moment_new = BETA_ONE * moment + (1.0 - BETA_ONE) * gradient
    second_new = BETA_TWO * second + (1.0 - BETA_TWO) * gradient * gradient
    fix_one = 1.0 - BETA_ONE**STEP
    fix_two = 1.0 - BETA_TWO**STEP
    update = moment_new / fix_one / (jnp.sqrt(second_new / fix_two) + ADAM_EPS)
    return (weight - GAIN_RATE * update, moment_new, second_new)


def body(
    net,
    inputs,
    cotangent,
    lengths,
    gains,
    w_qkv,
    m_qkv,
    v_qkv,
    w_out,
    m_out,
    v_out,
    w_gu,
    m_gu,
    v_gu,
    w_down,
    m_down,
    v_down,
    m_gain,
    v_gain,
):
    own_rows = inputs.shape[0]
    rows = 2 * own_rows
    shard = w_qkv.shape[1]
    width = w_qkv.shape[2]
    half_units = w_gu.shape[2] // 2
    dp, mp = lax.axis_index("dp"), lax.axis_index("mp")
    core = lax.rem(mp, 2)
    pos = jnp.stack([dp // 2, lax.rem(dp, 2)]).astype(jnp.int32)

    if own_rows % L == 0:
        each = own_rows // L
        seqs = 2 * each
        pair = mp + 1 - 2 * core
        own_len = lax.dynamic_slice(lengths, (mp * each,), (each,))
        other_len = lax.dynamic_slice(lengths, (pair * each,), (each,))
        meta = jnp.concatenate([own_len, other_len, jnp.zeros((seqs,), jnp.int32)])
    else:
        seqs = rows // L
        len_here = lax.dynamic_slice(lengths, ((mp // 2) * seqs,), (seqs,))
        meta = jnp.concatenate([len_here, jnp.full((seqs,), core * own_rows, jnp.int32)])

    x_in = net.core(inputs)
    back_in = net.core(cotangent)
    pack_a = pack_attend(net, w_qkv, w_out, gains)
    packs_f = pack_feed(after(w_gu, pack_a), w_down.T)
    stack_a = stacked(net, after(gather_line(net, pack_a), packs_f))
    pack_one, pack_two = after(packs_f, stack_a)
    line_one = gather_line(net, pack_one)
    plane_a = Plane(net, stack_a, True)
    gain_given = None
    if not net.fast:
        gain_all = lax.all_gather(gains.astype(BF), "dp", axis=1, tiled=True).astype(F32)
        gain_given = jnp.pad(gain_all, ((0, 6), (0, 0)))

    x_pair = jnp.concatenate([inputs, x_in], axis=0)
    back = jnp.concatenate([cotangent, back_in], axis=0)
    x_pair, back = together(x_pair, back)
    h1, gain_wide, qkv_own, wqkv_own, wout_own = project(net, pos, x_pair, plane_a.own(), width, gain_given, True)
    plane_a.turn()
    qkv_own, line_one, pack_two = together(qkv_own, line_one, pack_two)
    feed_one = Plane(net, stacked(net, line_one), True)
    two_in = [net.z(pack_two, 2)] if net.fast else []
    o_own, *saved_own = attend(meta, qkv_own, width, seqs)
    o_own, plane_a.far_in, two_in = together(o_own, plane_a.far_in, two_in)
    two_last = [net.z(jnp.stack([pack_two] + two_in), 1)] if net.fast else []

    h1_late = after(h1, o_own)
    qkv_other, wqkv_other, wout_other = project(net, pos, h1_late, plane_a.other(), width)
    o_other, *saved_other = attend(meta, qkv_other, width, seqs)
    o_other, feed_one.near_in, two_last = together(o_other, feed_one.near_in, two_last)
    feed_one.turn()

    o_other = after(o_other, feed_one.halves)
    branch = (dot_nt(o_own, wout_own) + dot_nt(o_other, wout_other)).astype(BF)
    branch_in = net.core(branch)
    line_two = [pack_two]
    if net.fast:
        line_two = [pack_two, two_last[0][0], two_in[0], two_last[0][1]]
    feed_two = Plane(net, stacked(net, line_two), True)
    h2 = second_norm(x_pair, branch, branch_in, gain_wide)

    pack_width = 3 * half_units
    f_spans = [(0, (0, 0), 0, 2 * half_units), (1, (0, 2 * half_units), 2 * half_units, half_units)]

    def feed_grads(mid, far):
        return grad_pack(net, pos, h2, back, mid, mid, f_spans, pack_width, far)

    mid_own, f_part, d_part = feed(net, pos, h2, back, feed_one.own(), half_units, [])
    mid_other, f_part, d_part = feed(net, pos, h2, back, feed_one.other(), half_units, [f_part, d_part])
    one_other = feed_grads(mid_other, True)
    one_own = feed_grads(mid_own, False)
    f_part, d_part, feed_two.near_in = together(f_part, d_part, after(feed_two.near_in, (one_own, one_other)))
    feed_two.turn()
    mid_own, f_part, d_part = feed(net, pos, h2, back, feed_two.own(), half_units, [f_part, d_part])
    sum_one = Scatter(net, pos, after(one_other, d_part))
    sum_one.own(one_own)
    mid_other, f_part, d_part = feed(net, pos, h2, back, feed_two.other(), half_units, [f_part, d_part])
    mid_other, f_part, d_part, sum_one.far_in = together(mid_other, f_part, d_part, sum_one.far_in)
    d_in = net.core(d_part)
    g_other = feed_grads(after(mid_other, d_part), True)
    sum_two = Scatter(net, pos, g_other)
    g_own = feed_grads(after(mid_own, g_other), False)
    sum_two.own(g_own)
    sum_one.gate = g_own
    sum_one.turn()
    d_in = after(d_in, sum_one.marks())

    da, do_own, do_other, dx2 = middle(
        x_pair, branch, branch_in, back, d_part, d_in, gain_wide, wout_own, wout_other
    )
    da, do_own, do_other, dx2, sum_two.far_in = together(da, do_own, do_other, dx2, sum_two.far_in)
    heads = tuple(range(width // DH))
    dqkv_other = attend_back(qkv_other, do_other, o_other, saved_other, width, seqs, heads)
    a_spans = [(0, (0, 0), 0, 3 * width), (1, (1, 0), 3 * width, width)]
    g_other = grad_pack(net, pos, h1, da, dqkv_other, o_other, a_spans, 4 * width, True)
    sum_a = Scatter(net, pos, g_other)
    sum_one.gate = g_other[0]
    sum_one.pair()
    sum_two.gate = sum_one.mark
    sum_two.turn()
    do_own = after(do_own, (g_other, sum_one.mark, sum_two.marks()))
    dqkv_own = attend_back(qkv_own, do_own, o_own, saved_own, width, seqs, heads[:2], light=True)
    dqkv_own, sum_a.far_in = together(dqkv_own, sum_a.far_in)
    dqkv_own = attend_back(qkv_own, do_own, o_own, saved_own, width, seqs, heads[2:], dqkv_own)
    dqkv_own, sum_one.pair_in = together(dqkv_own, sum_one.pair_in)
    g_own = grad_pack(net, pos, h1, da, dqkv_own, o_own, a_spans, 4 * width, False)
    sum_a.own(g_own)
    sum_a.turn()
    sum_one.gate = sum_two.gate = sum_a.sums
    pieces_one = sum_one.finish_pair()
    sum_two.pair()
    dqkv_own, dqkv_last = after((dqkv_own, dqkv_other), (sum_one.last_sum, sum_two.mark))
    send, dh1 = first_grad(dqkv_own, dqkv_last, wqkv_own, wqkv_other, f_part)
    send, sum_two.pair_in, pieces_one = together(send, sum_two.pair_in, pieces_one)
    sum_two.gate = send
    pieces_two = sum_two.finish_pair()
    sum_a.near_in = after(sum_a.near_in, sum_two.last_sum)
    pieces_a = sum_a.finish()
    last_in = net.core(after(send, sum_a.mark))

    output, input_grad = last(inputs, branch, branch_in, f_part, last_in, dh1, gain_wide, dx2)
    states_f = [w_gu, m_gu, v_gu, w_down.T, m_down.T, v_down.T]
    feed_new = adam_call(adam_feed_kernel, after(pieces_one + pieces_two, output), states_f, "adam_feed", True)
    pieces_a = after(pieces_a, feed_new[-1])
    total_a, gain_one = total_attend(pieces_a, w_qkv)
    terms = jnp.concatenate([gain_one[0:1], feed_new[-1][0:1]], axis=0)
    states_a = [w_qkv, m_qkv, v_qkv, w_out, m_out, v_out]
    attend_new = adam_call(adam_attend_kernel, [total_a], states_a, "adam_attend", False)
    total = terms + net.core(terms) + net.x(terms) + net.cross(terms)
    gain_grad = total[:, :shard] / round_low(gains)
    new_gains, gain_moment, gain_second = gain_step(gains, m_gain, v_gain, gain_grad)
    return (
        (output, input_grad, new_gains, gain_moment, gain_second)
        + tuple(attend_new[:6])
        + tuple(feed_new[:3])
        + tuple(v.T for v in feed_new[3:6])
    )


def solution(mesh):
    net = Net(mesh.shape["dp"], mesh.shape["mp"])
    rows = P(("dp", "mp"), None)
    gain = P(None, "dp")
    wide = P(None, "dp", "mp")
    tall = P("mp", "dp")
    return jax.shard_map(
        functools.partial(body, net),
        mesh=mesh,
        in_specs=(rows, rows, P("dp"), gain) + (wide,) * 3 + (tall,) * 3 + (wide,) * 3 + (tall,) * 3 + (gain,) * 2,
        out_specs=(rows, rows) + (gain,) * 3 + (wide,) * 3 + (tall,) * 3 + (wide,) * 3 + (tall,) * 3,
        check_vma=False,
    )
```
